32 devices in a mesh: roll: 16 (over z, y, core), trans: 2 (over x).
Axes of the slice: x: 2, y: 2, z: 4, core: 2. Of those that a mesh axis runs over, the one named last changes fastest.
Arguments:
- adjoint: float32 [4, 2, 32, 128, 256], P(None, None, None, 'roll', 'trans'), may hold values from -6 to 6
- source: float32 [4, 2, 32, 128, 256], P(None, None, None, 'roll', 'trans'), may hold values from -6 to 6
- pressure: float32 [2, 128, 256], P(None, 'roll', 'trans'), may hold values from -4 to 4
- film: float32 [128, 256], P('roll', 'trans'), may hold values from 0.6 to 1.4
- cavity: int32 [2, 128, 256], P(None, 'roll', 'trans'), may hold values 0 or 1
- temp_index: int32 [2], replicated, may hold values from 0 to 7
Outputs:
- adjoint_out: float32 [4, 2, 32, 128, 256], P(None, None, None, 'roll', 'trans')
- wall_step: float32 [128, 256], P('roll', 'trans')
The draws below stay inside these ranges and needn't reach their ends.
All inputs are finite; a program needn't handle non-finite values. No bound on the sum of `cavity` on one device may be relied on, other than what follows from the above.
Results may differ from the reference program's by a relative error of at most 0.00002.
Values sent between devices are 32-bit elements; how exact they have to be, the bound alone decides.
No kernel may reach another device: no remote copies, remote signals or barrier semaphores. Data moves between devices by JAX's collectives and lax.ppermute only.
A program may use at most 64 MiB of HBM per device.

```python
import jax
import jax.numpy as jnp
from jax import lax

NZ = 32
CASES = 2
SECTIONS = 2
NX = 128
NY = 256


def touch_ends(values, stream_key, low, largest):
    longest = values.shape.index(max(values.shape))
    spots = []
    for shift in (0, 1):
        where = [jax.random.randint(jax.random.fold_in(stream_key, axis), (), 0, length) for axis, length in enumerate(values.shape)]
        where[longest] = (where[longest] + shift) % values.shape[longest]
        spots.append(tuple(where))
    return values.at[spots[0]].set(low).at[spots[1]].set(largest)


def levels(own_key, extent, split, smallest, largest):
    gain = 1.0
    for position, parts in split:
        draws = jax.random.uniform(jax.random.fold_in(jax.random.fold_in(own_key, 6), position), (parts,), jnp.float32, smallest / len(split), largest / len(split))
        gain = gain * jnp.repeat(jnp.exp(draws), extent[position] // parts).reshape((-1,) + (1,) * (len(extent) - 1 - position))
    return gain


def gaussian(own_key, extent, width, most, shards=(), held_as=jnp.bfloat16):
    array = width * jax.random.normal(own_key, extent, jnp.float32)
    if shards:
        array = array * levels(own_key, extent, shards, -0.22, 0.18)
    return jnp.clip(array, -most, most).astype(held_as)


def setup_inputs(seed: int = 0) -> dict:
    key_of = jax.random.split(jax.random.key(seed), 7)
    return {
        "adjoint": gaussian(key_of[0], (4, CASES, NZ, NX, NY), 1.0, 6.0, ((3, 16), (4, 2)), jnp.float32),
        "source": gaussian(key_of[1], (4, CASES, NZ, NX, NY), 1.0, 6.0, ((3, 16), (4, 2)), jnp.float32),
        "pressure": gaussian(key_of[2], (CASES, NX, NY), 1.0, 4.0, ((1, 16), (2, 2)), jnp.float32),
        "film": jnp.clip(0.6 + 0.79999995 * jax.random.uniform(key_of[3], (NX, NY), jnp.float32) ** levels(key_of[3], (NX, NY), ((0, 16), (1, 2)), -0.2, 0.2), 0.6, 1.4),
        "cavity": touch_ends((jax.random.randint(key_of[4], (CASES, NX, NY), 0, 3) < 1).astype(jnp.int32), jax.random.fold_in(key_of[4], 1), 0, 1),
        "temp_index": jax.random.randint(key_of[5], (CASES,), 0, 8).astype(jnp.int32),
    }


VISCOSITY_PRESS = 0.3
VISCOSITY_TEMP = 0.5
THETA_STEP = 0.2
SOUND = 0.5
KAPPA = 0.6
HEATING = 0.3
ROLL_SPEED = 1.0
COURANT = 0.8

def coefficients(pressure, film, cavity, temp_index):
    implicit_weight = THETA_STEP * temp_index.astype(jnp.float32)
    fluid_viscosity = jnp.exp(VISCOSITY_PRESS * pressure - VISCOSITY_TEMP * implicit_weight[:, None, None])
    film_coef = 4.0 * fluid_viscosity / (film * film)
    density = 1.0 - 0.6 * cavity.astype(jnp.float32)
    pseudo_step = COURANT / (32.0 / 3.0 * fluid_viscosity + 4.0 * film_coef + 2.0 * SOUND + 1.0)
    return jnp.stack([fluid_viscosity, film_coef, density, pseudo_step])

def time_section(padded, source, coeffs):
    depth = source.shape[-3]
    width_x = source.shape[-2]
    width_y = source.shape[-1]

    def along_x(offset):
        return padded[..., 2 + offset:2 + offset + width_x, 2:2 + width_y]

    def along_y(offset):
        return padded[..., 2:2 + width_x, 2 + offset:2 + offset + width_y]
    center = along_x(0)
    second_x = (-along_x(2) + 16.0 * along_x(1) - 30.0 * center + 16.0 * along_x(-1) - along_x(-2)) / 12.0
    second_y = (-along_y(2) + 16.0 * along_y(1) - 30.0 * center + 16.0 * along_y(-1) - along_y(-2)) / 12.0
    first_x = (-along_x(2) + 8.0 * along_x(1) - 8.0 * along_x(-1) + along_x(-2)) / 12.0
    first_y = (-along_y(2) + 8.0 * along_y(1) - 8.0 * along_y(-1) + along_y(-2)) / 12.0
    layered = jnp.pad(center, ((0, 0), (0, 0), (1, 1), (0, 0), (0, 0)))
    second_z = layered[:, :, 2:] - 2.0 * center + layered[:, :, :-2]
    fluid_viscosity = coeffs[0][:, None]
    film_coef = coeffs[1][:, None]
    density = coeffs[2][:, None]
    pseudo_step = coeffs[3][:, None]
    film_height = ((jnp.arange(depth).astype(jnp.float32) + 0.5) / depth)[:, None, None]
    diffused = fluid_viscosity * (second_x + second_y) + film_coef * second_z
    carried = density * ROLL_SPEED * film_height * first_x
    resid_density = 0.5 * diffused[0] + carried[0] + SOUND * (first_x[1] + first_y[2])
    resid_along = diffused[1] + carried[1] + SOUND * first_x[0]
    resid_across = diffused[2] + carried[2] + SOUND * first_y[0]
    resid_energy = KAPPA * diffused[3] + carried[3] + HEATING * fluid_viscosity * center[1]
    residual = jnp.stack([resid_density, resid_along, resid_across, resid_energy])
    return center + pseudo_step * (residual + source)

def wall_terms(padded_mean, momentum, coeffs, film):
    width_x = momentum.shape[-2]
    depth = momentum.shape[-3]
    slope = (-padded_mean[:, 4:4 + width_x] + 8.0 * padded_mean[:, 3:3 + width_x] - 8.0 * padded_mean[:, 1:1 + width_x] + padded_mean[:, 0:width_x]) / 12.0
    layered = jnp.pad(momentum, ((0, 0), (1, 1), (0, 0), (0, 0)))
    bending = layered[:, 2:] - 2.0 * momentum + layered[:, :-2]
    curvature = lax.optimization_barrier(jnp.sum(momentum * bending, axis=1)) / depth
    flux = coeffs[2] * ROLL_SPEED * film / 2.0
    return flux * slope - 8.0 * coeffs[0] / (film * film * film) * curvature

def reference(adjoint, source, pressure, film, cavity, temp_index):

    def one_case(model_inputs):
        state_case, source_case, pressure_case, cavity_case, level_case = model_inputs
        state = state_case[:, None]
        forcing = source_case[:, None]
        coeffs = coefficients(pressure_case[None], film, cavity_case[None], level_case[None])
        for section_index in range(SECTIONS):
            padded = jnp.pad(state, ((0, 0), (0, 0), (0, 0), (2, 2), (2, 2)))
            state = time_section(padded, forcing, coeffs)
        depth = state.shape[2]
        mean_density = lax.optimization_barrier(jnp.sum(state[0], axis=1)) / depth
        padded_mean = jnp.pad(mean_density, ((0, 0), (2, 2), (0, 0)))
        terms = wall_terms(padded_mean, state[1], coeffs, film)
        return (state[:, 0], terms[0])
    states, terms = lax.map(one_case, (jnp.moveaxis(adjoint, 1, 0), jnp.moveaxis(source, 1, 0), pressure, cavity, temp_index))
    adjoint_out = jnp.moveaxis(states, 0, 1)
    wall_grad = lax.optimization_barrier(jnp.sum(terms, axis=0))
    total = jnp.sum(wall_grad * wall_grad)
    wall_step = wall_grad / jnp.sqrt(total / (NX * NY) + 1e-06)
    return (adjoint_out, wall_step)
```

```python
import functools

import jax
import jax.numpy as jnp
from jax import lax
from jax.experimental import pallas as pl
from jax.experimental.pallas import tpu as pltpu
from jax.sharding import PartitionSpec as P

SECTIONS = 2


VISCOSITY_PRESS = 0.3
VISCOSITY_TEMP = 0.5
THETA_STEP = 0.2
SOUND = 0.5
KAPPA = 0.6
HEATING = 0.3
ROLL_SPEED = 1.0
COURANT = 0.8

VM = pl.BlockSpec(memory_space=pltpu.VMEM)
SM = pl.BlockSpec(memory_space=pltpu.SMEM)
WEIGHTS = (0.5, 1.0, 1.0, KAPPA)
N_COEF = 13


def lanes_of(shape):
    return lax.broadcasted_iota(jnp.int32, shape, 1)


def rows_of(shape):
    return lax.broadcasted_iota(jnp.int32, shape, 0)


def pack_rows(state_ref, up_ref, down_ref, planes):
    for row in range(2):
        for i in range(planes // 8):
            here = pl.ds(row * planes + 8 * i, 8)
            up_ref[here, :] = state_ref[pl.ds(64 * i + 6 + row, 8, stride=8), :]
            down_ref[here, :] = state_ref[pl.ds(64 * i + row, 8, stride=8), :]


def unpack_rows(halo_ref, below_ref, above_ref, planes):
    for row in range(2):
        for i in range(planes // 8):
            here = pl.ds(row * planes + 8 * i, 8)
            halo_ref[pl.ds(64 * i + 6 + row, 8, stride=8), :] = below_ref[here, :]
            halo_ref[pl.ds(64 * i + row, 8, stride=8), :] = above_ref[here, :]


def pack_columns(packed, plane, k, lane):
    return jnp.where(lane // 4 == k, pltpu.roll(plane, 4 * k + 2, 1), packed)


def pack_kernel(depth, cases, state_ref, up_ref, down_ref, cols_ref):
    planes = 4 * cases * depth
    pack_rows(state_ref, up_ref, down_ref, planes)
    lane = lanes_of((8, 128))
    for group in range(4 * cases):

        def step(k, packed):
            plane = state_ref[pl.ds(pl.multiple_of((group * depth + k) * 8, 8), 8), :]
            return pack_columns(packed, plane, k, lane)

        packed = lax.fori_loop(0, depth, step, jnp.zeros((8, 128), jnp.float32), unroll=8)
        cols_ref[pl.ds(group * 8, 8), :] = packed


def shifted(plane, halo, place, axis, size):
    def moved(edge, by):
        return pltpu.roll(jnp.where(edge, halo, plane), by, axis)

    before = moved(place == size - 1, 1), moved(place >= size - 2, 2)
    after = moved(place == 0, size - 1), moved(place < 2, size - 2)
    return before + after


def derivatives(plane, halo, cols, lane, row):
    ym1, ym2, yp1, yp2 = shifted(plane, cols, lane, 1, 128)
    xm1, xm2, xp1, xp2 = shifted(plane, halo, row, 0, 8)
    second = 16.0 * ((xm1 + xp1) + (ym1 + yp1)) - ((xm2 + xp2) + (ym2 + yp2))
    first_x = 8.0 * (xp1 - xm1) - (xp2 - xm2)
    first_y = 8.0 * (yp1 - ym1) - (yp2 - ym2)
    return second, first_x, first_y


def coefficient_planes(pressure, film, cavity, level):
    theta = THETA_STEP * level.astype(jnp.float32)
    viscosity = jnp.exp(VISCOSITY_PRESS * pressure - VISCOSITY_TEMP * theta)
    film_coef = 4.0 * viscosity / (film * film)
    density = 1.0 - 0.6 * cavity.astype(jnp.float32)
    step = COURANT / (32.0 / 3.0 * viscosity + 4.0 * film_coef + 2.0 * SOUND + 1.0)
    planes = []
    for weight in (0.5, 1.0, KAPPA):
        spread = (weight / 12.0) * step * viscosity
        across = weight * step * film_coef
        planes += [1.0 - 60.0 * spread - 2.0 * across, spread, across]
    planes += [(ROLL_SPEED / 12.0) * step * density, (SOUND / 12.0) * step, step, HEATING * step * viscosity]
    return planes, viscosity, density


def section_kernel(
    depth,
    cases,
    final,
    trans,
    level_ref,
    state_ref,
    source_ref,
    below_ref,
    above_ref,
    side_ref,
    pressure_ref,
    film_ref,
    cavity_ref,
    *rest,
):
    if final:
        out_ref, terms_ref, mean_up_ref, mean_down_ref, halo_ref, coef_ref = rest
    else:
        out_ref, up_ref, down_ref, cols_ref, halo_ref, coef_ref = rest
    planes = 4 * cases * depth
    lane, row = lanes_of((8, 128)), rows_of((8, 128))
    unpack_rows(halo_ref, below_ref, above_ref, planes)
    place = lax.axis_index(trans)
    from_left = jnp.where(place > 0, 1.0, 0.0)
    from_right = jnp.where(place < lax.axis_size(trans) - 1, 1.0, 0.0)
    side_mask = jnp.where(lane % 4 < 2, from_left, from_right)
    film = film_ref[...]
    wall = jnp.zeros((8, 128), jnp.float32)
    for case in range(cases):
        coefs, viscosity, density = coefficient_planes(
            pressure_ref[pl.ds(case * 8, 8), :], film, cavity_ref[pl.ds(case * 8, 8), :], level_ref[case]
        )
        for i, plane in enumerate(coefs):
            coef_ref[pl.ds(i * 8, 8), :] = plane
        sides = [side_ref[pl.ds((c * cases + case) * 8, 8), :] * side_mask for c in range(4)]

        def at(component, k):
            return pl.ds(pl.multiple_of(((component * cases + case) * depth + k) * 8, 8), 8)

        def coef(i):
            return coef_ref[pl.ds(i * 8, 8), :]

        def body(k, carry):
            before, now, extra = carry
            height = (k.astype(jnp.float32) + 0.5) / depth
            flag = jnp.where(k + 1 < depth, 1.0, 0.0)
            later = [state_ref[at(c, jnp.minimum(k + 1, depth - 1)), :] * flag for c in range(4)]
            parts = [
                derivatives(now[c], halo_ref[at(c, k), :], pltpu.roll(sides[c], 126 + 128 - 4 * k, 1), lane, row)
                for c in range(4)
            ]
            new = []
            density_step = coef(9) * height
            sound = coef(10)
            for c in range(4):
                which = (0, 1, 1, 2)[c]
                second, first_x, _ = parts[c]
                value = coef(3 * which) * now[c] + coef(3 * which + 1) * second
                value += coef(3 * which + 2) * (before[c] + later[c])
                value += density_step * first_x + coef(11) * source_ref[at(c, k), :]
                if c == 0:
                    value += sound * (parts[1][1] + parts[2][2])
                elif c == 1:
                    value += sound * parts[0][1]
                elif c == 2:
                    value += sound * parts[0][2]
                else:
                    value += coef(12) * now[1]
                out_ref[at(c, k), :] = value
                new.append(value)
            if final:
                total, bend, last = extra
                change = new[1] - last
                extra = (total + new[0], bend + change * change, new[1])
            else:
                extra = tuple(pack_columns(packed, value, k, lane) for packed, value in zip(extra, new, strict=True))
            return now, later, extra

        zero = jnp.zeros((8, 128), jnp.float32)
        start = [state_ref[at(c, 0), :] for c in range(4)]
        _, _, extra = lax.fori_loop(0, depth, body, ([zero] * 4, start, (zero,) * (3 if final else 4)), unroll=2)
        if final:
            total, bend, last = extra
            mean = total * (1.0 / depth)
            curvature = -(bend + last * last) * (1.0 / depth)
            wall = wall - 8.0 * viscosity / (film * film * film) * curvature
            terms_ref[pl.ds(case * 8, 8), :] = mean
            terms_ref[pl.ds((cases + case) * 8, 8), :] = (ROLL_SPEED / 24.0) * density * film
        else:
            for c in range(4):
                cols_ref[pl.ds((c * cases + case) * 8, 8), :] = extra[c]
    if final:
        terms_ref[pl.ds(2 * cases * 8, 8), :] = wall
        for case in range(cases):
            mean_up_ref[pl.ds(case * 8, 8), :] = terms_ref[pl.ds(case * 8, 8), :]
            mean_down_ref[pl.ds(case * 8, 8), :] = terms_ref[pl.ds(case * 8, 8), :]
    else:
        pack_rows(out_ref, up_ref, down_ref, planes)


def wall_kernel(cases, terms_ref, below_ref, above_ref, grad_ref, sums_ref):
    row = rows_of((8, 128))
    grad = terms_ref[pl.ds(2 * cases * 8, 8), :]
    for case in range(cases):
        mean = terms_ref[pl.ds(case * 8, 8), :]
        halo = jnp.where(row >= 4, below_ref[pl.ds(case * 8, 8), :], above_ref[pl.ds(case * 8, 8), :])
        xm1, xm2, xp1, xp2 = shifted(mean, halo, row, 0, 8)
        slope = 8.0 * (xp1 - xm1) - (xp2 - xm2)
        grad += terms_ref[pl.ds((cases + case) * 8, 8), :] * slope
    grad_ref[...] = grad
    part = jnp.sum(grad * grad, axis=0, keepdims=True)
    sums_ref[...] = jnp.broadcast_to(part[None], sums_ref.shape)


def scale_kernel(cells, grad_ref, sums_ref, out_ref):
    total = jnp.sum(sums_ref[...], axis=0)
    total = jnp.sum(total, axis=1, keepdims=True)
    out_ref[...] = grad_ref[...] / jnp.sqrt(total / cells + 1e-06)


def f32(*shape):
    return jax.ShapeDtypeStruct(shape, jnp.float32)


def neighbours(axis):
    size = lax.axis_size(axis)
    up = [(i, i + 1) for i in range(size - 1)]
    return up, [(j, i) for i, j in up]


def exchange_rows(up, down):
    ahead, back = neighbours("roll")
    return lax.ppermute(up, "roll", ahead), lax.ppermute(down, "roll", back)


def exchange_columns(cols):
    ahead, back = neighbours("trans")
    if lax.axis_size("trans") == 2:
        return lax.ppermute(cols, "trans", ahead + back)
    left, right = lax.ppermute(cols, "trans", ahead), lax.ppermute(cols, "trans", back)
    return jnp.where(lanes_of(cols.shape) % 4 < 2, left, right)


def on_device(adjoint, source, pressure, film, cavity, temp_index):
    components, cases, depth, width_x, width_y = adjoint.shape
    planes = components * cases * depth
    assert (components, width_x, width_y, 4 * depth) == (4, 8, 128, 128)
    state = adjoint.reshape(planes * 8, 128)
    forcing = source.reshape(planes * 8, 128)
    pressure = pressure.reshape(cases * 8, 128)
    cavity = cavity.reshape(cases * 8, 128)
    message = (f32(planes * 2, 128), f32(planes * 2, 128), f32(components * cases * 8, 128))
    params = pltpu.CompilerParams(vmem_limit_bytes=24 * 1024 * 1024)
    up, down, cols = pl.pallas_call(
        functools.partial(pack_kernel, depth, cases),
        out_shape=message,
        in_specs=[VM],
        out_specs=(VM,) * 3,
        compiler_params=params,
    )(state)
    for index in range(SECTIONS):
        final = index == SECTIONS - 1
        side = exchange_columns(cols)
        below, above = exchange_rows(up, down)
        if final:
            shapes = (f32(planes * 8, 128), f32((2 * cases + 1) * 8, 128), f32(cases * 8, 128), f32(cases * 8, 128))
        else:
            shapes = (f32(planes * 8, 128),) + message
        results = pl.pallas_call(
            functools.partial(section_kernel, depth, cases, final, "trans"),
            out_shape=shapes,
            in_specs=[SM] + [VM] * 8,
            out_specs=(VM,) * len(shapes),
            scratch_shapes=[pltpu.VMEM((planes * 8, 128), jnp.float32), pltpu.VMEM((N_COEF * 8, 128), jnp.float32)],
            compiler_params=params,
        )(temp_index, state, forcing, below, above, side, pressure, film, cavity)
        if final:
            state, terms, up, down = results
        else:
            state, up, down, cols = results
    below, above = exchange_rows(up, down)
    devices = lax.axis_size("roll") * lax.axis_size("trans")
    grad, sums = pl.pallas_call(
        functools.partial(wall_kernel, cases),
        out_shape=(f32(8, 128), f32(devices, 1, 128)),
        in_specs=[VM] * 3,
        out_specs=(VM,) * 2,
    )(terms, below, above)
    sums = lax.all_to_all(sums, ("roll", "trans"), 0, 0, tiled=True)
    wall_step = pl.pallas_call(
        functools.partial(scale_kernel, devices * width_x * width_y),
        out_shape=f32(8, 128),
        in_specs=[VM] * 2,
        out_specs=VM,
    )(grad, sums)
    return (state.reshape(adjoint.shape), wall_step)


def solution(mesh):
    placed = (
        P(None, None, None, "roll", "trans"),
        P(None, None, None, "roll", "trans"),
        P(None, "roll", "trans"),
        P("roll", "trans"),
        P(None, "roll", "trans"),
        P(),
    )
    return jax.shard_map(
        on_device,
        mesh=mesh,
        in_specs=placed,
        out_specs=(P(None, None, None, "roll", "trans"), P("roll", "trans")),
        check_vma=False,
    )
```

```python
import functools

import jax
import jax.numpy as jnp
from jax import lax
from jax.experimental import pallas as pl
from jax.experimental.pallas import tpu as pltpu
from jax.sharding import PartitionSpec as P

SECTIONS = 2


VISCOSITY_PRESS = 0.3
VISCOSITY_TEMP = 0.5
THETA_STEP = 0.2
SOUND = 0.5
KAPPA = 0.6
HEATING = 0.3
ROLL_SPEED = 1.0
COURANT = 0.8

VM = pl.BlockSpec(memory_space=pltpu.VMEM)
SM = pl.BlockSpec(memory_space=pltpu.SMEM)
PARAMS = pltpu.CompilerParams(vmem_limit_bytes=16 * 1024 * 1024)

PAD = 8
CENTER, SPREAD, ACROSS = (0, 3, 6)
CARRY, SOUND_STEP, STEP, HEAT, FLUX, BEND = range(9, 15)
N_COEF = 15
N_PACKED = 5
WEIGHT = (0, 1, 1, 2)


def lanes_of(shape):
    return lax.broadcasted_iota(jnp.int32, shape, 1)


def rows_of(shape):
    return lax.broadcasted_iota(jnp.int32, shape, 0)


def rows(start, count=8):
    return pl.ds(start, count)


def strided(start):
    return pl.ds(start, 8, stride=8)


def coefficient_kernel(depth, cases, level_ref, place_ref, pressure_ref, film_ref, cavity_ref, coef_ref, packed_ref, mask_ref):
    lane, row = lanes_of((8, 128)), rows_of((8, 128))
    film = film_ref[...]
    height = ((depth - 1 - lane // 4).astype(jnp.float32) + 0.5) / depth
    for case in range(cases):
        theta = THETA_STEP * level_ref[case].astype(jnp.float32)
        viscosity = jnp.exp(VISCOSITY_PRESS * pressure_ref[rows(case * 8), :] - VISCOSITY_TEMP * theta)
        film_coef = 4.0 * viscosity / (film * film)
        density = 1.0 - 0.6 * cavity_ref[rows(case * 8), :].astype(jnp.float32)
        step = COURANT / (32.0 / 3.0 * viscosity + 4.0 * film_coef + 2.0 * SOUND + 1.0)
        planes = [None] * N_COEF
        for i, weight in enumerate((0.5, 1.0, KAPPA)):
            planes[SPREAD + i] = (weight / 12.0) * step * viscosity
            planes[ACROSS + i] = weight * step * film_coef
            planes[CENTER + i] = 1.0 - 60.0 * planes[SPREAD + i] - 2.0 * planes[ACROSS + i]
        planes[CARRY] = (ROLL_SPEED / 12.0) * step * density
        planes[SOUND_STEP] = (SOUND / 12.0) * step
        planes[STEP] = step
        planes[HEAT] = HEATING * step * viscosity
        planes[FLUX] = (ROLL_SPEED / (24.0 * depth)) * density * film
        planes[BEND] = (8.0 / depth) * viscosity / (film * film * film)
        for i, plane in enumerate(planes):
            coef_ref[rows((case * N_COEF + i) * 8), :] = plane
        wanted = jnp.concatenate(planes[SPREAD : SPREAD + 3] + [planes[CARRY], planes[SOUND_STEP]], axis=0)
        packed = exact_dot(wanted, edge_columns())
        for i in range(N_PACKED):
            plane = packed[i * 8 : i * 8 + 8]
            packed_ref[rows((case * N_PACKED + i) * 8), :] = plane * height if i == 3 else plane
    from_left = jnp.where(place_ref[0] > 0, 1.0, 0.0)
    from_right = jnp.where(place_ref[0] < place_ref[1] - 1, 1.0, 0.0)
    mask_ref[...] = jnp.where(lane % 4 < 2, from_left, from_right)


def edge_columns():
    source = lanes_of((128, 128)) % 4
    source = jnp.where(source < 2, 126 + source, source - 2)
    return jnp.where(rows_of((128, 128)) == source, 1.0, 0.0).astype(jnp.bfloat16)


def in_parts(value):
    high = value.astype(jnp.bfloat16)
    rest = value - high.astype(jnp.float32)
    middle = rest.astype(jnp.bfloat16)
    return jnp.concatenate([high, middle], axis=1), (rest - middle.astype(jnp.float32)).astype(jnp.bfloat16)


def exact_dot(value, weights):
    upper, low = in_parts(value)
    part = jnp.dot(upper, jnp.concatenate([weights, weights], axis=0), preferred_element_type=jnp.float32)
    return part + jnp.dot(low, weights, preferred_element_type=jnp.float32)


def send_edges(cols_ref, up_ref, down_ref, planes):
    for row in range(2):
        up_ref[rows(2 * planes + 8 * row), :] = cols_ref[strided(6 + row), :]
        down_ref[rows(2 * planes + 8 * row), :] = cols_ref[strided(row), :]


def pack_kernel(depth, cases, state_ref, tiles_ref, up_ref, down_ref, cols_ref):
    planes = 4 * cases * depth
    lane = lanes_of((8, 128))

    def one(pair, _):
        held = jnp.zeros((8, 128), jnp.float32)
        for layer in range(depth):
            group = depth - 1 - layer
            plane = state_ref[rows(pl.multiple_of((pair * depth + layer) * 8, 8)), :]
            held = jnp.where(lane // 4 == group, pltpu.roll(plane, (4 * group + 2) % 128, 1), held)
        cols_ref[rows(pl.multiple_of(pair * 8, 8)), :] = held
        for row in (0, 1, 6, 7, 2, 3, 4, 5):
            for block in range(depth // 8):
                first = pl.multiple_of(pair * depth + 8 * block, 8)
                tile = state_ref[strided(first * 8 + row), :]
                tiles_ref[rows(PAD + row * planes + first), :] = tile
                if row < 2:
                    down_ref[rows(row * planes + first), :] = tile
                if row > 5:
                    up_ref[rows((row - 6) * planes + first), :] = tile
        return 0

    lax.fori_loop(0, 4 * cases, one, 0)
    send_edges(cols_ref, up_ref, down_ref, planes)


def inner_kernel(depth, cases, tiles_ref, source_ref, coef_ref, *rest):
    out_ref, *cols_ref, deriv_ref = rest
    planes = 4 * cases * depth
    lane, layer = lanes_of((8, 128)), rows_of((8, 128))
    gap = rows_of((128, 256)) - lanes_of((128, 256)) % 128
    second = jnp.where(jnp.abs(gap) == 1, 16.0, jnp.where(jnp.abs(gap) == 2, -1.0, 0.0))
    first = jnp.where(gap == 1, 8.0, jnp.where(gap == -1, -8.0, jnp.where(gap == 2, -1.0, jnp.where(gap == -2, 1.0, 0.0))))
    weights = jnp.where(lanes_of((128, 256)) < 128, second, first).astype(jnp.bfloat16)
    for row in range(8):
        value = tiles_ref[rows(PAD + row * planes, planes), :]
        deriv_ref[rows(row * planes, planes), :] = exact_dot(value, weights)

    def one(index, _):
        case, block = index // (depth // 8), index % (depth // 8)
        k = layer + 8 * block
        height = (k.astype(jnp.float32) + 0.5) / depth
        offsets = [pl.multiple_of((c * cases + case) * depth + 8 * block, 8) for c in range(4)]
        tiles = [[tiles_ref[rows(PAD + row * planes + offsets[c]), :] for row in range(8)] for c in range(4)]

        for row in range(8):

            def coef(i):
                return coef_ref[pl.ds((case * N_COEF + i) * 8 + row, 1), :]

            along = []
            for c in range(4):
                near = [tiles[c][row + by] if 0 <= row + by < 8 else None for by in (-2, -1, 1, 2)]
                along.append(near)

            def first_x(c):
                m2, m1, p1, p2 = along[c]
                ones = 8.0 * (p1 - m1) if m1 is not None and p1 is not None else 8.0 * p1 if m1 is None else -8.0 * m1
                if m2 is not None and p2 is not None:
                    return ones - (p2 - m2)
                return ones - p2 if m2 is None else ones + m2

            def second_x(c):
                m2, m1, p1, p2 = along[c]
                ones = 16.0 * (p1 + m1) if m1 is not None and p1 is not None else 16.0 * (p1 if m1 is None else m1)
                if m2 is not None and p2 is not None:
                    return ones - (p2 + m2)
                return ones - (p2 if m2 is None else m2)

            carry = coef(CARRY) * height
            sound = coef(SOUND_STEP)
            step = coef(STEP)
            slopes = [first_x(c) for c in range(4)]
            for c in range(4):
                here = row * planes + offsets[c]
                behind = jnp.where(k > 0, tiles_ref[rows(PAD - 1 + here), :], 0.0)
                beyond = jnp.where(k < depth - 1, tiles_ref[rows(PAD + 1 + here), :], 0.0)
                source = source_ref[strided(offsets[c] * 8 + row), :]
                w = WEIGHT[c]
                value = coef(CENTER + w) * tiles[c][row] + coef(SPREAD + w) * (second_x(c) + deriv_ref[rows(here), 0:128])
                value += coef(ACROSS + w) * (behind + beyond) + step * source + carry * slopes[c]
                if c == 0:
                    other = row * planes + offsets[2]
                    value += sound * (slopes[1] + deriv_ref[rows(other), 128:256])
                elif c == 1:
                    value += sound * slopes[0]
                elif c == 2:
                    other = row * planes + offsets[0]
                    value += sound * deriv_ref[rows(other), 128:256]
                else:
                    value += coef(HEAT) * tiles[1][row]
                out_ref[rows(here), :] = value
        return 0

    lax.fori_loop(0, cases * (depth // 8), one, 0)

    if cols_ref:
        columns = edge_columns()
        group = (depth - 1) - rows_of((depth, 128))
        for row in range(8):
            edges = exact_dot(out_ref[rows(row * planes, planes), :], columns)
            for pair in range(4 * cases):
                kept = jnp.where(lanes_of((depth, 128)) // 4 == group, edges[pair * depth : (pair + 1) * depth], 0.0)
                cols_ref[0][pl.ds(pair * 8 + row, 1), :] = jnp.sum(kept, axis=0, keepdims=True)


def packed_coef(packed_ref, case):
    return [packed_ref[rows((case * N_PACKED + i) * 8), :] for i in range(N_PACKED)]


def columns_beyond(cases, side_ref, mask_ref, packed_ref, corr_ref):
    slot = lanes_of((8, 128)) % 4
    for case in range(cases):
        coefs = packed_coef(packed_ref, case)
        second, first = [], []
        for c in range(4):
            side = side_ref[rows((c * cases + case) * 8), :] * mask_ref[...]
            p1 = jnp.where(slot == 1, pltpu.roll(side, 127, 1), 0.0)
            p2 = jnp.where(slot < 2, pltpu.roll(side, 126, 1), 0.0)
            m1 = jnp.where(slot == 2, pltpu.roll(side, 1, 1), 0.0)
            m2 = jnp.where(slot >= 2, pltpu.roll(side, 2, 1), 0.0)
            second.append(16.0 * (p1 + m1) - (p2 + m2))
            first.append(8.0 * (p1 - m1) - (p2 - m2))
        for c in range(4):
            value = coefs[WEIGHT[c]] * second[c]
            if c == 0:
                value += coefs[4] * first[2]
            elif c == 2:
                value += coefs[4] * first[0]
            corr_ref[rows((c * cases + case) * 8), :] = value


def packed_edges(cases, planes, edge_ref, corr_ref, below_ref, above_ref, packed_ref, cols_ref, halo_ref):
    row = rows_of((8, 128))
    for i in range(2):
        halo_ref[strided(6 + i), :] = below_ref[rows(2 * planes + 8 * i), :]
        halo_ref[strided(i), :] = above_ref[rows(2 * planes + 8 * i), :]
    for case in range(cases):
        coefs = packed_coef(packed_ref, case)
        second, first = [], []
        for c in range(4):
            halo = halo_ref[rows((c * cases + case) * 8), :]
            m1 = pltpu.roll(jnp.where(row == 7, halo, 0.0), 1, 0)
            m2 = pltpu.roll(jnp.where(row >= 6, halo, 0.0), 2, 0)
            p1 = pltpu.roll(jnp.where(row == 0, halo, 0.0), 7, 0)
            p2 = pltpu.roll(jnp.where(row < 2, halo, 0.0), 6, 0)
            second.append(16.0 * (p1 + m1) - (p2 + m2))
            first.append(8.0 * (p1 - m1) - (p2 - m2))
        for c in range(4):
            here = rows((c * cases + case) * 8)
            value = edge_ref[here, :] + corr_ref[here, :] + coefs[WEIGHT[c]] * second[c] + coefs[3] * first[c]
            if c < 2:
                value += coefs[4] * first[1 - c]
            cols_ref[here, :] = value


def whole_rows(depth, cases, planes, inner_ref, below_ref, above_ref, coef_ref, corr_ref, lane, layer, store):
    edge = (lane < 2) | (lane >= 126)

    def one(case, _):
        for block in range(depth // 8):
            tile_rows(case, block)
        return 0

    def tile_rows(case, block):
        height = ((layer + 8 * block).astype(jnp.float32) + 0.5) / depth
        offsets = [pl.multiple_of((c * cases + case) * depth + 8 * block, 8) for c in range(4)]
        arrived = [
            [ref[rows(i * planes + offsets[c]), :] for ref in (below_ref, above_ref) for i in range(2)] for c in range(4)
        ]
        for row in (0, 1, 6, 7, 2, 3, 4, 5):

            def coef(i):
                return coef_ref[pl.ds((case * N_COEF + i) * 8 + row, 1), :]

            second, first = [], []
            for c in range(4):
                m2, m1, p1, p2 = arrived[c]
                if row == 0:
                    second.append(16.0 * m1 - m2)
                    first.append(m2 - 8.0 * m1)
                elif row == 1:
                    second.append(-m1)
                    first.append(m1)
                elif row == 6:
                    second.append(-p1)
                    first.append(-p1)
                elif row == 7:
                    second.append(16.0 * p1 - p2)
                    first.append(8.0 * p1 - p2)
            for c in range(4):
                value = inner_ref[rows(row * planes + offsets[c]), :]
                if second:
                    value += coef(SPREAD + WEIGHT[c]) * second[c] + coef(CARRY) * height * first[c]
                    if c < 2:
                        value += coef(SOUND_STEP) * first[1 - c]
                line = corr_ref[pl.ds((c * cases + case) * 8 + row, 1), :]
                moved = pltpu.roll(jnp.broadcast_to(line, (8, 128)), 2 + 32 * block, 1, stride=4, stride_axis=0)
                store(c, case, block, row, offsets[c], value + jnp.where(edge, moved, 0.0))

    lax.fori_loop(0, cases, one, 0)


def joined_kernel(
    depth,
    cases,
    inner_ref,
    edge_ref,
    below_ref,
    above_ref,
    side_ref,
    mask_ref,
    coef_ref,
    packed_ref,
    tiles_ref,
    up_ref,
    down_ref,
    cols_ref,
    corr_ref,
    halo_ref,
):
    planes = 4 * cases * depth
    lane, layer = lanes_of((8, 128)), rows_of((8, 128))
    columns_beyond(cases, side_ref, mask_ref, packed_ref, corr_ref)
    packed_edges(cases, planes, edge_ref, corr_ref, below_ref, above_ref, packed_ref, cols_ref, halo_ref)
    send_edges(cols_ref, up_ref, down_ref, planes)

    def store(c, case, block, row, offset, value):
        tiles_ref[rows(PAD + row * planes + offset), :] = value
        if row < 2:
            down_ref[rows(row * planes + offset), :] = value
        if row > 5:
            up_ref[rows((row - 6) * planes + offset), :] = value

    whole_rows(depth, cases, planes, inner_ref, below_ref, above_ref, coef_ref, corr_ref, lane, layer, store)


def final_kernel(
    depth,
    cases,
    inner_ref,
    below_ref,
    above_ref,
    side_ref,
    mask_ref,
    coef_ref,
    packed_ref,
    out_ref,
    mean_ref,
    wall_ref,
    corr_ref,
    density_ref,
    momentum_ref,
    bend_ref,
):
    planes = 4 * cases * depth
    lane, layer = lanes_of((8, 128)), rows_of((8, 128))
    columns_beyond(cases, side_ref, mask_ref, packed_ref, corr_ref)
    span = depth + 16

    def store(c, case, block, row, offset, value):
        out_ref[strided(offset * 8 + row), :] = value
        if c == 0:
            density_ref[rows(pl.multiple_of((case * 8 + row) * depth + 8 * block, 8)), :] = value
        if c == 1:
            momentum_ref[rows(pl.multiple_of((case * 8 + row) * span + 8 + 8 * block, 8)), :] = value

    whole_rows(depth, cases, planes, inner_ref, below_ref, above_ref, coef_ref, corr_ref, lane, layer, store)
    zero = jnp.zeros((8, 128), jnp.float32)
    for line in range(cases * 8):
        total, bend = zero, zero
        momentum_ref[rows(line * span), :] = zero
        momentum_ref[rows(line * span + 8 + depth), :] = zero
        for block in range(depth // 8):
            total += density_ref[rows(line * depth + 8 * block), :]
        for block in range(depth // 8 + 1):
            at = line * span + 8 + 8 * block
            change = momentum_ref[rows(at), :] - momentum_ref[rows(at - 1), :]
            bend += change * change
        mean_ref[pl.ds(line, 1), :] = jnp.sum(total, axis=0, keepdims=True)
        bend_ref[pl.ds(line, 1), :] = jnp.sum(bend, axis=0, keepdims=True)
    wall = zero
    for case in range(cases):
        wall += coef_ref[rows((case * N_COEF + BEND) * 8), :] * bend_ref[rows(case * 8), :]
    wall_ref[...] = wall


def wall_kernel(cases, wall_ref, mean_ref, below_ref, above_ref, coef_ref, grad_ref, sums_ref):
    row = rows_of((8, 128))
    grad = wall_ref[...]
    for case in range(cases):
        mean = mean_ref[rows(case * 8), :]
        halo = jnp.where(row >= 4, below_ref[rows(case * 8), :], above_ref[rows(case * 8), :])
        m1 = pltpu.roll(jnp.where(row == 7, halo, mean), 1, 0)
        m2 = pltpu.roll(jnp.where(row >= 6, halo, mean), 2, 0)
        p1 = pltpu.roll(jnp.where(row == 0, halo, mean), 7, 0)
        p2 = pltpu.roll(jnp.where(row < 2, halo, mean), 6, 0)
        grad += coef_ref[rows((case * N_COEF + FLUX) * 8), :] * (8.0 * (p1 - m1) - (p2 - m2))
    grad_ref[...] = grad
    part = jnp.sum(grad * grad, axis=0, keepdims=True)
    sums_ref[...] = jnp.broadcast_to(part[None], sums_ref.shape)


def scale_kernel(cells, grad_ref, sums_ref, out_ref):
    total = jnp.sum(sums_ref[...], axis=0)
    total = jnp.sum(total, axis=1, keepdims=True)
    out_ref[...] = grad_ref[...] / jnp.sqrt(total / cells + 1e-06)


def f32(*shape):
    return jax.ShapeDtypeStruct(shape, jnp.float32)


def call(kernel, *args, outs, scratch=(), smem=0):
    return pl.pallas_call(
        kernel,
        out_shape=outs,
        in_specs=[SM] * smem + [VM] * (len(args) - smem),
        out_specs=tuple([VM] * len(outs)),
        scratch_shapes=[pltpu.VMEM(shape, jnp.float32) for shape in scratch],
        compiler_params=PARAMS,
    )(*args)


def neighbours(axis):
    size = lax.axis_size(axis)
    up = [(i, i + 1) for i in range(size - 1)]
    return up, [(j, i) for i, j in up]


def exchange_rows(up, down):
    ahead, back = neighbours("roll")
    return lax.ppermute(up, "roll", ahead), lax.ppermute(down, "roll", back)


def exchange_columns(cols):
    ahead, back = neighbours("trans")
    if lax.axis_size("trans") == 2:
        return lax.ppermute(cols, "trans", ahead + back)
    left, right = lax.ppermute(cols, "trans", ahead), lax.ppermute(cols, "trans", back)
    return jnp.where(lanes_of(cols.shape) % 4 < 2, left, right)


def on_device(adjoint, source, pressure, film, cavity, temp_index):
    components, cases, depth, width_x, width_y = adjoint.shape
    planes = components * cases * depth
    assert (components, width_x, width_y, 4 * depth) == (4, 8, 128, 128)
    state = adjoint.reshape(planes * 8, 128)
    forcing = source.reshape(planes * 8, 128)
    place = jnp.stack([lax.axis_index("trans"), lax.axis_size("trans")]).astype(jnp.int32)
    whole, inner = f32(planes * 8 + 2 * PAD, 128), f32(planes * 8, 128)
    message, cols_shape = f32(planes * 2 + 16, 128), f32(components * cases * 8, 128)
    coef, packed, mask = call(
        functools.partial(coefficient_kernel, depth, cases),
        temp_index,
        place,
        pressure.reshape(cases * 8, 128),
        film,
        cavity.reshape(cases * 8, 128),
        outs=(f32(cases * N_COEF * 8, 128), f32(cases * N_PACKED * 8, 128), f32(8, 128)),
        smem=2,
    )
    tiles, up, down, cols = call(
        functools.partial(pack_kernel, depth, cases), state, outs=(whole, message, message, cols_shape)
    )
    for index in range(SECTIONS):
        below, above = exchange_rows(up, down)
        side = exchange_columns(cols)
        more = index < SECTIONS - 1
        part, *edges = call(
            functools.partial(inner_kernel, depth, cases),
            tiles,
            forcing,
            coef,
            outs=(inner, cols_shape) if more else (inner,),
            scratch=[(planes * 8, 256)],
        )
        arrived = (part, *edges, below, above, side, mask, coef, packed)
        if more:
            tiles, up, down, cols = call(
                functools.partial(joined_kernel, depth, cases),
                *arrived,
                outs=(whole, message, message, cols_shape),
                scratch=[cols_shape.shape] * 2,
            )
        else:
            state, mean, wall = call(
                functools.partial(final_kernel, depth, cases),
                *arrived,
                outs=(inner, f32(cases * 8, 128), f32(8, 128)),
                scratch=[
                    cols_shape.shape,
                    (cases * 8 * depth, 128),
                    (cases * 8 * (depth + 16), 128),
                    (cases * 8, 128),
                ],
            )
    below, above = exchange_rows(mean, mean)
    devices = lax.axis_size("roll") * lax.axis_size("trans")
    grad, sums = call(
        functools.partial(wall_kernel, cases), wall, mean, below, above, coef, outs=(f32(8, 128), f32(devices, 1, 128))
    )
    sums = lax.all_to_all(sums, ("roll", "trans"), 0, 0, tiled=True)
    (wall_step,) = call(functools.partial(scale_kernel, devices * width_x * width_y), grad, sums, outs=(f32(8, 128),))
    return (state.reshape(adjoint.shape), wall_step)


def solution(mesh):
    placed = (
        P(None, None, None, "roll", "trans"),
        P(None, None, None, "roll", "trans"),
        P(None, "roll", "trans"),
        P("roll", "trans"),
        P(None, "roll", "trans"),
        P(),
    )
    return jax.shard_map(
        on_device,
        mesh=mesh,
        in_specs=placed,
        out_specs=(P(None, None, None, "roll", "trans"), P("roll", "trans")),
        check_vma=False,
    )
```

```python
import functools

import jax
import jax.numpy as jnp
from jax import lax
from jax.experimental import pallas as pl
from jax.experimental.pallas import tpu as pltpu
from jax.sharding import PartitionSpec as P

SECTIONS = 2


VISCOSITY_PRESS = 0.3
VISCOSITY_TEMP = 0.5
THETA_STEP = 0.2
SOUND = 0.5
KAPPA = 0.6
HEATING = 0.3
ROLL_SPEED = 1.0
COURANT = 0.8

VM = pl.BlockSpec(memory_space=pltpu.VMEM)
SM = pl.BlockSpec(memory_space=pltpu.SMEM)
PARAMS = pltpu.CompilerParams(vmem_limit_bytes=16 * 1024 * 1024)

PAD = 8
CENTER, SPREAD, ACROSS = (0, 3, 6)
CARRY, SOUND_STEP, STEP, HEAT, FLUX, BEND = range(9, 15)
N_COEF = 15
N_PACKED = 5
TAIL = 24
TRANS, TRANS_SIZE, ODD, DEVICE = range(4)
WEIGHT = (0, 1, 1, 2)


def lanes_of(shape):
    return lax.broadcasted_iota(jnp.int32, shape, 1)


def rows_of(shape):
    return lax.broadcasted_iota(jnp.int32, shape, 0)


def rows(start, count=8):
    return pl.ds(start, count)


def strided(start):
    return pl.ds(start, 8, stride=8)


def coefficient_kernel(depth, cases, level_ref, place_ref, pressure_ref, film_ref, cavity_ref, coef_ref, packed_ref, mask_ref):
    lane, row = lanes_of((8, 128)), rows_of((8, 128))
    film = film_ref[...]
    height = ((depth - 1 - lane // 4).astype(jnp.float32) + 0.5) / depth
    for case in range(cases):
        theta = THETA_STEP * level_ref[case].astype(jnp.float32)
        viscosity = jnp.exp(VISCOSITY_PRESS * pressure_ref[rows(case * 8), :] - VISCOSITY_TEMP * theta)
        film_coef = 4.0 * viscosity / (film * film)
        density = 1.0 - 0.6 * cavity_ref[rows(case * 8), :].astype(jnp.float32)
        step = COURANT / (32.0 / 3.0 * viscosity + 4.0 * film_coef + 2.0 * SOUND + 1.0)
        planes = [None] * N_COEF
        for i, weight in enumerate((0.5, 1.0, KAPPA)):
            planes[SPREAD + i] = (weight / 12.0) * step * viscosity
            planes[ACROSS + i] = weight * step * film_coef
            planes[CENTER + i] = 1.0 - 60.0 * planes[SPREAD + i] - 2.0 * planes[ACROSS + i]
        planes[CARRY] = (ROLL_SPEED / 12.0) * step * density
        planes[SOUND_STEP] = (SOUND / 12.0) * step
        planes[STEP] = step
        planes[HEAT] = HEATING * step * viscosity
        planes[FLUX] = (ROLL_SPEED / (24.0 * depth)) * density * film
        planes[BEND] = (8.0 / depth) * viscosity / (film * film * film)
        for i, plane in enumerate(planes):
            coef_ref[rows((case * N_COEF + i) * 8), :] = plane
        wanted = jnp.concatenate(planes[SPREAD : SPREAD + 3] + [planes[CARRY], planes[SOUND_STEP]], axis=0)
        packed = exact_dot(wanted, edge_columns())
        for i in range(N_PACKED):
            plane = packed[i * 8 : i * 8 + 8]
            packed_ref[rows((case * N_PACKED + i) * 8), :] = plane * height if i == 3 else plane
    from_left = jnp.where(place_ref[TRANS] > 0, 1.0, 0.0)
    from_right = jnp.where(place_ref[TRANS] < place_ref[TRANS_SIZE] - 1, 1.0, 0.0)
    mask_ref[...] = jnp.where(lane % 4 < 2, from_left, from_right)


def edge_columns():
    source = lanes_of((128, 128)) % 4
    source = jnp.where(source < 2, 126 + source, source - 2)
    return jnp.where(rows_of((128, 128)) == source, 1.0, 0.0).astype(jnp.bfloat16)


def in_parts(value):
    high = value.astype(jnp.bfloat16)
    rest = value - high.astype(jnp.float32)
    middle = rest.astype(jnp.bfloat16)
    return jnp.concatenate([high, middle], axis=1), (rest - middle.astype(jnp.float32)).astype(jnp.bfloat16)


def exact_dot(value, weights):
    upper, low = in_parts(value)
    part = jnp.dot(upper, jnp.concatenate([weights, weights], axis=0), preferred_element_type=jnp.float32)
    return part + jnp.dot(low, weights, preferred_element_type=jnp.float32)


class Post:
    def __init__(self, place_ref, first_ref, second_ref):
        self.odd = place_ref[ODD] == 1
        self.refs = first_ref, second_ref

    def put(self, where, up, down):
        first, second = self.refs
        first[where, :] = jnp.where(self.odd, down, up)
        second[where, :] = jnp.where(self.odd, up, down)

    def get(self, where):
        first, second = (ref[where, :] for ref in self.refs)
        return jnp.where(self.odd, first, second), jnp.where(self.odd, second, first)

    def put_tiles(self, planes, first, tiles):
        for i in range(2):
            self.put(rows(i * planes + first), tiles[6 + i], tiles[i])

    def put_edges(self, planes, cols_ref):
        for i in range(2):
            self.put(rows(2 * planes + 8 * i), cols_ref[strided(6 + i), :], cols_ref[strided(i), :])


def pack_kernel(depth, cases, place_ref, state_ref, tiles_ref, first_ref, second_ref, cols_ref):
    planes = 4 * cases * depth
    lane = lanes_of((8, 128))
    post = Post(place_ref, first_ref, second_ref)

    def one(pair, _):
        held = jnp.zeros((8, 128), jnp.float32)
        for layer in range(depth):
            group = depth - 1 - layer
            plane = state_ref[rows(pl.multiple_of((pair * depth + layer) * 8, 8)), :]
            held = jnp.where(lane // 4 == group, pltpu.roll(plane, (4 * group + 2) % 128, 1), held)
        cols_ref[rows(pl.multiple_of(pair * 8, 8)), :] = held
        for block in range(depth // 8):
            first = pl.multiple_of(pair * depth + 8 * block, 8)
            tiles = [state_ref[strided(first * 8 + row), :] for row in range(8)]
            for row in range(8):
                tiles_ref[rows(PAD + row * planes + first), :] = tiles[row]
            post.put_tiles(planes, first, tiles)
        return 0

    lax.fori_loop(0, 4 * cases, one, 0)
    post.put_edges(planes, cols_ref)


def inner_kernel(depth, cases, tiles_ref, source_ref, coef_ref, *rest):
    out_ref, *more_refs, deriv_ref = rest
    planes = 4 * cases * depth
    lane, layer = lanes_of((8, 128)), rows_of((8, 128))
    gap = rows_of((128, 256)) - lanes_of((128, 256)) % 128
    second = jnp.where(jnp.abs(gap) == 1, 16.0, jnp.where(jnp.abs(gap) == 2, -1.0, 0.0))
    first = jnp.where(gap == 1, 8.0, jnp.where(gap == -1, -8.0, jnp.where(gap == 2, -1.0, jnp.where(gap == -2, 1.0, 0.0))))
    weights = jnp.where(lanes_of((128, 256)) < 128, second, first).astype(jnp.bfloat16)
    for row in range(8):
        value = tiles_ref[rows(PAD + row * planes, planes), :]
        deriv_ref[rows(row * planes, planes), :] = exact_dot(value, weights)

    def one(index, _):
        case, block = index // (depth // 8), index % (depth // 8)
        k = layer + 8 * block
        height = (k.astype(jnp.float32) + 0.5) / depth
        offsets = [pl.multiple_of((c * cases + case) * depth + 8 * block, 8) for c in range(4)]
        tiles = [[tiles_ref[rows(PAD + row * planes + offsets[c]), :] for row in range(8)] for c in range(4)]

        for row in range(8):

            def coef(i):
                return coef_ref[pl.ds((case * N_COEF + i) * 8 + row, 1), :]

            along = []
            for c in range(4):
                near = [tiles[c][row + by] if 0 <= row + by < 8 else None for by in (-2, -1, 1, 2)]
                along.append(near)

            def first_x(c):
                m2, m1, p1, p2 = along[c]
                ones = 8.0 * (p1 - m1) if m1 is not None and p1 is not None else 8.0 * p1 if m1 is None else -8.0 * m1
                if m2 is not None and p2 is not None:
                    return ones - (p2 - m2)
                return ones - p2 if m2 is None else ones + m2

            def second_x(c):
                m2, m1, p1, p2 = along[c]
                ones = 16.0 * (p1 + m1) if m1 is not None and p1 is not None else 16.0 * (p1 if m1 is None else m1)
                if m2 is not None and p2 is not None:
                    return ones - (p2 + m2)
                return ones - (p2 if m2 is None else m2)

            carry = coef(CARRY) * height
            sound = coef(SOUND_STEP)
            step = coef(STEP)
            slopes = [first_x(c) for c in range(4)]
            for c in range(4):
                here = row * planes + offsets[c]
                behind = jnp.where(k > 0, tiles_ref[rows(PAD - 1 + here), :], 0.0)
                beyond = jnp.where(k < depth - 1, tiles_ref[rows(PAD + 1 + here), :], 0.0)
                source = source_ref[strided(offsets[c] * 8 + row), :]
                w = WEIGHT[c]
                value = coef(CENTER + w) * tiles[c][row] + coef(SPREAD + w) * (second_x(c) + deriv_ref[rows(here), 0:128])
                value += coef(ACROSS + w) * (behind + beyond) + step * source + carry * slopes[c]
                if c == 0:
                    other = row * planes + offsets[2]
                    value += sound * (slopes[1] + deriv_ref[rows(other), 128:256])
                elif c == 1:
                    value += sound * slopes[0]
                elif c == 2:
                    other = row * planes + offsets[0]
                    value += sound * deriv_ref[rows(other), 128:256]
                else:
                    value += coef(HEAT) * tiles[1][row]
                out_ref[rows(here), :] = value
        return 0

    lax.fori_loop(0, cases * (depth // 8), one, 0)

    if more_refs:
        cols_ref, total_ref = more_refs
        for case in range(cases):
            for row in range(8):
                total = jnp.zeros((8, 128), jnp.float32)
                for block in range(depth // 8):
                    total += source_ref[strided((case * depth + 8 * block) * 8 + row), :]
                total_ref[pl.ds(case * 8 + row, 1), :] = jnp.sum(total, axis=0, keepdims=True)
        columns = edge_columns()
        group = (depth - 1) - rows_of((depth, 128))
        for row in range(8):
            edges = exact_dot(out_ref[rows(row * planes, planes), :], columns)
            for pair in range(4 * cases):
                kept = jnp.where(lanes_of((depth, 128)) // 4 == group, edges[pair * depth : (pair + 1) * depth], 0.0)
                cols_ref[pl.ds(pair * 8 + row, 1), :] = jnp.sum(kept, axis=0, keepdims=True)


def packed_coef(packed_ref, case):
    return [packed_ref[rows((case * N_PACKED + i) * 8), :] for i in range(N_PACKED)]


def columns_beyond(cases, side_ref, mask_ref, packed_ref, corr_ref):
    slot = lanes_of((8, 128)) % 4
    for case in range(cases):
        coefs = packed_coef(packed_ref, case)
        second, first = [], []
        for c in range(4):
            side = side_ref[rows((c * cases + case) * 8), :] * mask_ref[...]
            p1 = jnp.where(slot == 1, pltpu.roll(side, 127, 1), 0.0)
            p2 = jnp.where(slot < 2, pltpu.roll(side, 126, 1), 0.0)
            m1 = jnp.where(slot == 2, pltpu.roll(side, 1, 1), 0.0)
            m2 = jnp.where(slot >= 2, pltpu.roll(side, 2, 1), 0.0)
            second.append(16.0 * (p1 + m1) - (p2 + m2))
            first.append(8.0 * (p1 - m1) - (p2 - m2))
        for c in range(4):
            value = coefs[WEIGHT[c]] * second[c]
            if c == 0:
                value += coefs[4] * first[2]
            elif c == 2:
                value += coefs[4] * first[0]
            corr_ref[rows((c * cases + case) * 8), :] = value


def packed_edges(cases, planes, edge_ref, corr_ref, post, packed_ref, cols_ref, halo_ref):
    row = rows_of((8, 128))
    for i in range(2):
        below, above = post.get(rows(2 * planes + 8 * i))
        halo_ref[strided(6 + i), :] = below
        halo_ref[strided(i), :] = above
    for case in range(cases):
        coefs = packed_coef(packed_ref, case)
        second, first = [], []
        for c in range(4):
            halo = halo_ref[rows((c * cases + case) * 8), :]
            m1 = pltpu.roll(jnp.where(row == 7, halo, 0.0), 1, 0)
            m2 = pltpu.roll(jnp.where(row >= 6, halo, 0.0), 2, 0)
            p1 = pltpu.roll(jnp.where(row == 0, halo, 0.0), 7, 0)
            p2 = pltpu.roll(jnp.where(row < 2, halo, 0.0), 6, 0)
            second.append(16.0 * (p1 + m1) - (p2 + m2))
            first.append(8.0 * (p1 - m1) - (p2 - m2))
        for c in range(4):
            here = rows((c * cases + case) * 8)
            value = edge_ref[here, :] + corr_ref[here, :] + coefs[WEIGHT[c]] * second[c] + coefs[3] * first[c]
            if c < 2:
                value += coefs[4] * first[1 - c]
            cols_ref[here, :] = value


def whole_rows(depth, cases, planes, inner_ref, post, coef_ref, corr_ref, lane, layer, store):
    edge = (lane < 2) | (lane >= 126)

    def one(case, _):
        for block in range(depth // 8):
            tile_rows(case, block)
        return 0

    def tile_rows(case, block):
        height = ((layer + 8 * block).astype(jnp.float32) + 0.5) / depth
        offsets = [pl.multiple_of((c * cases + case) * depth + 8 * block, 8) for c in range(4)]
        arrived = []
        for c in range(4):
            pairs = [post.get(rows(i * planes + offsets[c])) for i in range(2)]
            arrived.append([pairs[0][0], pairs[1][0], pairs[0][1], pairs[1][1]])
        whole = [[None] * 8 for _ in range(4)]
        for row in (0, 1, 6, 7, 2, 3, 4, 5):

            def coef(i):
                return coef_ref[pl.ds((case * N_COEF + i) * 8 + row, 1), :]

            second, first = [], []
            for c in range(4):
                m2, m1, p1, p2 = arrived[c]
                if row == 0:
                    second.append(16.0 * m1 - m2)
                    first.append(m2 - 8.0 * m1)
                elif row == 1:
                    second.append(-m1)
                    first.append(m1)
                elif row == 6:
                    second.append(-p1)
                    first.append(-p1)
                elif row == 7:
                    second.append(16.0 * p1 - p2)
                    first.append(8.0 * p1 - p2)
            for c in range(4):
                value = inner_ref[rows(row * planes + offsets[c]), :]
                if second:
                    value += coef(SPREAD + WEIGHT[c]) * second[c] + coef(CARRY) * height * first[c]
                    if c < 2:
                        value += coef(SOUND_STEP) * first[1 - c]
                line = corr_ref[pl.ds((c * cases + case) * 8 + row, 1), :]
                moved = pltpu.roll(jnp.broadcast_to(line, (8, 128)), 2 + 32 * block, 1, stride=4, stride_axis=0)
                whole[c][row] = value + jnp.where(edge, moved, 0.0)
        for c in range(4):
            store(c, case, block, offsets[c], whole[c])

    lax.fori_loop(0, cases, one, 0)


def depth_sum(tiles):
    total = tiles[0]
    for tile in tiles[1:]:
        total = total + tile
    return jnp.sum(total, axis=0, keepdims=True)


def edge_rows(post, planes, place, plane):
    post.put(pl.ds(2 * planes + place, 2), plane[6:8], plane[0:2])


def joined_kernel(
    depth,
    cases,
    place_ref,
    inner_ref,
    edge_ref,
    source_total_ref,
    first_in_ref,
    second_in_ref,
    side_ref,
    mask_ref,
    coef_ref,
    packed_ref,
    tiles_ref,
    first_ref,
    second_ref,
    cols_ref,
    moment_ref,
    corr_ref,
    halo_ref,
):
    planes = 4 * cases * depth
    lane, layer = lanes_of((8, 128)), rows_of((8, 128))
    post, arrived = Post(place_ref, first_ref, second_ref), Post(place_ref, first_in_ref, second_in_ref)
    columns_beyond(cases, side_ref, mask_ref, packed_ref, corr_ref)
    packed_edges(cases, planes, edge_ref, corr_ref, arrived, packed_ref, cols_ref, halo_ref)

    def store(c, case, block, offset, tiles):
        for row in range(8):
            tiles_ref[rows(PAD + row * planes + offset), :] = tiles[row]
        post.put_tiles(planes, offset, tiles)

    whole_rows(depth, cases, planes, inner_ref, arrived, coef_ref, corr_ref, lane, layer, store)

    blocks = depth // 8
    for case in range(cases):
        for row in range(8):

            def tiles_of(c):
                start = PAD + row * planes + (c * cases + case) * depth
                return [tiles_ref[rows(start + 8 * block), :] for block in range(blocks)]

            density, heights = tiles_of(0), [(layer + (8 * block + 0.5)).astype(jnp.float32) / depth for block in range(blocks)]
            lines = (
                depth_sum(density),
                depth_sum([tile * height for tile, height in zip(density, heights, strict=True)]),
                depth_sum(tiles_of(1)),
                depth_sum(tiles_of(2)),
                density[0][0:1] + density[-1][7:8],
            )
            for i, line in enumerate(lines):
                moment_ref[pl.ds((case * 5 + i) * 8 + row, 1), :] = line
    for case in range(cases):

        def coef(i):
            return coef_ref[rows((case * N_COEF + i) * 8), :]

        total, lifted, along, across, walls = (moment_ref[rows((case * 5 + i) * 8), :] for i in range(5))

        def x_parts(plane):
            m1, m2 = jnp.where(layer >= 1, pltpu.roll(plane, 1, 0), 0.0), jnp.where(layer >= 2, pltpu.roll(plane, 2, 0), 0.0)
            p1, p2 = jnp.where(layer < 7, pltpu.roll(plane, 7, 0), 0.0), jnp.where(layer < 6, pltpu.roll(plane, 6, 0), 0.0)
            return 16.0 * (p1 + m1) - (p2 + m2), 8.0 * (p1 - m1) - (p2 - m2)

        def y_parts(plane):
            m1, m2 = jnp.where(lane >= 1, pltpu.roll(plane, 1, 1), 0.0), jnp.where(lane >= 2, pltpu.roll(plane, 2, 1), 0.0)
            p1, p2 = jnp.where(lane < 127, pltpu.roll(plane, 127, 1), 0.0), jnp.where(lane < 126, pltpu.roll(plane, 126, 1), 0.0)
            return 16.0 * (p1 + m1) - (p2 + m2), 8.0 * (p1 - m1) - (p2 - m2)

        value = coef(CENTER) * total + coef(SPREAD) * (x_parts(total)[0] + y_parts(total)[0])
        value += coef(ACROSS) * (2.0 * total - walls) + coef(CARRY) * x_parts(lifted)[1]
        value += coef(SOUND_STEP) * (x_parts(along)[1] + y_parts(across)[1]) + coef(STEP) * source_total_ref[rows(case * 8), :]
        sent = (value, coef(SPREAD), coef(CARRY), coef(SOUND_STEP), coef(FLUX))
        for i, plane in enumerate(sent):
            edge_rows(post, planes, (case * 5 + i) * 2, plane)


def edge_sums(tile):
    for by in (4, 8, 16, 32, 64):
        tile = tile + pltpu.roll(tile, by, 1)
    return pltpu.roll(tile, 2, 1)


def final_kernel(
    depth,
    cases,
    place_ref,
    inner_ref,
    first_in_ref,
    second_in_ref,
    side_ref,
    mask_ref,
    coef_ref,
    packed_ref,
    moment_ref,
    out_ref,
    grad_ref,
    sums_ref,
    corr_ref,
    density_ref,
    momentum_ref,
    mean_ref,
    bend_ref,
):
    planes = 4 * cases * depth
    lane, layer = lanes_of((8, 128)), rows_of((8, 128))
    arrived = Post(place_ref, first_in_ref, second_in_ref)
    columns_beyond(cases, side_ref, mask_ref, packed_ref, corr_ref)
    span = depth + 16

    def store(c, case, block, offset, tiles):
        for row in range(8):
            out_ref[strided(offset * 8 + row), :] = tiles[row]
            if c == 0:
                density_ref[rows(pl.multiple_of((case * 8 + row) * depth + 8 * block, 8)), :] = tiles[row]
            if c == 1:
                momentum_ref[rows(pl.multiple_of((case * 8 + row) * span + 8 + 8 * block, 8)), :] = tiles[row]

    whole_rows(depth, cases, planes, inner_ref, arrived, coef_ref, corr_ref, lane, layer, store)
    zero = jnp.zeros((8, 128), jnp.float32)
    for line in range(cases * 8):
        bend = zero
        momentum_ref[rows(line * span), :] = zero
        momentum_ref[rows(line * span + 8 + depth), :] = zero
        for block in range(depth // 8 + 1):
            at = line * span + 8 + 8 * block
            change = momentum_ref[rows(at), :] - momentum_ref[rows(at - 1), :]
            bend += change * change
        mean_ref[pl.ds(line, 1), :] = depth_sum([density_ref[rows(line * depth + 8 * block), :] for block in range(depth // 8)])
        bend_ref[pl.ds(line, 1), :] = jnp.sum(bend, axis=0, keepdims=True)

    grad, missing = zero, zero
    for case in range(cases):

        def coef(i):
            return coef_ref[rows((case * N_COEF + i) * 8), :]

        pairs = [arrived.get(pl.ds(2 * planes + (case * 5 + i) * 2, 2)) for i in range(5)]
        below, above = [pair[0] for pair in pairs], [pair[1] for pair in pairs]
        total, lifted, along = (moment_ref[rows((case * 5 + i) * 8), :] for i in range(3))

        def beyond(plane):
            first, second, last, before = plane[0:1], plane[1:2], plane[7:8], plane[6:7]
            none = jnp.zeros((1, 128), jnp.float32)
            down = (jnp.concatenate([-first, 16.0 * first - second], 0), jnp.concatenate([-first, 8.0 * first - second], 0))
            up = (jnp.concatenate([16.0 * last - before, -last], 0), jnp.concatenate([before - 8.0 * last, last], 0))
            return down, up, none

        down, up, _ = zip(beyond(total), beyond(lifted), beyond(along), strict=True)
        mean_below = below[0] + below[1] * down[0][0] + below[2] * down[1][1] + below[3] * down[2][1]
        mean_above = above[0] + above[1] * up[0][0] + above[2] * up[1][1] + above[3] * up[2][1]
        mean = mean_ref[rows(case * 8), :]
        halo = jnp.concatenate([mean_above, zero[0:4], mean_below], axis=0)
        m1 = pltpu.roll(jnp.where(layer == 7, halo, mean), 1, 0)
        m2 = pltpu.roll(jnp.where(layer >= 6, halo, mean), 2, 0)
        p1 = pltpu.roll(jnp.where(layer == 0, halo, mean), 7, 0)
        p2 = pltpu.roll(jnp.where(layer < 2, halo, mean), 6, 0)
        grad += coef(FLUX) * (8.0 * (p1 - m1) - (p2 - m2)) + coef(BEND) * bend_ref[rows(case * 8), :]
        change = edge_sums(corr_ref[rows(case * 8), :])
        down_rows = jnp.concatenate([change[6:7] - 8.0 * change[7:8], change[7:8]], axis=0)
        up_rows = jnp.concatenate([-change[0:1], 8.0 * change[0:1] - change[1:2]], axis=0)
        missing += jnp.concatenate([above[4] * down_rows, zero[0:4], below[4] * up_rows], axis=0)
    corner = ((lane < 2) | (lane >= 126)) & ((layer < 2) | (layer >= 6))
    grad_ref[...] = grad
    inside = jnp.where(corner, 0.0, grad)
    rest = jnp.sum(inside * inside, axis=0, keepdims=True)
    corners = pltpu.roll(jnp.where(corner, grad, 0.0), 2, 1, stride=4, stride_axis=0)
    shares = pltpu.roll(jnp.where(corner, missing, 0.0), 34, 1, stride=4, stride_axis=0)
    line = jnp.sum(corners + shares, axis=0, keepdims=True)
    line = jnp.where(lanes_of((1, 128)) < 64, line, rest + pltpu.roll(rest, 64, 1))
    sums_ref[...] = jnp.broadcast_to(line[None], sums_ref.shape)


def scale_kernel(cells, devices, trans, place_ref, grad_ref, sums_ref, out_ref, lines_ref, shares_ref):
    pad = -(-trans // 8) * 8
    lane, row = lanes_of((8, 128)), rows_of((8, 128))
    zero = jnp.zeros((pad, 128), jnp.float32)
    lines_ref[rows(0, pad), :] = zero
    lines_ref[rows(pad + devices, pad), :] = zero
    for device in range(devices):
        lines_ref[pl.ds(pad + device, 1), :] = sums_ref[device]
    total = jnp.zeros((8, 128), jnp.float32)
    for block in range(devices // 8):
        here = lines_ref[rows(pad + 8 * block), :]
        below, above = lines_ref[rows(pad - trans + 8 * block), :], lines_ref[rows(pad + trans + 8 * block), :]
        share = pltpu.roll(jnp.where(lane < 48, below, above), 96, 1)
        shares_ref[rows(8 * block), :] = share
        corner = here + share
        total += jnp.where(lane < 32, corner * corner, jnp.where(lane >= 64, here, 0.0))
    total = jnp.sum(jnp.sum(total, axis=0, keepdims=True), axis=1, keepdims=True)
    own = jnp.broadcast_to(shares_ref[pl.ds(place_ref[DEVICE], 1), :], (8, 128))
    grad = grad_ref[...]
    edge = (lane < 2) | (lane >= 126)
    for i in (0, 1, 6, 7):
        grad += jnp.where((row == i) & edge, pltpu.roll(own, (126 - 4 * i) % 128, 1), 0.0)
    out_ref[...] = grad / jnp.sqrt(total / cells + 1e-06)


def f32(*shape):
    return jax.ShapeDtypeStruct(shape, jnp.float32)


def call(kernel, *args, outs, scratch=(), smem=0):
    return pl.pallas_call(
        kernel,
        out_shape=outs,
        in_specs=[SM] * smem + [VM] * (len(args) - smem),
        out_specs=tuple([VM] * len(outs)),
        scratch_shapes=[pltpu.VMEM(shape, jnp.float32) for shape in scratch],
        compiler_params=PARAMS,
    )(*args)


def neighbours(axis):
    size = lax.axis_size(axis)
    up = [(i, i + 1) for i in range(size - 1)]
    return up, [(j, i) for i, j in up]


def exchange_rows(first, second):
    size = lax.axis_size("roll")
    inner = [(i, i ^ 1) for i in range(size) if i ^ 1 < size]
    outer = [pair for i in range(1, size - 1, 2) for pair in ((i, i + 1), (i + 1, i))]
    return lax.ppermute(first, "roll", inner), lax.ppermute(second, "roll", outer)


def exchange_columns(cols):
    ahead, back = neighbours("trans")
    if lax.axis_size("trans") == 2:
        return lax.ppermute(cols, "trans", ahead + back)
    left, right = lax.ppermute(cols, "trans", ahead), lax.ppermute(cols, "trans", back)
    return jnp.where(lanes_of(cols.shape) % 4 < 2, left, right)


def on_device(adjoint, source, pressure, film, cavity, temp_index):
    components, cases, depth, width_x, width_y = adjoint.shape
    planes = components * cases * depth
    assert (components, width_x, width_y, 4 * depth) == (4, 8, 128, 128)
    state = adjoint.reshape(planes * 8, 128)
    forcing = source.reshape(planes * 8, 128)
    roll, trans, trans_size = lax.axis_index("roll"), lax.axis_index("trans"), lax.axis_size("trans")
    place = jnp.stack([trans, trans_size, roll % 2, roll * trans_size + trans]).astype(jnp.int32)
    devices = lax.axis_size("roll") * trans_size
    whole, inner = f32(planes * 8 + 2 * PAD, 128), f32(planes * 8, 128)
    message, cols_shape = f32(planes * 2 + TAIL, 128), f32(components * cases * 8, 128)
    coef, packed, mask = call(
        functools.partial(coefficient_kernel, depth, cases),
        temp_index,
        place,
        pressure.reshape(cases * 8, 128),
        film,
        cavity.reshape(cases * 8, 128),
        outs=(f32(cases * N_COEF * 8, 128), f32(cases * N_PACKED * 8, 128), f32(8, 128)),
        smem=2,
    )
    tiles, first, second, cols = call(
        functools.partial(pack_kernel, depth, cases), place, state, outs=(whole, message, message, cols_shape), smem=1
    )
    for index in range(SECTIONS):
        first, second = exchange_rows(first, second)
        side = exchange_columns(cols)
        more = index < SECTIONS - 1
        part, *edges = call(
            functools.partial(inner_kernel, depth, cases),
            tiles,
            forcing,
            coef,
            outs=(inner, cols_shape, f32(cases * 8, 128)) if more else (inner,),
            scratch=[(planes * 8, 256)],
        )
        arrived = (place, part, *edges, first, second, side, mask, coef, packed)
        if more:
            tiles, first, second, cols, moments = call(
                functools.partial(joined_kernel, depth, cases),
                *arrived,
                outs=(whole, message, message, cols_shape, f32(cases * 5 * 8, 128)),
                scratch=[cols_shape.shape] * 2,
                smem=1,
            )
        else:
            state, grad, sums = call(
                functools.partial(final_kernel, depth, cases),
                *arrived,
                moments,
                outs=(inner, f32(8, 128), f32(devices, 1, 128)),
                scratch=[
                    cols_shape.shape,
                    (cases * 8 * depth, 128),
                    (cases * 8 * (depth + 16), 128),
                    (cases * 8, 128),
                    (cases * 8, 128),
                ],
                smem=1,
            )
    sums = lax.all_to_all(sums, ("roll", "trans"), 0, 0, tiled=True)
    pad = -(-trans_size // 8) * 8
    (wall_step,) = call(
        functools.partial(scale_kernel, devices * width_x * width_y, devices, trans_size),
        place,
        grad,
        sums,
        outs=(f32(8, 128),),
        scratch=[(devices + 2 * pad, 128), (devices, 128)],
        smem=1,
    )
    return (state.reshape(adjoint.shape), wall_step)


def solution(mesh):
    placed = (
        P(None, None, None, "roll", "trans"),
        P(None, None, None, "roll", "trans"),
        P(None, "roll", "trans"),
        P("roll", "trans"),
        P(None, "roll", "trans"),
        P(),
    )
    return jax.shard_map(
        on_device,
        mesh=mesh,
        in_specs=placed,
        out_specs=(P(None, None, None, "roll", "trans"), P("roll", "trans")),
        check_vma=False,
    )
```

```python
import functools

import jax
import jax.numpy as jnp
from jax import lax
from jax.experimental import pallas as pl
from jax.experimental.pallas import tpu as pltpu
from jax.sharding import PartitionSpec as P

SECTIONS = 2


VISCOSITY_PRESS = 0.3
VISCOSITY_TEMP = 0.5
THETA_STEP = 0.2
SOUND = 0.5
KAPPA = 0.6
HEATING = 0.3
ROLL_SPEED = 1.0
COURANT = 0.8

VM = pl.BlockSpec(memory_space=pltpu.VMEM)
SM = pl.BlockSpec(memory_space=pltpu.SMEM)
HB = pl.BlockSpec(memory_space=pltpu.HBM)
PARAMS = pltpu.CompilerParams(vmem_limit_bytes=16 * 1024 * 1024)

PAD = 8
CENTER, SPREAD, ACROSS = (0, 3, 6)
CARRY, SOUND_STEP, STEP, HEAT, FLUX, BEND = range(9, 15)
N_COEF = 15
N_PACKED = 4
PIECES = 4
TAIL = 24
MIDDLE, OUTER = (2, 3, 4, 5), (0, 1, 6, 7)
TRANS, TRANS_SIZE, ODD, DEVICE = range(4)
WEIGHT = (0, 1, 1, 2)


def lanes_of(shape):
    return lax.broadcasted_iota(jnp.int32, shape, 1)


def rows_of(shape):
    return lax.broadcasted_iota(jnp.int32, shape, 0)


def rows(start, count=8):
    return pl.ds(start, count)


def strided(start):
    return pl.ds(start, 8, stride=8)


def coefficient_kernel(depth, cases, level_ref, place_ref, pressure_ref, film_ref, cavity_ref, coef_ref, packed_ref, mask_ref):
    lane, row = lanes_of((8, 128)), rows_of((8, 128))
    film = film_ref[...]
    for case in range(cases):
        theta = THETA_STEP * level_ref[case].astype(jnp.float32)
        viscosity = jnp.exp(VISCOSITY_PRESS * pressure_ref[rows(case * 8), :] - VISCOSITY_TEMP * theta)
        film_coef = 4.0 * viscosity / (film * film)
        density = 1.0 - 0.6 * cavity_ref[rows(case * 8), :].astype(jnp.float32)
        step = COURANT / (32.0 / 3.0 * viscosity + 4.0 * film_coef + 2.0 * SOUND + 1.0)
        planes = [None] * N_COEF
        for i, weight in enumerate((0.5, 1.0, KAPPA)):
            planes[SPREAD + i] = (weight / 12.0) * step * viscosity
            planes[ACROSS + i] = weight * step * film_coef
            planes[CENTER + i] = 1.0 - 60.0 * planes[SPREAD + i] - 2.0 * planes[ACROSS + i]
        planes[CARRY] = (ROLL_SPEED / 12.0) * step * density
        planes[SOUND_STEP] = (SOUND / 12.0) * step
        planes[STEP] = step
        planes[HEAT] = HEATING * step * viscosity
        planes[FLUX] = (ROLL_SPEED / (24.0 * depth)) * density * film
        planes[BEND] = (8.0 / depth) * viscosity / (film * film * film)
        for i, plane in enumerate(planes):
            coef_ref[rows((case * N_COEF + i) * 8), :] = plane
        wanted = jnp.concatenate(planes[SPREAD : SPREAD + 3] + [planes[SOUND_STEP]], axis=0)
        packed = exact_dot(wanted, edge_columns())
        for i in range(N_PACKED):
            packed_ref[rows((case * N_PACKED + i) * 8), :] = packed[i * 8 : i * 8 + 8]
    from_left = jnp.where(place_ref[TRANS] > 0, 1.0, 0.0)
    from_right = jnp.where(place_ref[TRANS] < place_ref[TRANS_SIZE] - 1, 1.0, 0.0)
    mask_ref[...] = jnp.where(lane % 4 < 2, from_left, from_right)


def edge_columns():
    source = lanes_of((128, 128)) % 4
    source = jnp.where(source < 2, 126 + source, source - 2)
    return jnp.where(rows_of((128, 128)) == source, 1.0, 0.0).astype(jnp.bfloat16)


def in_parts(value):
    high = value.astype(jnp.bfloat16)
    rest = value - high.astype(jnp.float32)
    middle = rest.astype(jnp.bfloat16)
    return jnp.concatenate([high, middle], axis=1), (rest - middle.astype(jnp.float32)).astype(jnp.bfloat16)


def exact_dot(value, weights):
    upper, low = in_parts(value)
    part = jnp.dot(upper, jnp.concatenate([weights, weights], axis=0), preferred_element_type=jnp.float32)
    return part + jnp.dot(low, weights, preferred_element_type=jnp.float32)


class Post:
    def __init__(self, place_ref, first_ref, second_ref):
        self.odd = place_ref[ODD] == 1
        self.refs = first_ref, second_ref

    def put(self, where, up, down):
        first, second = self.refs
        first[where, :] = jnp.where(self.odd, down, up)
        second[where, :] = jnp.where(self.odd, up, down)

    def get(self, where):
        first, second = (ref[where, :] for ref in self.refs)
        return jnp.where(self.odd, first, second), jnp.where(self.odd, second, first)

    def put_tiles(self, planes, first, tiles):
        for i in range(2):
            self.put(rows(i * planes + first), tiles[6 + i], tiles[i])


def row_place(refs, row, planes):
    if row in MIDDLE:
        return refs[0], PAD + MIDDLE.index(row) * planes
    return refs[1], PAD + OUTER.index(row) * planes


def send_kernel(depth, cases, place_ref, state_ref, copy_ref, first_ref, second_ref, sems):
    planes = 4 * cases * depth
    post = Post(place_ref, first_ref, second_ref)

    def piece(i):
        here = rows(i * (planes * 8 // PIECES), planes * 8 // PIECES)
        return pltpu.make_async_copy(state_ref.at[here, :], copy_ref.at[here, :], sems.at[i])

    for i in range(PIECES):
        piece(i).start()
    for i in range(PIECES):
        piece(i).wait()
        for first in range(i * planes // PIECES, (i + 1) * planes // PIECES, 8):
            post.put_tiles(planes, first, {row: copy_ref[strided(first * 8 + row), :] for row in (0, 1, 6, 7)})


def pack_kernel(depth, cases, state_ref, source_ref, middle_ref, outer_ref, cols_ref, copy_ref, sem):
    planes = 4 * cases * depth
    lane = lanes_of((8, 128))
    copy = pltpu.make_async_copy(source_ref, copy_ref, sem)
    copy.start()

    def one(pair, _):
        held = jnp.zeros((8, 128), jnp.float32)
        for layer in range(depth):
            group = depth - 1 - layer
            plane = state_ref[rows(pl.multiple_of((pair * depth + layer) * 8, 8)), :]
            held = jnp.where(lane // 4 == group, pltpu.roll(plane, (4 * group + 2) % 128, 1), held)
        cols_ref[rows(pl.multiple_of(pair * 8, 8)), :] = held
        for row in range(8):
            for block in range(depth // 8):
                first = pl.multiple_of(pair * depth + 8 * block, 8)
                ref, place = row_place((middle_ref, outer_ref), row, planes)
                ref[rows(place + first), :] = state_ref[strided(first * 8 + row), :]
        return 0

    lax.fori_loop(0, 4 * cases, one, 0)
    copy.wait()


def columns_kernel(depth, cases, middle_ref, outer_ref, cols_ref):
    planes = 4 * cases * depth
    columns = edge_columns()
    mine = lanes_of((depth, 128)) // 4 == (depth - 1) - rows_of((depth, 128))
    for row in range(8):
        ref, place = row_place((middle_ref, outer_ref), row, planes)
        edges = exact_dot(ref[rows(place, planes), :], columns)
        for pair in range(4 * cases):
            kept = jnp.where(mine, edges[pair * depth : (pair + 1) * depth], 0.0)
            cols_ref[pl.ds(pair * 8 + row, 1), :] = jnp.sum(kept, axis=0, keepdims=True)


def inner_kernel(depth, cases, middle_ref, outer_ref, source_ref, coef_ref, *rest):
    out_ref, *more_refs, deriv_ref = rest
    planes = 4 * cases * depth
    lane, layer = lanes_of((8, 128)), rows_of((8, 128))
    gap = rows_of((128, 256)) - lanes_of((128, 256)) % 128
    second = jnp.where(jnp.abs(gap) == 1, 16.0, jnp.where(jnp.abs(gap) == 2, -1.0, 0.0))
    first = jnp.where(gap == 1, 8.0, jnp.where(gap == -1, -8.0, jnp.where(gap == 2, -1.0, jnp.where(gap == -2, 1.0, 0.0))))
    weights = jnp.where(lanes_of((128, 256)) < 128, second, first).astype(jnp.bfloat16)
    for row in range(8):
        ref, place = row_place((middle_ref, outer_ref), row, planes)
        value = ref[rows(place, planes), :]
        deriv_ref[rows(row * planes, planes), :] = exact_dot(value, weights)

    def one(index, _):
        case, block = index // (depth // 8), index % (depth // 8)
        k = layer + 8 * block
        height = (k.astype(jnp.float32) + 0.5) / depth
        offsets = [pl.multiple_of((c * cases + case) * depth + 8 * block, 8) for c in range(4)]
        places = [row_place((middle_ref, outer_ref), row, planes) for row in range(8)]
        tiles = [[ref[rows(place + offsets[c]), :] for ref, place in places] for c in range(4)]

        for row in range(8):

            def coef(i):
                return coef_ref[pl.ds((case * N_COEF + i) * 8 + row, 1), :]

            along = []
            for c in range(4):
                near = [tiles[c][row + by] if 0 <= row + by < 8 else None for by in (-2, -1, 1, 2)]
                along.append(near)

            def first_x(c):
                m2, m1, p1, p2 = along[c]
                ones = 8.0 * (p1 - m1) if m1 is not None and p1 is not None else 8.0 * p1 if m1 is None else -8.0 * m1
                if m2 is not None and p2 is not None:
                    return ones - (p2 - m2)
                return ones - p2 if m2 is None else ones + m2

            def second_x(c):
                m2, m1, p1, p2 = along[c]
                ones = 16.0 * (p1 + m1) if m1 is not None and p1 is not None else 16.0 * (p1 if m1 is None else m1)
                if m2 is not None and p2 is not None:
                    return ones - (p2 + m2)
                return ones - (p2 if m2 is None else m2)

            carry = coef(CARRY) * height
            sound = coef(SOUND_STEP)
            step = coef(STEP)
            slopes = [first_x(c) for c in range(4)]
            for c in range(4):
                here = row * planes + offsets[c]
                ref, place = places[row]
                behind = jnp.where(k > 0, ref[rows(place + offsets[c] - 1), :], 0.0)
                beyond = jnp.where(k < depth - 1, ref[rows(place + offsets[c] + 1), :], 0.0)
                source = source_ref[strided(offsets[c] * 8 + row), :]
                w = WEIGHT[c]
                value = coef(CENTER + w) * tiles[c][row] + coef(SPREAD + w) * (second_x(c) + deriv_ref[rows(here), 0:128])
                value += coef(ACROSS + w) * (behind + beyond) + step * source + carry * slopes[c]
                if c == 0:
                    other = row * planes + offsets[2]
                    value += sound * (slopes[1] + deriv_ref[rows(other), 128:256])
                elif c == 1:
                    value += sound * slopes[0]
                elif c == 2:
                    other = row * planes + offsets[0]
                    value += sound * deriv_ref[rows(other), 128:256]
                else:
                    value += coef(HEAT) * tiles[1][row]
                out_ref[rows(here), :] = value
        return 0

    lax.fori_loop(0, cases * (depth // 8), one, 0)

    if more_refs:
        (total_ref,) = more_refs
        for case in range(cases):
            for row in range(8):
                total = jnp.zeros((8, 128), jnp.float32)
                for block in range(depth // 8):
                    total += source_ref[strided((case * depth + 8 * block) * 8 + row), :]
                total_ref[pl.ds(case * 8 + row, 1), :] = jnp.sum(total, axis=0, keepdims=True)


def columns_beyond(cases, side_ref, mask_ref, packed_ref, corr_ref):
    slot = lanes_of((8, 128)) % 4
    for case in range(cases):
        coefs = [packed_ref[rows((case * N_PACKED + i) * 8), :] for i in range(N_PACKED)]
        second, first = [], []
        for c in range(4):
            side = side_ref[rows((c * cases + case) * 8), :] * mask_ref[...]
            p1 = jnp.where(slot == 1, pltpu.roll(side, 127, 1), 0.0)
            p2 = jnp.where(slot < 2, pltpu.roll(side, 126, 1), 0.0)
            m1 = jnp.where(slot == 2, pltpu.roll(side, 1, 1), 0.0)
            m2 = jnp.where(slot >= 2, pltpu.roll(side, 2, 1), 0.0)
            second.append(16.0 * (p1 + m1) - (p2 + m2))
            first.append(8.0 * (p1 - m1) - (p2 - m2))
        for c in range(4):
            value = coefs[WEIGHT[c]] * second[c]
            if c == 0:
                value += coefs[3] * first[2]
            elif c == 2:
                value += coefs[3] * first[0]
            corr_ref[rows((c * cases + case) * 8), :] = value


def depth_sum(tiles):
    total = tiles[0]
    for tile in tiles[1:]:
        total = total + tile
    return jnp.sum(total, axis=0, keepdims=True)


def next_moments(depth, tiles_of, layer):
    density = tiles_of(0)
    heights = [(layer + (8 * block + 0.5)).astype(jnp.float32) / depth for block in range(depth // 8)]
    return (
        depth_sum(density),
        depth_sum([tile * height for tile, height in zip(density, heights, strict=True)]),
        depth_sum(tiles_of(1)),
        depth_sum(tiles_of(2)),
        density[0][0:1] + density[-1][7:8],
    )


def wall_sums(depth, tiles_of, layer):
    momentum, before = tiles_of(1), tiles_of(1, -1)
    changes = [momentum[0] - jnp.where(layer > 0, before[0], 0.0)]
    changes += [here - there for here, there in zip(momentum[1:], before[1:], strict=True)]
    squares = [change * change for change in changes] + [jnp.where(layer == 7, momentum[-1] * momentum[-1], 0.0)]
    return depth_sum(tiles_of(0)), depth_sum(squares)


def line_sums(depth, cases, planes, sums, ref, which, out_ref, layer):
    for case in range(cases):
        for i, row in enumerate(which):

            def tiles_of(c, by=0):
                start = PAD + i * planes + (c * cases + case) * depth
                return [ref[rows(start + by + 8 * block), :] for block in range(depth // 8)]

            lines = sums(depth, tiles_of, layer)
            for n, line in enumerate(lines):
                out_ref[pl.ds((case * len(lines) + n) * 8 + row, 1), :] = line


def joined_sums(middle_ref, outer_ref, index, layer):
    return jnp.where((layer >= 2) & (layer < 6), middle_ref[rows(index * 8), :], outer_ref[rows(index * 8), :])


def sides_kernel(depth, cases, sums, inner_ref, side_ref, mask_ref, packed_ref, middle_ref, loose_ref, sums_ref, corr_ref):
    planes = 4 * cases * depth
    lane, layer = lanes_of((8, 128)), rows_of((8, 128))
    edge = (lane < 2) | (lane >= 126)
    columns_beyond(cases, side_ref, mask_ref, packed_ref, corr_ref)

    def one(case, _):
        for row in range(8):
            for c in range(4):
                line = jnp.broadcast_to(corr_ref[pl.ds((c * cases + case) * 8 + row, 1), :], (8, 128))
                for block in range(depth // 8):
                    offset = pl.multiple_of((c * cases + case) * depth + 8 * block, 8)
                    moved = pltpu.roll(line, 2 + 32 * block, 1, stride=4, stride_axis=0)
                    value = inner_ref[rows(row * planes + offset), :] + jnp.where(edge, moved, 0.0)
                    ref, place = row_place((middle_ref, loose_ref), row, planes)
                    ref[rows(place + offset), :] = value
        return 0

    lax.fori_loop(0, cases, one, 0)
    line_sums(depth, cases, planes, sums, middle_ref, MIDDLE, sums_ref, layer)


def outer_rows(depth, cases, planes, parts, loose_ref, post, coef_ref, store):
    layer = rows_of((8, 128))

    def one(case, _):
        for block in range(depth // 8):
            height = ((layer + 8 * block).astype(jnp.float32) + 0.5) / depth
            offsets = [pl.multiple_of((c * cases + case) * depth + 8 * block, 8) for c in range(4)]
            near = {c: [post.get(rows(i * planes + offsets[c])) for i in range(2)] for c in {*parts, *range(2)}}
            whole = {c: {} for c in parts}
            for i, row in enumerate(OUTER):

                def coef(n):
                    return coef_ref[pl.ds((case * N_COEF + n) * 8 + row, 1), :]

                second, first = {}, {}
                for c, ((m2, p1), (m1, p2)) in near.items():
                    if row == 0:
                        second[c], first[c] = 16.0 * m1 - m2, m2 - 8.0 * m1
                    elif row == 1:
                        second[c], first[c] = -m1, m1
                    elif row == 6:
                        second[c], first[c] = -p1, -p1
                    else:
                        second[c], first[c] = 16.0 * p1 - p2, 8.0 * p1 - p2
                for c in parts:
                    value = loose_ref[rows(PAD + i * planes + offsets[c]), :]
                    value += coef(SPREAD + WEIGHT[c]) * second[c] + coef(CARRY) * height * first[c]
                    if c < 2:
                        value += coef(SOUND_STEP) * first[1 - c]
                    whole[c][row] = value
            for c in parts:
                store(c, case, block, offsets[c], whole[c])
        return 0

    lax.fori_loop(0, cases, one, 0)


def joined_kernel(
    depth,
    cases,
    place_ref,
    loose_ref,
    middle_sums_ref,
    source_total_ref,
    first_in_ref,
    second_in_ref,
    coef_ref,
    outer_ref,
    first_ref,
    second_ref,
    moment_ref,
    outer_sums_ref,
):
    planes = 4 * cases * depth
    lane, layer = lanes_of((8, 128)), rows_of((8, 128))
    post, arrived = Post(place_ref, first_ref, second_ref), Post(place_ref, first_in_ref, second_in_ref)

    def store(c, case, block, offset, tiles):
        for i, row in enumerate(OUTER):
            outer_ref[rows(PAD + i * planes + offset), :] = tiles[row]
        post.put_tiles(planes, offset, tiles)

    outer_rows(depth, cases, planes, range(4), loose_ref, arrived, coef_ref, store)

    line_sums(depth, cases, planes, next_moments, outer_ref, OUTER, outer_sums_ref, layer)
    for case in range(cases):

        def coef(i):
            return coef_ref[rows((case * N_COEF + i) * 8), :]

        moments = [joined_sums(middle_sums_ref, outer_sums_ref, case * 5 + i, layer) for i in range(5)]
        total, lifted, along, across, walls = moments
        for i in range(3):
            moment_ref[rows((case * 3 + i) * 8), :] = moments[i]

        def x_parts(plane):
            m1, m2 = jnp.where(layer >= 1, pltpu.roll(plane, 1, 0), 0.0), jnp.where(layer >= 2, pltpu.roll(plane, 2, 0), 0.0)
            p1, p2 = jnp.where(layer < 7, pltpu.roll(plane, 7, 0), 0.0), jnp.where(layer < 6, pltpu.roll(plane, 6, 0), 0.0)
            return 16.0 * (p1 + m1) - (p2 + m2), 8.0 * (p1 - m1) - (p2 - m2)

        def y_parts(plane):
            m1, m2 = jnp.where(lane >= 1, pltpu.roll(plane, 1, 1), 0.0), jnp.where(lane >= 2, pltpu.roll(plane, 2, 1), 0.0)
            p1, p2 = jnp.where(lane < 127, pltpu.roll(plane, 127, 1), 0.0), jnp.where(lane < 126, pltpu.roll(plane, 126, 1), 0.0)
            return 16.0 * (p1 + m1) - (p2 + m2), 8.0 * (p1 - m1) - (p2 - m2)

        value = coef(CENTER) * total + coef(SPREAD) * (x_parts(total)[0] + y_parts(total)[0])
        value += coef(ACROSS) * (2.0 * total - walls) + coef(CARRY) * x_parts(lifted)[1]
        value += coef(SOUND_STEP) * (x_parts(along)[1] + y_parts(across)[1]) + coef(STEP) * source_total_ref[rows(case * 8), :]
        sent = (value, coef(SPREAD), coef(CARRY), coef(SOUND_STEP), coef(FLUX))
        for i, plane in enumerate(sent):
            post.put(pl.ds(2 * planes + (case * 5 + i) * 2, 2), plane[6:8], plane[0:2])


def edge_sums(tile):
    for by in (4, 8, 16, 32, 64):
        tile = tile + pltpu.roll(tile, by, 1)
    return pltpu.roll(tile, 2, 1)


def final_kernel(
    depth,
    cases,
    place_ref,
    loose_ref,
    middle_sums_ref,
    corr_ref,
    first_in_ref,
    second_in_ref,
    coef_ref,
    moment_ref,
    outer_ref,
    grad_ref,
    line_ref,
    outer_sums_ref,
):
    planes = 4 * cases * depth
    lane, layer = lanes_of((8, 128)), rows_of((8, 128))
    arrived = Post(place_ref, first_in_ref, second_in_ref)

    def store(c, case, block, offset, tiles):
        for i, row in enumerate(OUTER):
            outer_ref[rows(PAD + i * planes + offset), :] = tiles[row]

    outer_rows(depth, cases, planes, range(2), loose_ref, arrived, coef_ref, store)
    line_sums(depth, cases, planes, wall_sums, outer_ref, OUTER, outer_sums_ref, layer)

    zero = jnp.zeros((8, 128), jnp.float32)
    grad, missing = zero, zero
    for case in range(cases):

        def coef(i):
            return coef_ref[rows((case * N_COEF + i) * 8), :]

        pairs = [arrived.get(pl.ds(2 * planes + (case * 5 + i) * 2, 2)) for i in range(5)]
        below, above = [pair[0] for pair in pairs], [pair[1] for pair in pairs]
        total, lifted, along = (moment_ref[rows((case * 3 + i) * 8), :] for i in range(3))

        def beyond(plane):
            first, second, last, before = plane[0:1], plane[1:2], plane[7:8], plane[6:7]
            down = (jnp.concatenate([-first, 16.0 * first - second], 0), jnp.concatenate([-first, 8.0 * first - second], 0))
            up = (jnp.concatenate([16.0 * last - before, -last], 0), jnp.concatenate([before - 8.0 * last, last], 0))
            return down, up

        down, up = zip(beyond(total), beyond(lifted), beyond(along), strict=True)
        mean_below = below[0] + below[1] * down[0][0] + below[2] * down[1][1] + below[3] * down[2][1]
        mean_above = above[0] + above[1] * up[0][0] + above[2] * up[1][1] + above[3] * up[2][1]
        mean, bend = (joined_sums(middle_sums_ref, outer_sums_ref, case * 2 + i, layer) for i in range(2))
        halo = jnp.concatenate([mean_above, zero[0:4], mean_below], axis=0)
        m1 = pltpu.roll(jnp.where(layer == 7, halo, mean), 1, 0)
        m2 = pltpu.roll(jnp.where(layer >= 6, halo, mean), 2, 0)
        p1 = pltpu.roll(jnp.where(layer == 0, halo, mean), 7, 0)
        p2 = pltpu.roll(jnp.where(layer < 2, halo, mean), 6, 0)
        grad += coef(FLUX) * (8.0 * (p1 - m1) - (p2 - m2)) + coef(BEND) * bend
        change = edge_sums(corr_ref[rows(case * 8), :])
        down_rows = jnp.concatenate([change[6:7] - 8.0 * change[7:8], change[7:8]], axis=0)
        up_rows = jnp.concatenate([-change[0:1], 8.0 * change[0:1] - change[1:2]], axis=0)
        missing += jnp.concatenate([above[4] * down_rows, zero[0:4], below[4] * up_rows], axis=0)
    corner = ((lane < 2) | (lane >= 126)) & ((layer < 2) | (layer >= 6))
    grad_ref[...] = grad
    inside = jnp.where(corner, 0.0, grad)
    rest = jnp.sum(inside * inside, axis=0, keepdims=True)
    corners = pltpu.roll(jnp.where(corner, grad, 0.0), 2, 1, stride=4, stride_axis=0)
    shares = pltpu.roll(jnp.where(corner, missing, 0.0), 34, 1, stride=4, stride_axis=0)
    line = jnp.sum(corners + shares, axis=0, keepdims=True)
    line = jnp.where(lanes_of((1, 128)) < 64, line, rest + pltpu.roll(rest, 64, 1))
    line_ref[...] = jnp.broadcast_to(line[None], line_ref.shape)


def rest_kernel(
    depth,
    cases,
    place_ref,
    loose_ref,
    middle_ref,
    early_ref,
    first_in_ref,
    second_in_ref,
    coef_ref,
    out_ref,
    state_ref,
    sems,
):
    planes = 4 * cases * depth
    half = planes * 4
    copies = [pltpu.make_async_copy(state_ref.at[rows(i * half, half), :], out_ref.at[rows(i * half, half), :], sems.at[i]) for i in range(2)]

    def place_tiles(c, refs):
        def one(case, _):
            for block in range(depth // 8):
                offset = pl.multiple_of((c * cases + case) * depth + 8 * block, 8)
                for row in range(8):
                    if refs[row] is not None:
                        ref, place = row_place(refs[row], row, planes)
                        state_ref[strided(offset * 8 + row), :] = ref[rows(place + offset), :]
            return 0

        lax.fori_loop(0, cases, one, 0)

    both = (middle_ref, early_ref)
    for c in range(2):
        place_tiles(c, [both] * 8)
    copies[0].start()
    for c in range(2, 4):
        place_tiles(c, [both if row in MIDDLE else None for row in range(8)])

    def store(c, case, block, offset, tiles):
        for row, tile in tiles.items():
            state_ref[strided(offset * 8 + row), :] = tile

    arrived = Post(place_ref, first_in_ref, second_in_ref)
    outer_rows(depth, cases, planes, (2, 3), loose_ref, arrived, coef_ref, store)
    copies[1].start()
    copies[0].wait()
    copies[1].wait()


def scale_kernel(cells, devices, trans, place_ref, grad_ref, sums_ref, out_ref, lines_ref, shares_ref):
    pad = -(-trans // 8) * 8
    lane, row = lanes_of((8, 128)), rows_of((8, 128))
    zero = jnp.zeros((pad, 128), jnp.float32)
    lines_ref[rows(0, pad), :] = zero
    lines_ref[rows(pad + devices, pad), :] = zero
    lines_ref[rows(pad, devices), :] = sums_ref[...]
    total = jnp.zeros((8, 128), jnp.float32)
    for block in range(devices // 8):
        here = lines_ref[rows(pad + 8 * block), :]
        below, above = lines_ref[rows(pad - trans + 8 * block), :], lines_ref[rows(pad + trans + 8 * block), :]
        share = pltpu.roll(jnp.where(lane < 48, below, above), 96, 1)
        shares_ref[rows(8 * block), :] = share
        corner = here + share
        total += jnp.where(lane < 32, corner * corner, jnp.where(lane >= 64, here, 0.0))
    total = jnp.sum(jnp.sum(total, axis=0, keepdims=True), axis=1, keepdims=True)
    own = jnp.broadcast_to(shares_ref[pl.ds(place_ref[DEVICE], 1), :], (8, 128))
    grad = grad_ref[...]
    edge = (lane < 2) | (lane >= 126)
    for i in (0, 1, 6, 7):
        grad += jnp.where((row == i) & edge, pltpu.roll(own, (126 - 4 * i) % 128, 1), 0.0)
    out_ref[...] = grad / jnp.sqrt(total / cells + 1e-06)


def f32(*shape):
    return jax.ShapeDtypeStruct(shape, jnp.float32)


def in_hbm(array):
    return pltpu.with_memory_space_constraint(array, pltpu.HBM)


def call(kernel, *args, outs, scratch=(), smem=0, hbm=0, hbm_at=None, out=VM):
    specs = [VM] * len(args)
    specs[:smem] = [SM] * smem
    at = smem if hbm_at is None else hbm_at
    specs[at : at + hbm] = [HB] * hbm
    return pl.pallas_call(
        kernel,
        out_shape=outs,
        in_specs=specs,
        out_specs=tuple([out] * len(outs)),
        scratch_shapes=[pltpu.VMEM(shape, jnp.float32) if isinstance(shape, tuple) else shape for shape in scratch],
        compiler_params=PARAMS,
    )(*args)


def neighbours(axis):
    size = lax.axis_size(axis)
    up = [(i, i + 1) for i in range(size - 1)]
    return up, [(j, i) for i, j in up]


def exchange_rows(first, second):
    size = lax.axis_size("roll")
    inner = [(i, i ^ 1) for i in range(size) if i ^ 1 < size]
    outer = [pair for i in range(1, size - 1, 2) for pair in ((i, i + 1), (i + 1, i))]
    return lax.ppermute(first, "roll", inner), lax.ppermute(second, "roll", outer)


def exchange_columns(cols):
    ahead, back = neighbours("trans")
    if lax.axis_size("trans") == 2:
        return lax.ppermute(cols, "trans", ahead + back)
    left, right = lax.ppermute(cols, "trans", ahead), lax.ppermute(cols, "trans", back)
    return jnp.where(lanes_of(cols.shape) % 4 < 2, left, right)


def on_device(adjoint, source, pressure, film, cavity, temp_index):
    components, cases, depth, width_x, width_y = adjoint.shape
    planes = components * cases * depth
    assert (components, width_x, width_y, 4 * depth) == (4, 8, 128, 128)
    state = adjoint.reshape(planes * 8, 128)
    forcing = source.reshape(planes * 8, 128)
    roll, trans, trans_size = lax.axis_index("roll"), lax.axis_index("trans"), lax.axis_size("trans")
    place = jnp.stack([trans, trans_size, roll % 2, roll * trans_size + trans]).astype(jnp.int32)
    devices = lax.axis_size("roll") * trans_size
    inner, part = f32(planes * 8, 128), f32(planes * 4 + 2 * PAD, 128)
    message, cols_shape = f32(planes * 2 + TAIL, 128), f32(components * cases * 8, 128)
    coef, packed, mask = call(
        functools.partial(coefficient_kernel, depth, cases),
        temp_index,
        place,
        pressure.reshape(cases * 8, 128),
        film,
        cavity.reshape(cases * 8, 128),
        outs=(f32(cases * N_COEF * 8, 128), f32(cases * N_PACKED * 8, 128), f32(8, 128)),
        smem=2,
    )
    state, first, second = call(
        functools.partial(send_kernel, depth, cases),
        place,
        in_hbm(state),
        outs=(inner, message, message),
        scratch=[pltpu.SemaphoreType.DMA((PIECES,))],
        smem=1,
        hbm=1,
    )
    middle, outer, cols, forcing = call(
        functools.partial(pack_kernel, depth, cases),
        state,
        in_hbm(forcing),
        outs=(part, part, cols_shape, inner),
        scratch=[pltpu.SemaphoreType.DMA],
        hbm=1,
        hbm_at=1,
    )
    for index in range(SECTIONS):
        more = index < SECTIONS - 1
        first, second = exchange_rows(first, second)
        side = exchange_columns(cols)
        whole, *total = call(
            functools.partial(inner_kernel, depth, cases),
            middle,
            outer,
            forcing,
            coef,
            outs=(inner, f32(cases * 8, 128)) if more else (inner,),
            scratch=[(planes * 8, 256)],
        )
        middle, loose, sums, corr = call(
            functools.partial(sides_kernel, depth, cases, next_moments if more else wall_sums),
            whole,
            side,
            mask,
            packed,
            outs=(part, part, f32(cases * (5 if more else 2) * 8, 128), cols_shape),
        )
        if more:
            outer, first, second, moments = call(
                functools.partial(joined_kernel, depth, cases),
                place,
                loose,
                sums,
                *total,
                first,
                second,
                coef,
                outs=(part, message, message, f32(cases * 3 * 8, 128)),
                scratch=[(cases * 5 * 8, 128)],
                smem=1,
            )
            (cols,) = call(functools.partial(columns_kernel, depth, cases), middle, outer, outs=(cols_shape,))
        else:
            early, grad, sums = call(
                functools.partial(final_kernel, depth, cases),
                place,
                loose,
                sums,
                corr,
                first,
                second,
                coef,
                moments,
                outs=(part, f32(8, 128), pltpu.VMEM((devices, 1, 128), jnp.float32)),
                scratch=[(cases * 2 * 8, 128)],
                smem=1,
            )
            (state,) = call(
                functools.partial(rest_kernel, depth, cases),
                place,
                loose,
                middle,
                early,
                first,
                second,
                coef,
                outs=(pltpu.HBM(inner.shape, jnp.float32),),
                scratch=[inner.shape, pltpu.SemaphoreType.DMA((2,))],
                smem=1,
                out=HB,
            )
    sums = lax.all_to_all(sums, ("roll", "trans"), 0, 0, tiled=True).reshape(devices, 128)
    pad = -(-trans_size // 8) * 8
    (wall_step,) = call(
        functools.partial(scale_kernel, devices * width_x * width_y, devices, trans_size),
        place,
        grad,
        sums,
        outs=(f32(8, 128),),
        scratch=[(devices + 2 * pad, 128), (devices, 128)],
        smem=1,
    )
    return (state.reshape(adjoint.shape), wall_step)


def solution(mesh):
    placed = (
        P(None, None, None, "roll", "trans"),
        P(None, None, None, "roll", "trans"),
        P(None, "roll", "trans"),
        P("roll", "trans"),
        P(None, "roll", "trans"),
        P(),
    )
    return jax.shard_map(
        on_device,
        mesh=mesh,
        in_specs=placed,
        out_specs=(P(None, None, None, "roll", "trans"), P("roll", "trans")),
        check_vma=False,
    )
```

```python
import functools

import jax
import jax.numpy as jnp
from jax import lax
from jax.experimental import pallas as pl
from jax.experimental.pallas import tpu as pltpu
from jax.sharding import PartitionSpec as P

SECTIONS = 2


VISCOSITY_PRESS = 0.3
VISCOSITY_TEMP = 0.5
THETA_STEP = 0.2
SOUND = 0.5
KAPPA = 0.6
HEATING = 0.3
ROLL_SPEED = 1.0
COURANT = 0.8

VM = pl.BlockSpec(memory_space=pltpu.VMEM)
HB = pl.BlockSpec(memory_space=pltpu.HBM)
PARAMS = pltpu.CompilerParams(vmem_limit_bytes=16 * 1024 * 1024)

PAD = 8
CENTER, SPREAD, ACROSS = (0, 3, 6)
CARRY, SOUND_STEP, STEP, HEAT, FLUX, BEND = range(9, 15)
N_COEF = 15
N_PACKED = 4
PIECES = 4
TAIL = 24
MIDDLE, OUTER = (2, 3, 4, 5), (0, 1, 6, 7)
TRANS, TRANS_SIZE, ODD, DEVICE = range(4)
WEIGHT = (0, 1, 1, 2)


def lanes_of(shape):
    return lax.broadcasted_iota(jnp.int32, shape, 1)


def rows_of(shape):
    return lax.broadcasted_iota(jnp.int32, shape, 0)


def rows(start, count=8):
    return pl.ds(start, count)


def strided(start):
    return pl.ds(start, 8, stride=8)


def coefficient_kernel(depth, cases, level_ref, place_ref, pressure_ref, film_ref, cavity_ref, coef_ref, packed_ref, mask_ref):
    lane, row = lanes_of((8, 128)), rows_of((8, 128))
    film = film_ref[...]
    for case in range(cases):
        theta = THETA_STEP * level_ref[rows(case * 8), :].astype(jnp.float32)
        viscosity = jnp.exp(VISCOSITY_PRESS * pressure_ref[rows(case * 8), :] - VISCOSITY_TEMP * theta)
        film_coef = 4.0 * viscosity / (film * film)
        density = 1.0 - 0.6 * cavity_ref[rows(case * 8), :].astype(jnp.float32)
        step = COURANT / (32.0 / 3.0 * viscosity + 4.0 * film_coef + 2.0 * SOUND + 1.0)
        planes = [None] * N_COEF
        for i, weight in enumerate((0.5, 1.0, KAPPA)):
            planes[SPREAD + i] = (weight / 12.0) * step * viscosity
            planes[ACROSS + i] = weight * step * film_coef
            planes[CENTER + i] = 1.0 - 60.0 * planes[SPREAD + i] - 2.0 * planes[ACROSS + i]
        planes[CARRY] = (ROLL_SPEED / 12.0) * step * density
        planes[SOUND_STEP] = (SOUND / 12.0) * step
        planes[STEP] = step
        planes[HEAT] = HEATING * step * viscosity
        planes[FLUX] = (ROLL_SPEED / (24.0 * depth)) * density * film
        planes[BEND] = (8.0 / depth) * viscosity / (film * film * film)
        for i, plane in enumerate(planes):
            coef_ref[rows((case * N_COEF + i) * 8), :] = plane
        wanted = jnp.concatenate(planes[SPREAD : SPREAD + 3] + [planes[SOUND_STEP]], axis=0)
        packed = exact_dot(wanted, edge_columns())
        for i in range(N_PACKED):
            packed_ref[rows((case * N_PACKED + i) * 8), :] = packed[i * 8 : i * 8 + 8]
    trans = place_ref[rows(TRANS * 8), :]
    from_left = jnp.where(trans > 0, 1.0, 0.0)
    from_right = jnp.where(trans < place_ref[rows(TRANS_SIZE * 8), :] - 1, 1.0, 0.0)
    mask_ref[...] = jnp.where(lane % 4 < 2, from_left, from_right)


def edge_columns():
    source = lanes_of((128, 128)) % 4
    source = jnp.where(source < 2, 126 + source, source - 2)
    return jnp.where(rows_of((128, 128)) == source, 1.0, 0.0).astype(jnp.bfloat16)


def in_parts(value):
    high = value.astype(jnp.bfloat16)
    rest = value - high.astype(jnp.float32)
    middle = rest.astype(jnp.bfloat16)
    return jnp.concatenate([high, middle], axis=1), (rest - middle.astype(jnp.float32)).astype(jnp.bfloat16)


def exact_dot(value, weights):
    upper, low = in_parts(value)
    part = jnp.dot(upper, jnp.concatenate([weights, weights], axis=0), preferred_element_type=jnp.float32)
    return part + jnp.dot(low, weights, preferred_element_type=jnp.float32)


class Post:
    def __init__(self, place_ref, first_ref, second_ref):
        self.odd = place_ref[rows(ODD * 8), :] == 1
        self.refs = first_ref, second_ref

    def put(self, where, up, down):
        first, second = self.refs
        odd = self.odd[: where.size]
        first[where, :] = jnp.where(odd, down, up)
        second[where, :] = jnp.where(odd, up, down)

    def get(self, where):
        first, second = (ref[where, :] for ref in self.refs)
        odd = self.odd[: where.size]
        return jnp.where(odd, first, second), jnp.where(odd, second, first)

    def put_tiles(self, planes, first, tiles):
        for i in range(2):
            self.put(rows(i * planes + first), tiles[6 + i], tiles[i])


def row_place(refs, row, planes):
    if row in MIDDLE:
        return refs[0], PAD + MIDDLE.index(row) * planes
    return refs[1], PAD + OUTER.index(row) * planes


def send_kernel(depth, cases, place_ref, state_ref, copy_ref, first_ref, second_ref, sems):
    planes = 4 * cases * depth
    post = Post(place_ref, first_ref, second_ref)

    def piece(i):
        here = rows(i * (planes * 8 // PIECES), planes * 8 // PIECES)
        return pltpu.make_async_copy(state_ref.at[here, :], copy_ref.at[here, :], sems.at[i])

    for i in range(PIECES):
        piece(i).start()
    for i in range(PIECES):
        piece(i).wait()
        for first in range(i * planes // PIECES, (i + 1) * planes // PIECES, 8):
            post.put_tiles(planes, first, {row: copy_ref[strided(first * 8 + row), :] for row in (0, 1, 6, 7)})


def pack_kernel(depth, cases, state_ref, source_ref, middle_ref, outer_ref, cols_ref, copy_ref, sem):
    planes = 4 * cases * depth
    lane = lanes_of((8, 128))
    copy = pltpu.make_async_copy(source_ref, copy_ref, sem)
    copy.start()

    def one(pair, _):
        held = jnp.zeros((8, 128), jnp.float32)
        for layer in range(depth):
            group = depth - 1 - layer
            plane = state_ref[rows(pl.multiple_of((pair * depth + layer) * 8, 8)), :]
            held = jnp.where(lane // 4 == group, pltpu.roll(plane, (4 * group + 2) % 128, 1), held)
        cols_ref[rows(pl.multiple_of(pair * 8, 8)), :] = held
        for row in range(8):
            for block in range(depth // 8):
                first = pl.multiple_of(pair * depth + 8 * block, 8)
                ref, place = row_place((middle_ref, outer_ref), row, planes)
                ref[rows(place + first), :] = state_ref[strided(first * 8 + row), :]
        return 0

    lax.fori_loop(0, 4 * cases, one, 0)
    copy.wait()


def columns_kernel(depth, cases, middle_ref, outer_ref, cols_ref):
    planes = 4 * cases * depth
    columns = edge_columns()
    mine = lanes_of((depth, 128)) // 4 == (depth - 1) - rows_of((depth, 128))
    for row in range(8):
        ref, place = row_place((middle_ref, outer_ref), row, planes)
        edges = exact_dot(ref[rows(place, planes), :], columns)
        for pair in range(4 * cases):
            kept = jnp.where(mine, edges[pair * depth : (pair + 1) * depth], 0.0)
            cols_ref[pl.ds(pair * 8 + row, 1), :] = jnp.sum(kept, axis=0, keepdims=True)


def inner_kernel(depth, cases, middle_ref, outer_ref, source_ref, coef_ref, *rest):
    out_ref, *more_refs, deriv_ref = rest
    planes = 4 * cases * depth
    lane, layer = lanes_of((8, 128)), rows_of((8, 128))
    gap = rows_of((128, 256)) - lanes_of((128, 256)) % 128
    second = jnp.where(jnp.abs(gap) == 1, 16.0, jnp.where(jnp.abs(gap) == 2, -1.0, 0.0))
    first = jnp.where(gap == 1, 8.0, jnp.where(gap == -1, -8.0, jnp.where(gap == 2, -1.0, jnp.where(gap == -2, 1.0, 0.0))))
    weights = jnp.where(lanes_of((128, 256)) < 128, second, first).astype(jnp.bfloat16)
    for row in range(8):
        ref, place = row_place((middle_ref, outer_ref), row, planes)
        value = ref[rows(place, planes), :]
        deriv_ref[rows(row * planes, planes), :] = exact_dot(value, weights)

    def one(index, _):
        case, block = index // (depth // 8), index % (depth // 8)
        k = layer + 8 * block
        height = (k.astype(jnp.float32) + 0.5) / depth
        offsets = [pl.multiple_of((c * cases + case) * depth + 8 * block, 8) for c in range(4)]
        places = [row_place((middle_ref, outer_ref), row, planes) for row in range(8)]
        tiles = [[ref[rows(place + offsets[c]), :] for ref, place in places] for c in range(4)]

        for row in range(8):

            def coef(i):
                return coef_ref[pl.ds((case * N_COEF + i) * 8 + row, 1), :]

            along = []
            for c in range(4):
                near = [tiles[c][row + by] if 0 <= row + by < 8 else None for by in (-2, -1, 1, 2)]
                along.append(near)

            def first_x(c):
                m2, m1, p1, p2 = along[c]
                ones = 8.0 * (p1 - m1) if m1 is not None and p1 is not None else 8.0 * p1 if m1 is None else -8.0 * m1
                if m2 is not None and p2 is not None:
                    return ones - (p2 - m2)
                return ones - p2 if m2 is None else ones + m2

            def second_x(c):
                m2, m1, p1, p2 = along[c]
                ones = 16.0 * (p1 + m1) if m1 is not None and p1 is not None else 16.0 * (p1 if m1 is None else m1)
                if m2 is not None and p2 is not None:
                    return ones - (p2 + m2)
                return ones - (p2 if m2 is None else m2)

            carry = coef(CARRY) * height
            sound = coef(SOUND_STEP)
            step = coef(STEP)
            slopes = [first_x(c) for c in range(4)]
            for c in range(4):
                here = row * planes + offsets[c]
                ref, place = places[row]
                behind = jnp.where(k > 0, ref[rows(place + offsets[c] - 1), :], 0.0)
                beyond = jnp.where(k < depth - 1, ref[rows(place + offsets[c] + 1), :], 0.0)
                source = source_ref[strided(offsets[c] * 8 + row), :]
                w = WEIGHT[c]
                value = coef(CENTER + w) * tiles[c][row] + coef(SPREAD + w) * (second_x(c) + deriv_ref[rows(here), 0:128])
                value += coef(ACROSS + w) * (behind + beyond) + step * source + carry * slopes[c]
                if c == 0:
                    other = row * planes + offsets[2]
                    value += sound * (slopes[1] + deriv_ref[rows(other), 128:256])
                elif c == 1:
                    value += sound * slopes[0]
                elif c == 2:
                    other = row * planes + offsets[0]
                    value += sound * deriv_ref[rows(other), 128:256]
                else:
                    value += coef(HEAT) * tiles[1][row]
                out_ref[rows(here), :] = value
        return 0

    lax.fori_loop(0, cases * (depth // 8), one, 0)

    if more_refs:
        (total_ref,) = more_refs
        for case in range(cases):
            for row in range(8):
                total = jnp.zeros((8, 128), jnp.float32)
                for block in range(depth // 8):
                    total += source_ref[strided((case * depth + 8 * block) * 8 + row), :]
                total_ref[pl.ds(case * 8 + row, 1), :] = jnp.sum(total, axis=0, keepdims=True)


def columns_beyond(cases, side_ref, mask_ref, packed_ref, corr_ref):
    slot = lanes_of((8, 128)) % 4
    for case in range(cases):
        coefs = [packed_ref[rows((case * N_PACKED + i) * 8), :] for i in range(N_PACKED)]
        second, first = [], []
        for c in range(4):
            side = side_ref[rows((c * cases + case) * 8), :] * mask_ref[...]
            p1 = jnp.where(slot == 1, pltpu.roll(side, 127, 1), 0.0)
            p2 = jnp.where(slot < 2, pltpu.roll(side, 126, 1), 0.0)
            m1 = jnp.where(slot == 2, pltpu.roll(side, 1, 1), 0.0)
            m2 = jnp.where(slot >= 2, pltpu.roll(side, 2, 1), 0.0)
            second.append(16.0 * (p1 + m1) - (p2 + m2))
            first.append(8.0 * (p1 - m1) - (p2 - m2))
        for c in range(4):
            value = coefs[WEIGHT[c]] * second[c]
            if c == 0:
                value += coefs[3] * first[2]
            elif c == 2:
                value += coefs[3] * first[0]
            corr_ref[rows((c * cases + case) * 8), :] = value


def depth_sum(tiles):
    total = tiles[0]
    for tile in tiles[1:]:
        total = total + tile
    return jnp.sum(total, axis=0, keepdims=True)


def next_moments(depth, tiles_of, layer):
    density = tiles_of(0)
    heights = [(layer + (8 * block + 0.5)).astype(jnp.float32) / depth for block in range(depth // 8)]
    return (
        depth_sum(density),
        depth_sum([tile * height for tile, height in zip(density, heights, strict=True)]),
        depth_sum(tiles_of(1)),
        depth_sum(tiles_of(2)),
        density[0][0:1] + density[-1][7:8],
    )


def wall_sums(depth, tiles_of, layer):
    momentum, before = tiles_of(1), tiles_of(1, -1)
    changes = [momentum[0] - jnp.where(layer > 0, before[0], 0.0)]
    changes += [here - there for here, there in zip(momentum[1:], before[1:], strict=True)]
    squares = [change * change for change in changes] + [jnp.where(layer == 7, momentum[-1] * momentum[-1], 0.0)]
    return depth_sum(tiles_of(0)), depth_sum(squares)


def line_sums(depth, cases, planes, sums, ref, which, out_ref, layer):
    for case in range(cases):
        for i, row in enumerate(which):

            def tiles_of(c, by=0):
                start = PAD + i * planes + (c * cases + case) * depth
                return [ref[rows(start + by + 8 * block), :] for block in range(depth // 8)]

            lines = sums(depth, tiles_of, layer)
            for n, line in enumerate(lines):
                out_ref[pl.ds((case * len(lines) + n) * 8 + row, 1), :] = line


def joined_sums(middle_ref, outer_ref, index, layer):
    return jnp.where((layer >= 2) & (layer < 6), middle_ref[rows(index * 8), :], outer_ref[rows(index * 8), :])


def sides_kernel(depth, cases, sums, inner_ref, side_ref, mask_ref, packed_ref, middle_ref, loose_ref, sums_ref, corr_ref):
    planes = 4 * cases * depth
    lane, layer = lanes_of((8, 128)), rows_of((8, 128))
    edge = (lane < 2) | (lane >= 126)
    columns_beyond(cases, side_ref, mask_ref, packed_ref, corr_ref)

    def one(case, _):
        for row in range(8):
            for c in range(4):
                line = jnp.broadcast_to(corr_ref[pl.ds((c * cases + case) * 8 + row, 1), :], (8, 128))
                for block in range(depth // 8):
                    offset = pl.multiple_of((c * cases + case) * depth + 8 * block, 8)
                    moved = pltpu.roll(line, 2 + 32 * block, 1, stride=4, stride_axis=0)
                    value = inner_ref[rows(row * planes + offset), :] + jnp.where(edge, moved, 0.0)
                    ref, place = row_place((middle_ref, loose_ref), row, planes)
                    ref[rows(place + offset), :] = value
        return 0

    lax.fori_loop(0, cases, one, 0)
    line_sums(depth, cases, planes, sums, middle_ref, MIDDLE, sums_ref, layer)


def outer_rows(depth, cases, planes, parts, loose_ref, post, coef_ref, store):
    layer = rows_of((8, 128))

    def one(case, _):
        for block in range(depth // 8):
            height = ((layer + 8 * block).astype(jnp.float32) + 0.5) / depth
            offsets = [pl.multiple_of((c * cases + case) * depth + 8 * block, 8) for c in range(4)]
            near = {c: [post.get(rows(i * planes + offsets[c])) for i in range(2)] for c in {*parts, *range(2)}}
            whole = {c: {} for c in parts}
            for i, row in enumerate(OUTER):

                def coef(n):
                    return coef_ref[pl.ds((case * N_COEF + n) * 8 + row, 1), :]

                second, first = {}, {}
                for c, ((m2, p1), (m1, p2)) in near.items():
                    if row == 0:
                        second[c], first[c] = 16.0 * m1 - m2, m2 - 8.0 * m1
                    elif row == 1:
                        second[c], first[c] = -m1, m1
                    elif row == 6:
                        second[c], first[c] = -p1, -p1
                    else:
                        second[c], first[c] = 16.0 * p1 - p2, 8.0 * p1 - p2
                for c in parts:
                    value = loose_ref[rows(PAD + i * planes + offsets[c]), :]
                    value += coef(SPREAD + WEIGHT[c]) * second[c] + coef(CARRY) * height * first[c]
                    if c < 2:
                        value += coef(SOUND_STEP) * first[1 - c]
                    whole[c][row] = value
            for c in parts:
                store(c, case, block, offsets[c], whole[c])
        return 0

    lax.fori_loop(0, cases, one, 0)


def joined_kernel(
    depth,
    cases,
    place_ref,
    loose_ref,
    middle_sums_ref,
    source_total_ref,
    first_in_ref,
    second_in_ref,
    coef_ref,
    outer_ref,
    first_ref,
    second_ref,
    moment_ref,
    outer_sums_ref,
):
    planes = 4 * cases * depth
    lane, layer = lanes_of((8, 128)), rows_of((8, 128))
    post, arrived = Post(place_ref, first_ref, second_ref), Post(place_ref, first_in_ref, second_in_ref)

    def store(c, case, block, offset, tiles):
        for i, row in enumerate(OUTER):
            outer_ref[rows(PAD + i * planes + offset), :] = tiles[row]
        post.put_tiles(planes, offset, tiles)

    outer_rows(depth, cases, planes, range(4), loose_ref, arrived, coef_ref, store)

    line_sums(depth, cases, planes, next_moments, outer_ref, OUTER, outer_sums_ref, layer)
    for case in range(cases):

        def coef(i):
            return coef_ref[rows((case * N_COEF + i) * 8), :]

        moments = [joined_sums(middle_sums_ref, outer_sums_ref, case * 5 + i, layer) for i in range(5)]
        total, lifted, along, across, walls = moments
        for i in range(3):
            moment_ref[rows((case * 3 + i) * 8), :] = moments[i]

        def x_parts(plane):
            m1, m2 = jnp.where(layer >= 1, pltpu.roll(plane, 1, 0), 0.0), jnp.where(layer >= 2, pltpu.roll(plane, 2, 0), 0.0)
            p1, p2 = jnp.where(layer < 7, pltpu.roll(plane, 7, 0), 0.0), jnp.where(layer < 6, pltpu.roll(plane, 6, 0), 0.0)
            return 16.0 * (p1 + m1) - (p2 + m2), 8.0 * (p1 - m1) - (p2 - m2)

        def y_parts(plane):
            m1, m2 = jnp.where(lane >= 1, pltpu.roll(plane, 1, 1), 0.0), jnp.where(lane >= 2, pltpu.roll(plane, 2, 1), 0.0)
            p1, p2 = jnp.where(lane < 127, pltpu.roll(plane, 127, 1), 0.0), jnp.where(lane < 126, pltpu.roll(plane, 126, 1), 0.0)
            return 16.0 * (p1 + m1) - (p2 + m2), 8.0 * (p1 - m1) - (p2 - m2)

        value = coef(CENTER) * total + coef(SPREAD) * (x_parts(total)[0] + y_parts(total)[0])
        value += coef(ACROSS) * (2.0 * total - walls) + coef(CARRY) * x_parts(lifted)[1]
        value += coef(SOUND_STEP) * (x_parts(along)[1] + y_parts(across)[1]) + coef(STEP) * source_total_ref[rows(case * 8), :]
        sent = (value, coef(SPREAD), coef(CARRY), coef(SOUND_STEP), coef(FLUX))
        for i, plane in enumerate(sent):
            post.put(pl.ds(2 * planes + (case * 5 + i) * 2, 2), plane[6:8], plane[0:2])


def edge_sums(tile):
    for by in (4, 8, 16, 32, 64):
        tile = tile + pltpu.roll(tile, by, 1)
    return pltpu.roll(tile, 2, 1)


def final_kernel(
    depth,
    cases,
    place_ref,
    loose_ref,
    middle_sums_ref,
    corr_ref,
    first_in_ref,
    second_in_ref,
    coef_ref,
    moment_ref,
    outer_ref,
    grad_ref,
    line_ref,
    outer_sums_ref,
):
    planes = 4 * cases * depth
    lane, layer = lanes_of((8, 128)), rows_of((8, 128))
    arrived = Post(place_ref, first_in_ref, second_in_ref)

    def store(c, case, block, offset, tiles):
        for i, row in enumerate(OUTER):
            outer_ref[rows(PAD + i * planes + offset), :] = tiles[row]

    outer_rows(depth, cases, planes, range(2), loose_ref, arrived, coef_ref, store)
    line_sums(depth, cases, planes, wall_sums, outer_ref, OUTER, outer_sums_ref, layer)

    zero = jnp.zeros((8, 128), jnp.float32)
    grad, missing = zero, zero
    for case in range(cases):

        def coef(i):
            return coef_ref[rows((case * N_COEF + i) * 8), :]

        pairs = [arrived.get(pl.ds(2 * planes + (case * 5 + i) * 2, 2)) for i in range(5)]
        below, above = [pair[0] for pair in pairs], [pair[1] for pair in pairs]
        total, lifted, along = (moment_ref[rows((case * 3 + i) * 8), :] for i in range(3))

        def beyond(plane):
            first, second, last, before = plane[0:1], plane[1:2], plane[7:8], plane[6:7]
            down = (jnp.concatenate([-first, 16.0 * first - second], 0), jnp.concatenate([-first, 8.0 * first - second], 0))
            up = (jnp.concatenate([16.0 * last - before, -last], 0), jnp.concatenate([before - 8.0 * last, last], 0))
            return down, up

        down, up = zip(beyond(total), beyond(lifted), beyond(along), strict=True)
        mean_below = below[0] + below[1] * down[0][0] + below[2] * down[1][1] + below[3] * down[2][1]
        mean_above = above[0] + above[1] * up[0][0] + above[2] * up[1][1] + above[3] * up[2][1]
        mean, bend = (joined_sums(middle_sums_ref, outer_sums_ref, case * 2 + i, layer) for i in range(2))
        halo = jnp.concatenate([mean_above, zero[0:4], mean_below], axis=0)
        m1 = pltpu.roll(jnp.where(layer == 7, halo, mean), 1, 0)
        m2 = pltpu.roll(jnp.where(layer >= 6, halo, mean), 2, 0)
        p1 = pltpu.roll(jnp.where(layer == 0, halo, mean), 7, 0)
        p2 = pltpu.roll(jnp.where(layer < 2, halo, mean), 6, 0)
        grad += coef(FLUX) * (8.0 * (p1 - m1) - (p2 - m2)) + coef(BEND) * bend
        change = edge_sums(corr_ref[rows(case * 8), :])
        down_rows = jnp.concatenate([change[6:7] - 8.0 * change[7:8], change[7:8]], axis=0)
        up_rows = jnp.concatenate([-change[0:1], 8.0 * change[0:1] - change[1:2]], axis=0)
        missing += jnp.concatenate([above[4] * down_rows, zero[0:4], below[4] * up_rows], axis=0)
    corner = ((lane < 2) | (lane >= 126)) & ((layer < 2) | (layer >= 6))
    grad_ref[...] = grad
    inside = jnp.where(corner, 0.0, grad)
    rest = jnp.sum(inside * inside, axis=0, keepdims=True)
    corners = pltpu.roll(jnp.where(corner, grad, 0.0), 2, 1, stride=4, stride_axis=0)
    shares = pltpu.roll(jnp.where(corner, missing, 0.0), 34, 1, stride=4, stride_axis=0)
    line = jnp.sum(corners + shares, axis=0, keepdims=True)
    line = jnp.where(lanes_of((1, 128)) < 64, line, rest + pltpu.roll(rest, 64, 1))
    line_ref[...] = jnp.broadcast_to(line[None], line_ref.shape)


def rest_kernel(
    depth,
    cases,
    place_ref,
    loose_ref,
    middle_ref,
    early_ref,
    first_in_ref,
    second_in_ref,
    coef_ref,
    out_ref,
    state_ref,
    sems,
):
    planes = 4 * cases * depth
    half = planes * 4
    copies = [pltpu.make_async_copy(state_ref.at[rows(i * half, half), :], out_ref.at[rows(i * half, half), :], sems.at[i]) for i in range(2)]

    def place_tiles(c, refs):
        def one(case, _):
            for block in range(depth // 8):
                offset = pl.multiple_of((c * cases + case) * depth + 8 * block, 8)
                for row in range(8):
                    if refs[row] is not None:
                        ref, place = row_place(refs[row], row, planes)
                        state_ref[strided(offset * 8 + row), :] = ref[rows(place + offset), :]
            return 0

        lax.fori_loop(0, cases, one, 0)

    both = (middle_ref, early_ref)
    for c in range(2):
        place_tiles(c, [both] * 8)
    copies[0].start()
    for c in range(2, 4):
        place_tiles(c, [both if row in MIDDLE else None for row in range(8)])

    def store(c, case, block, offset, tiles):
        for row, tile in tiles.items():
            state_ref[strided(offset * 8 + row), :] = tile

    arrived = Post(place_ref, first_in_ref, second_in_ref)
    outer_rows(depth, cases, planes, (2, 3), loose_ref, arrived, coef_ref, store)
    copies[1].start()
    copies[0].wait()
    copies[1].wait()


def scale_kernel(cells, devices, trans, place_ref, grad_ref, sums_ref, out_ref, lines_ref):
    pad = -(-trans // 8) * 8
    lane, row = lanes_of((8, 128)), rows_of((8, 128))
    zero = jnp.zeros((pad, 128), jnp.float32)
    lines_ref[rows(0, pad), :] = zero
    lines_ref[rows(pad + devices, pad), :] = zero
    lines_ref[rows(pad, devices), :] = sums_ref[...]
    total, own = jnp.zeros((8, 128), jnp.float32), jnp.zeros((8, 128), jnp.float32)
    device = place_ref[rows(DEVICE * 8), :]
    for block in range(devices // 8):
        here = lines_ref[rows(pad + 8 * block), :]
        below, above = lines_ref[rows(pad - trans + 8 * block), :], lines_ref[rows(pad + trans + 8 * block), :]
        share = pltpu.roll(jnp.where(lane < 48, below, above), 96, 1)
        own += jnp.where(row + 8 * block == device, share, 0.0)
        corner = here + share
        total += jnp.where(lane < 32, corner * corner, jnp.where(lane >= 64, here, 0.0))
    total = jnp.sum(jnp.sum(total, axis=0, keepdims=True), axis=1, keepdims=True)
    own = jnp.broadcast_to(jnp.sum(own, axis=0, keepdims=True), (8, 128))
    grad = grad_ref[...]
    edge = (lane < 2) | (lane >= 126)
    for i in (0, 1, 6, 7):
        grad += jnp.where((row == i) & edge, pltpu.roll(own, (126 - 4 * i) % 128, 1), 0.0)
    out_ref[...] = grad / jnp.sqrt(total / cells + 1e-06)


def f32(*shape):
    return jax.ShapeDtypeStruct(shape, jnp.float32)


def over_tiles(numbers):
    which = rows_of((8 * len(numbers), 128)) // 8
    held = jnp.full(which.shape, numbers[0], jnp.int32)
    for i, number in enumerate(numbers[1:], 1):
        held = jnp.where(which == i, number, held)
    return held


def in_hbm(array):
    return pltpu.with_memory_space_constraint(array, pltpu.HBM)


def call(kernel, *args, outs, scratch=(), hbm=None, out=VM):
    specs = [VM] * len(args)
    if hbm is not None:
        specs[hbm] = HB
    return pl.pallas_call(
        kernel,
        out_shape=outs,
        in_specs=specs,
        out_specs=tuple([out] * len(outs)),
        scratch_shapes=[pltpu.VMEM(shape, jnp.float32) if isinstance(shape, tuple) else shape for shape in scratch],
        compiler_params=PARAMS,
    )(*args)


def neighbours(axis):
    size = lax.axis_size(axis)
    up = [(i, i + 1) for i in range(size - 1)]
    return up, [(j, i) for i, j in up]


def exchange_rows(first, second):
    size = lax.axis_size("roll")
    inner = [(i, i ^ 1) for i in range(size) if i ^ 1 < size]
    outer = [pair for i in range(1, size - 1, 2) for pair in ((i, i + 1), (i + 1, i))]
    return lax.ppermute(first, "roll", inner), lax.ppermute(second, "roll", outer)


def exchange_columns(cols):
    ahead, back = neighbours("trans")
    if lax.axis_size("trans") == 2:
        return lax.ppermute(cols, "trans", ahead + back)
    left, right = lax.ppermute(cols, "trans", ahead), lax.ppermute(cols, "trans", back)
    return jnp.where(lanes_of(cols.shape) % 4 < 2, left, right)


def on_device(adjoint, source, pressure, film, cavity, temp_index):
    components, cases, depth, width_x, width_y = adjoint.shape
    planes = components * cases * depth
    assert (components, width_x, width_y, 4 * depth) == (4, 8, 128, 128)
    state = adjoint.reshape(planes * 8, 128)
    forcing = source.reshape(planes * 8, 128)
    roll, trans, trans_size = lax.axis_index("roll"), lax.axis_index("trans"), lax.axis_size("trans")
    place = over_tiles([trans, trans_size, roll % 2, roll * trans_size + trans])
    level = jnp.broadcast_to(temp_index[:, None, None], (cases, 8, 128)).reshape(cases * 8, 128)
    devices = lax.axis_size("roll") * trans_size
    inner, part = f32(planes * 8, 128), f32(planes * 4 + 2 * PAD, 128)
    message, cols_shape = f32(planes * 2 + TAIL, 128), f32(components * cases * 8, 128)
    coef, packed, mask = call(
        functools.partial(coefficient_kernel, depth, cases),
        level,
        place,
        pressure.reshape(cases * 8, 128),
        film,
        cavity.reshape(cases * 8, 128),
        outs=(f32(cases * N_COEF * 8, 128), f32(cases * N_PACKED * 8, 128), f32(8, 128)),
    )
    state, first, second = call(
        functools.partial(send_kernel, depth, cases),
        place,
        in_hbm(state),
        outs=(inner, message, message),
        scratch=[pltpu.SemaphoreType.DMA((PIECES,))],
        hbm=1,
    )
    middle, outer, cols, forcing = call(
        functools.partial(pack_kernel, depth, cases),
        state,
        in_hbm(forcing),
        outs=(part, part, cols_shape, inner),
        scratch=[pltpu.SemaphoreType.DMA],
        hbm=1,
    )
    for index in range(SECTIONS):
        more = index < SECTIONS - 1
        first, second = exchange_rows(first, second)
        side = exchange_columns(cols)
        whole, *total = call(
            functools.partial(inner_kernel, depth, cases),
            middle,
            outer,
            forcing,
            coef,
            outs=(inner, f32(cases * 8, 128)) if more else (inner,),
            scratch=[(planes * 8, 256)],
        )
        middle, loose, sums, corr = call(
            functools.partial(sides_kernel, depth, cases, next_moments if more else wall_sums),
            whole,
            side,
            mask,
            packed,
            outs=(part, part, f32(cases * (5 if more else 2) * 8, 128), cols_shape),
        )
        if more:
            outer, first, second, moments = call(
                functools.partial(joined_kernel, depth, cases),
                place,
                loose,
                sums,
                *total,
                first,
                second,
                coef,
                outs=(part, message, message, f32(cases * 3 * 8, 128)),
                scratch=[(cases * 5 * 8, 128)],
            )
            (cols,) = call(functools.partial(columns_kernel, depth, cases), middle, outer, outs=(cols_shape,))
        else:
            early, grad, sums = call(
                functools.partial(final_kernel, depth, cases),
                place,
                loose,
                sums,
                corr,
                first,
                second,
                coef,
                moments,
                outs=(part, f32(8, 128), pltpu.VMEM((devices, 1, 128), jnp.float32)),
                scratch=[(cases * 2 * 8, 128)],
            )
            (state,) = call(
                functools.partial(rest_kernel, depth, cases),
                place,
                loose,
                middle,
                early,
                first,
                second,
                coef,
                outs=(pltpu.HBM(inner.shape, jnp.float32),),
                scratch=[inner.shape, pltpu.SemaphoreType.DMA((2,))],
                out=HB,
            )
    sums = lax.all_to_all(sums, ("roll", "trans"), 0, 0, tiled=True).reshape(devices, 128)
    pad = -(-trans_size // 8) * 8
    (wall_step,) = call(
        functools.partial(scale_kernel, devices * width_x * width_y, devices, trans_size),
        place,
        grad,
        sums,
        outs=(f32(8, 128),),
        scratch=[(devices + 2 * pad, 128)],
    )
    return (state.reshape(adjoint.shape), wall_step)


def solution(mesh):
    placed = (
        P(None, None, None, "roll", "trans"),
        P(None, None, None, "roll", "trans"),
        P(None, "roll", "trans"),
        P("roll", "trans"),
        P(None, "roll", "trans"),
        P(),
    )
    return jax.shard_map(
        on_device,
        mesh=mesh,
        in_specs=placed,
        out_specs=(P(None, None, None, "roll", "trans"), P("roll", "trans")),
        check_vma=False,
    )
```

```python
import functools

import jax
import jax.numpy as jnp
from jax import lax
from jax.experimental import pallas as pl
from jax.experimental.pallas import tpu as pltpu
from jax.sharding import PartitionSpec as P

SECTIONS = 2


VISCOSITY_PRESS = 0.3
VISCOSITY_TEMP = 0.5
THETA_STEP = 0.2
SOUND = 0.5
KAPPA = 0.6
HEATING = 0.3
ROLL_SPEED = 1.0
COURANT = 0.8

VM = pl.BlockSpec(memory_space=pltpu.VMEM)
HB = pl.BlockSpec(memory_space=pltpu.HBM)
PARAMS = pltpu.CompilerParams(vmem_limit_bytes=16 * 1024 * 1024)

PAD = 8
CENTER, SPREAD, ACROSS = (0, 3, 6)
CARRY, SOUND_STEP, STEP, HEAT, FLUX, BEND = range(9, 15)
N_COEF = 15
N_PACKED = 4
PIECES = 4
TAIL = 24
MIDDLE, OUTER = (2, 3, 4, 5), (0, 1, 6, 7)
TRANS, TRANS_SIZE, ODD, DEVICE = range(4)
WEIGHT = (0, 1, 1, 2)


def lanes_of(shape):
    return lax.broadcasted_iota(jnp.int32, shape, 1)


def rows_of(shape):
    return lax.broadcasted_iota(jnp.int32, shape, 0)


def rows(start, count=8):
    return pl.ds(start, count)


def strided(start):
    return pl.ds(start, 8, stride=8)


def coefficient_kernel(depth, cases, level_ref, place_ref, pressure_ref, film_ref, cavity_ref, coef_ref, packed_ref, mask_ref):
    lane, row = lanes_of((8, 128)), rows_of((8, 128))
    film = film_ref[...]
    for case in range(cases):
        theta = THETA_STEP * level_ref[rows(case * 8), :].astype(jnp.float32)
        viscosity = jnp.exp(VISCOSITY_PRESS * pressure_ref[rows(case * 8), :] - VISCOSITY_TEMP * theta)
        film_coef = 4.0 * viscosity / (film * film)
        density = 1.0 - 0.6 * cavity_ref[rows(case * 8), :].astype(jnp.float32)
        step = COURANT / (32.0 / 3.0 * viscosity + 4.0 * film_coef + 2.0 * SOUND + 1.0)
        planes = [None] * N_COEF
        for i, weight in enumerate((0.5, 1.0, KAPPA)):
            planes[SPREAD + i] = (weight / 12.0) * step * viscosity
            planes[ACROSS + i] = weight * step * film_coef
            planes[CENTER + i] = 1.0 - 60.0 * planes[SPREAD + i] - 2.0 * planes[ACROSS + i]
        planes[CARRY] = (ROLL_SPEED / 12.0) * step * density
        planes[SOUND_STEP] = (SOUND / 12.0) * step
        planes[STEP] = step
        planes[HEAT] = HEATING * step * viscosity
        planes[FLUX] = (ROLL_SPEED / (24.0 * depth)) * density * film
        planes[BEND] = (8.0 / depth) * viscosity / (film * film * film)
        for i, plane in enumerate(planes):
            coef_ref[rows((case * N_COEF + i) * 8), :] = plane
        wanted = jnp.concatenate(planes[SPREAD : SPREAD + 3] + [planes[SOUND_STEP]], axis=0)
        packed = exact_dot(wanted, edge_columns())
        for i in range(N_PACKED):
            packed_ref[rows((case * N_PACKED + i) * 8), :] = packed[i * 8 : i * 8 + 8]
    trans = place_ref[rows(TRANS * 8), :]
    from_left = jnp.where(trans > 0, 1.0, 0.0)
    from_right = jnp.where(trans < place_ref[rows(TRANS_SIZE * 8), :] - 1, 1.0, 0.0)
    mask_ref[...] = jnp.where(lane % 4 < 2, from_left, from_right)


def edge_columns():
    source = lanes_of((128, 128)) % 4
    source = jnp.where(source < 2, 126 + source, source - 2)
    return jnp.where(rows_of((128, 128)) == source, 1.0, 0.0).astype(jnp.bfloat16)


def in_parts(value):
    high = value.astype(jnp.bfloat16)
    rest = value - high.astype(jnp.float32)
    middle = rest.astype(jnp.bfloat16)
    return jnp.concatenate([high, middle], axis=1), (rest - middle.astype(jnp.float32)).astype(jnp.bfloat16)


def exact_dot(value, weights):
    upper, low = in_parts(value)
    part = jnp.dot(upper, jnp.concatenate([weights, weights], axis=0), preferred_element_type=jnp.float32)
    return part + jnp.dot(low, weights, preferred_element_type=jnp.float32)


class Post:
    def __init__(self, place_ref, first_ref, second_ref):
        self.odd = place_ref[rows(ODD * 8), :] == 1
        self.refs = first_ref, second_ref

    def put(self, where, up, down):
        first, second = self.refs
        odd = self.odd[: where.size]
        first[where, :] = jnp.where(odd, down, up)
        second[where, :] = jnp.where(odd, up, down)

    def get(self, where):
        first, second = (ref[where, :] for ref in self.refs)
        odd = self.odd[: where.size]
        return jnp.where(odd, first, second), jnp.where(odd, second, first)

    def put_tiles(self, planes, first, tiles):
        for i in range(2):
            self.put(rows(i * planes + first), tiles[6 + i], tiles[i])


def row_place(refs, row, planes):
    if row in MIDDLE:
        return refs[0], PAD + MIDDLE.index(row) * planes
    return refs[1], PAD + OUTER.index(row) * planes


def send_kernel(depth, cases, place_ref, state_ref, copy_ref, first_ref, second_ref, sems):
    planes = 4 * cases * depth
    post = Post(place_ref, first_ref, second_ref)

    def piece(i):
        here = rows(i * (planes * 8 // PIECES), planes * 8 // PIECES)
        return pltpu.make_async_copy(state_ref.at[here, :], copy_ref.at[here, :], sems.at[i])

    for i in range(PIECES):
        piece(i).start()
    for i in range(PIECES):
        piece(i).wait()
        for first in range(i * planes // PIECES, (i + 1) * planes // PIECES, 8):
            post.put_tiles(planes, first, {row: copy_ref[strided(first * 8 + row), :] for row in (0, 1, 6, 7)})


def pack_kernel(depth, cases, state_ref, source_ref, middle_ref, outer_ref, cols_ref, copy_ref, sem):
    planes = 4 * cases * depth
    lane = lanes_of((8, 128))
    copy = pltpu.make_async_copy(source_ref, copy_ref, sem)
    copy.start()

    def one(pair, _):
        held = jnp.zeros((8, 128), jnp.float32)
        for layer in range(depth):
            group = depth - 1 - layer
            plane = state_ref[rows(pl.multiple_of((pair * depth + layer) * 8, 8)), :]
            held = jnp.where(lane // 4 == group, pltpu.roll(plane, (4 * group + 2) % 128, 1), held)
        cols_ref[rows(pl.multiple_of(pair * 8, 8)), :] = held
        for row in range(8):
            for block in range(depth // 8):
                first = pl.multiple_of(pair * depth + 8 * block, 8)
                ref, place = row_place((middle_ref, outer_ref), row, planes)
                ref[rows(place + first), :] = state_ref[strided(first * 8 + row), :]
        return 0

    lax.fori_loop(0, 4 * cases, one, 0)
    copy.wait()


def columns_kernel(depth, cases, middle_ref, outer_ref, cols_ref):
    planes = 4 * cases * depth
    columns = edge_columns()
    mine = lanes_of((depth, 128)) // 4 == (depth - 1) - rows_of((depth, 128))
    for row in range(8):
        ref, place = row_place((middle_ref, outer_ref), row, planes)
        edges = exact_dot(ref[rows(place, planes), :], columns)
        for pair in range(4 * cases):
            kept = jnp.where(mine, edges[pair * depth : (pair + 1) * depth], 0.0)
            cols_ref[pl.ds(pair * 8 + row, 1), :] = jnp.sum(kept, axis=0, keepdims=True)


def inner_kernel(depth, cases, middle_ref, outer_ref, source_ref, coef_ref, *rest):
    out_ref, *more_refs, deriv_ref = rest
    planes = 4 * cases * depth
    lane, layer = lanes_of((8, 128)), rows_of((8, 128))
    gap = rows_of((128, 256)) - lanes_of((128, 256)) % 128
    second = jnp.where(jnp.abs(gap) == 1, 16.0, jnp.where(jnp.abs(gap) == 2, -1.0, 0.0))
    first = jnp.where(gap == 1, 8.0, jnp.where(gap == -1, -8.0, jnp.where(gap == 2, -1.0, jnp.where(gap == -2, 1.0, 0.0))))
    weights = jnp.where(lanes_of((128, 256)) < 128, second, first).astype(jnp.bfloat16)
    for row in range(8):
        ref, place = row_place((middle_ref, outer_ref), row, planes)
        value = ref[rows(place, planes), :]
        deriv_ref[rows(row * planes, planes), :] = exact_dot(value, weights)

    def one(index, _):
        case, block = index // (depth // 8), index % (depth // 8)
        k = layer + 8 * block
        height = (k.astype(jnp.float32) + 0.5) / depth
        offsets = [pl.multiple_of((c * cases + case) * depth + 8 * block, 8) for c in range(4)]
        places = [row_place((middle_ref, outer_ref), row, planes) for row in range(8)]
        tiles = [[ref[rows(place + offsets[c]), :] for ref, place in places] for c in range(4)]

        for row in range(8):

            def coef(i):
                return coef_ref[pl.ds((case * N_COEF + i) * 8 + row, 1), :]

            along = []
            for c in range(4):
                near = [tiles[c][row + by] if 0 <= row + by < 8 else None for by in (-2, -1, 1, 2)]
                along.append(near)

            def first_x(c):
                m2, m1, p1, p2 = along[c]
                ones = 8.0 * (p1 - m1) if m1 is not None and p1 is not None else 8.0 * p1 if m1 is None else -8.0 * m1
                if m2 is not None and p2 is not None:
                    return ones - (p2 - m2)
                return ones - p2 if m2 is None else ones + m2

            def second_x(c):
                m2, m1, p1, p2 = along[c]
                ones = 16.0 * (p1 + m1) if m1 is not None and p1 is not None else 16.0 * (p1 if m1 is None else m1)
                if m2 is not None and p2 is not None:
                    return ones - (p2 + m2)
                return ones - (p2 if m2 is None else m2)

            carry = coef(CARRY) * height
            sound = coef(SOUND_STEP)
            step = coef(STEP)
            slopes = [first_x(c) for c in range(4)]
            for c in range(4):
                here = row * planes + offsets[c]
                ref, place = places[row]
                behind = jnp.where(k > 0, ref[rows(place + offsets[c] - 1), :], 0.0)
                beyond = jnp.where(k < depth - 1, ref[rows(place + offsets[c] + 1), :], 0.0)
                source = source_ref[strided(offsets[c] * 8 + row), :]
                w = WEIGHT[c]
                value = coef(CENTER + w) * tiles[c][row] + coef(SPREAD + w) * (second_x(c) + deriv_ref[rows(here), 0:128])
                value += coef(ACROSS + w) * (behind + beyond) + step * source + carry * slopes[c]
                if c == 0:
                    other = row * planes + offsets[2]
                    value += sound * (slopes[1] + deriv_ref[rows(other), 128:256])
                elif c == 1:
                    value += sound * slopes[0]
                elif c == 2:
                    other = row * planes + offsets[0]
                    value += sound * deriv_ref[rows(other), 128:256]
                else:
                    value += coef(HEAT) * tiles[1][row]
                out_ref[rows(here), :] = value
        return 0

    lax.fori_loop(0, cases * (depth // 8), one, 0)

    if more_refs:
        (total_ref,) = more_refs
        for case in range(cases):
            for row in range(8):
                total = jnp.zeros((8, 128), jnp.float32)
                for block in range(depth // 8):
                    total += source_ref[strided((case * depth + 8 * block) * 8 + row), :]
                total_ref[pl.ds(case * 8 + row, 1), :] = jnp.sum(total, axis=0, keepdims=True)


def columns_beyond(cases, side_ref, mask_ref, packed_ref, corr_ref):
    slot = lanes_of((8, 128)) % 4
    for case in range(cases):
        coefs = [packed_ref[rows((case * N_PACKED + i) * 8), :] for i in range(N_PACKED)]
        second, first = [], []
        for c in range(4):
            side = side_ref[rows((c * cases + case) * 8), :] * mask_ref[...]
            p1 = jnp.where(slot == 1, pltpu.roll(side, 127, 1), 0.0)
            p2 = jnp.where(slot < 2, pltpu.roll(side, 126, 1), 0.0)
            m1 = jnp.where(slot == 2, pltpu.roll(side, 1, 1), 0.0)
            m2 = jnp.where(slot >= 2, pltpu.roll(side, 2, 1), 0.0)
            second.append(16.0 * (p1 + m1) - (p2 + m2))
            first.append(8.0 * (p1 - m1) - (p2 - m2))
        for c in range(4):
            value = coefs[WEIGHT[c]] * second[c]
            if c == 0:
                value += coefs[3] * first[2]
            elif c == 2:
                value += coefs[3] * first[0]
            corr_ref[rows((c * cases + case) * 8), :] = value


def depth_sum(tiles):
    total = tiles[0]
    for tile in tiles[1:]:
        total = total + tile
    return jnp.sum(total, axis=0, keepdims=True)


def next_moments(depth, tiles_of, layer):
    density = tiles_of(0)
    heights = [(layer + (8 * block + 0.5)).astype(jnp.float32) / depth for block in range(depth // 8)]
    return (
        depth_sum(density),
        depth_sum([tile * height for tile, height in zip(density, heights, strict=True)]),
        depth_sum(tiles_of(1)),
        depth_sum(tiles_of(2)),
        density[0][0:1] + density[-1][7:8],
    )


def wall_sums(depth, tiles_of, layer):
    momentum, before = tiles_of(1), tiles_of(1, -1)
    changes = [momentum[0] - jnp.where(layer > 0, before[0], 0.0)]
    changes += [here - there for here, there in zip(momentum[1:], before[1:], strict=True)]
    squares = [change * change for change in changes] + [jnp.where(layer == 7, momentum[-1] * momentum[-1], 0.0)]
    return depth_sum(tiles_of(0)), depth_sum(squares)


def line_sums(depth, cases, planes, sums, ref, which, out_ref, layer):
    for case in range(cases):
        for i, row in enumerate(which):

            def tiles_of(c, by=0):
                start = PAD + i * planes + (c * cases + case) * depth
                return [ref[rows(start + by + 8 * block), :] for block in range(depth // 8)]

            lines = sums(depth, tiles_of, layer)
            for n, line in enumerate(lines):
                out_ref[pl.ds((case * len(lines) + n) * 8 + row, 1), :] = line


def joined_sums(middle_ref, outer_ref, index, layer):
    return jnp.where((layer >= 2) & (layer < 6), middle_ref[rows(index * 8), :], outer_ref[rows(index * 8), :])


def sides_kernel(depth, cases, sums, inner_ref, side_ref, mask_ref, packed_ref, middle_ref, loose_ref, sums_ref, corr_ref):
    planes = 4 * cases * depth
    lane, layer = lanes_of((8, 128)), rows_of((8, 128))
    edge = (lane < 2) | (lane >= 126)
    columns_beyond(cases, side_ref, mask_ref, packed_ref, corr_ref)

    def one(case, _):
        for row in range(8):
            for c in range(4):
                line = jnp.broadcast_to(corr_ref[pl.ds((c * cases + case) * 8 + row, 1), :], (8, 128))
                for block in range(depth // 8):
                    offset = pl.multiple_of((c * cases + case) * depth + 8 * block, 8)
                    moved = pltpu.roll(line, 2 + 32 * block, 1, stride=4, stride_axis=0)
                    value = inner_ref[rows(row * planes + offset), :] + jnp.where(edge, moved, 0.0)
                    ref, place = row_place((middle_ref, loose_ref), row, planes)
                    ref[rows(place + offset), :] = value
        return 0

    lax.fori_loop(0, cases, one, 0)
    line_sums(depth, cases, planes, sums, middle_ref, MIDDLE, sums_ref, layer)


def outer_rows(depth, cases, planes, parts, loose_ref, post, coef_ref, store):
    layer = rows_of((8, 128))

    def one(case, _):
        for block in range(depth // 8):
            height = ((layer + 8 * block).astype(jnp.float32) + 0.5) / depth
            offsets = [pl.multiple_of((c * cases + case) * depth + 8 * block, 8) for c in range(4)]
            near = {c: [post.get(rows(i * planes + offsets[c])) for i in range(2)] for c in {*parts, *range(2)}}
            whole = {c: {} for c in parts}
            for i, row in enumerate(OUTER):

                def coef(n):
                    return coef_ref[pl.ds((case * N_COEF + n) * 8 + row, 1), :]

                second, first = {}, {}
                for c, ((m2, p1), (m1, p2)) in near.items():
                    if row == 0:
                        second[c], first[c] = 16.0 * m1 - m2, m2 - 8.0 * m1
                    elif row == 1:
                        second[c], first[c] = -m1, m1
                    elif row == 6:
                        second[c], first[c] = -p1, -p1
                    else:
                        second[c], first[c] = 16.0 * p1 - p2, 8.0 * p1 - p2
                for c in parts:
                    value = loose_ref[rows(PAD + i * planes + offsets[c]), :]
                    value += coef(SPREAD + WEIGHT[c]) * second[c] + coef(CARRY) * height * first[c]
                    if c < 2:
                        value += coef(SOUND_STEP) * first[1 - c]
                    whole[c][row] = value
            for c in parts:
                store(c, case, block, offsets[c], whole[c])
        return 0

    lax.fori_loop(0, cases, one, 0)


def joined_kernel(
    depth,
    cases,
    place_ref,
    loose_ref,
    middle_sums_ref,
    source_total_ref,
    second_in_ref,
    first_in_ref,
    coef_ref,
    outer_ref,
    second_ref,
    first_ref,
    moment_ref,
    outer_sums_ref,
):
    planes = 4 * cases * depth
    lane, layer = lanes_of((8, 128)), rows_of((8, 128))
    post, arrived = Post(place_ref, first_ref, second_ref), Post(place_ref, first_in_ref, second_in_ref)

    def store(c, case, block, offset, tiles):
        for i, row in enumerate(OUTER):
            outer_ref[rows(PAD + i * planes + offset), :] = tiles[row]
        post.put_tiles(planes, offset, tiles)

    outer_rows(depth, cases, planes, range(4), loose_ref, arrived, coef_ref, store)

    line_sums(depth, cases, planes, next_moments, outer_ref, OUTER, outer_sums_ref, layer)
    for case in range(cases):

        def coef(i):
            return coef_ref[rows((case * N_COEF + i) * 8), :]

        moments = [joined_sums(middle_sums_ref, outer_sums_ref, case * 5 + i, layer) for i in range(5)]
        total, lifted, along, across, walls = moments
        for i in range(3):
            moment_ref[rows((case * 3 + i) * 8), :] = moments[i]

        def x_parts(plane):
            m1, m2 = jnp.where(layer >= 1, pltpu.roll(plane, 1, 0), 0.0), jnp.where(layer >= 2, pltpu.roll(plane, 2, 0), 0.0)
            p1, p2 = jnp.where(layer < 7, pltpu.roll(plane, 7, 0), 0.0), jnp.where(layer < 6, pltpu.roll(plane, 6, 0), 0.0)
            return 16.0 * (p1 + m1) - (p2 + m2), 8.0 * (p1 - m1) - (p2 - m2)

        def y_parts(plane):
            m1, m2 = jnp.where(lane >= 1, pltpu.roll(plane, 1, 1), 0.0), jnp.where(lane >= 2, pltpu.roll(plane, 2, 1), 0.0)
            p1, p2 = jnp.where(lane < 127, pltpu.roll(plane, 127, 1), 0.0), jnp.where(lane < 126, pltpu.roll(plane, 126, 1), 0.0)
            return 16.0 * (p1 + m1) - (p2 + m2), 8.0 * (p1 - m1) - (p2 - m2)

        value = coef(CENTER) * total + coef(SPREAD) * (x_parts(total)[0] + y_parts(total)[0])
        value += coef(ACROSS) * (2.0 * total - walls) + coef(CARRY) * x_parts(lifted)[1]
        value += coef(SOUND_STEP) * (x_parts(along)[1] + y_parts(across)[1]) + coef(STEP) * source_total_ref[rows(case * 8), :]
        sent = (value, coef(SPREAD), coef(CARRY), coef(SOUND_STEP), coef(FLUX))
        for i, plane in enumerate(sent):
            post.put(pl.ds(2 * planes + (case * 5 + i) * 2, 2), plane[6:8], plane[0:2])


def edge_sums(tile):
    for by in (4, 8, 16, 32, 64):
        tile = tile + pltpu.roll(tile, by, 1)
    return pltpu.roll(tile, 2, 1)


def final_kernel(
    depth,
    cases,
    place_ref,
    loose_ref,
    middle_sums_ref,
    corr_ref,
    second_in_ref,
    first_in_ref,
    coef_ref,
    moment_ref,
    outer_ref,
    grad_ref,
    line_ref,
    outer_sums_ref,
):
    planes = 4 * cases * depth
    lane, layer = lanes_of((8, 128)), rows_of((8, 128))
    arrived = Post(place_ref, first_in_ref, second_in_ref)

    def store(c, case, block, offset, tiles):
        for i, row in enumerate(OUTER):
            outer_ref[rows(PAD + i * planes + offset), :] = tiles[row]

    outer_rows(depth, cases, planes, range(2), loose_ref, arrived, coef_ref, store)
    line_sums(depth, cases, planes, wall_sums, outer_ref, OUTER, outer_sums_ref, layer)

    zero = jnp.zeros((8, 128), jnp.float32)
    grad, missing = zero, zero
    for case in range(cases):

        def coef(i):
            return coef_ref[rows((case * N_COEF + i) * 8), :]

        pairs = [arrived.get(pl.ds(2 * planes + (case * 5 + i) * 2, 2)) for i in range(5)]
        below, above = [pair[0] for pair in pairs], [pair[1] for pair in pairs]
        total, lifted, along = (moment_ref[rows((case * 3 + i) * 8), :] for i in range(3))

        def beyond(plane):
            first, second, last, before = plane[0:1], plane[1:2], plane[7:8], plane[6:7]
            down = (jnp.concatenate([-first, 16.0 * first - second], 0), jnp.concatenate([-first, 8.0 * first - second], 0))
            up = (jnp.concatenate([16.0 * last - before, -last], 0), jnp.concatenate([before - 8.0 * last, last], 0))
            return down, up

        down, up = zip(beyond(total), beyond(lifted), beyond(along), strict=True)
        mean_below = below[0] + below[1] * down[0][0] + below[2] * down[1][1] + below[3] * down[2][1]
        mean_above = above[0] + above[1] * up[0][0] + above[2] * up[1][1] + above[3] * up[2][1]
        mean, bend = (joined_sums(middle_sums_ref, outer_sums_ref, case * 2 + i, layer) for i in range(2))
        halo = jnp.concatenate([mean_above, zero[0:4], mean_below], axis=0)
        m1 = pltpu.roll(jnp.where(layer == 7, halo, mean), 1, 0)
        m2 = pltpu.roll(jnp.where(layer >= 6, halo, mean), 2, 0)
        p1 = pltpu.roll(jnp.where(layer == 0, halo, mean), 7, 0)
        p2 = pltpu.roll(jnp.where(layer < 2, halo, mean), 6, 0)
        grad += coef(FLUX) * (8.0 * (p1 - m1) - (p2 - m2)) + coef(BEND) * bend
        change = edge_sums(corr_ref[rows(case * 8), :])
        down_rows = jnp.concatenate([change[6:7] - 8.0 * change[7:8], change[7:8]], axis=0)
        up_rows = jnp.concatenate([-change[0:1], 8.0 * change[0:1] - change[1:2]], axis=0)
        missing += jnp.concatenate([above[4] * down_rows, zero[0:4], below[4] * up_rows], axis=0)
    corner = ((lane < 2) | (lane >= 126)) & ((layer < 2) | (layer >= 6))
    grad_ref[...] = grad
    inside = jnp.where(corner, 0.0, grad)
    rest = jnp.sum(inside * inside, axis=0, keepdims=True)
    corners = pltpu.roll(jnp.where(corner, grad, 0.0), 2, 1, stride=4, stride_axis=0)
    shares = pltpu.roll(jnp.where(corner, missing, 0.0), 34, 1, stride=4, stride_axis=0)
    line = jnp.sum(corners + shares, axis=0, keepdims=True)
    line = jnp.where(lanes_of((1, 128)) < 64, line, rest + pltpu.roll(rest, 64, 1))
    line_ref[...] = jnp.broadcast_to(line[None], line_ref.shape)


def rest_kernel(
    depth,
    cases,
    place_ref,
    loose_ref,
    middle_ref,
    early_ref,
    second_in_ref,
    first_in_ref,
    coef_ref,
    out_ref,
    state_ref,
    sems,
):
    planes = 4 * cases * depth
    half = planes * 4
    copies = [pltpu.make_async_copy(state_ref.at[rows(i * half, half), :], out_ref.at[rows(i * half, half), :], sems.at[i]) for i in range(2)]

    def place_tiles(c, refs):
        def one(case, _):
            for block in range(depth // 8):
                offset = pl.multiple_of((c * cases + case) * depth + 8 * block, 8)
                for row in range(8):
                    if refs[row] is not None:
                        ref, place = row_place(refs[row], row, planes)
                        state_ref[strided(offset * 8 + row), :] = ref[rows(place + offset), :]
            return 0

        lax.fori_loop(0, cases, one, 0)

    both = (middle_ref, early_ref)
    for c in range(2):
        place_tiles(c, [both] * 8)
    copies[0].start()
    for c in range(2, 4):
        place_tiles(c, [both if row in MIDDLE else None for row in range(8)])

    def store(c, case, block, offset, tiles):
        for row, tile in tiles.items():
            state_ref[strided(offset * 8 + row), :] = tile

    arrived = Post(place_ref, first_in_ref, second_in_ref)
    outer_rows(depth, cases, planes, (2, 3), loose_ref, arrived, coef_ref, store)
    copies[1].start()
    copies[0].wait()
    copies[1].wait()


def scale_kernel(cells, devices, trans, place_ref, grad_ref, sums_ref, out_ref, lines_ref):
    pad = -(-trans // 8) * 8
    lane, row = lanes_of((8, 128)), rows_of((8, 128))
    zero = jnp.zeros((pad, 128), jnp.float32)
    lines_ref[rows(0, pad), :] = zero
    lines_ref[rows(pad + devices, pad), :] = zero
    lines_ref[rows(pad, devices), :] = sums_ref[...]
    total, own = jnp.zeros((8, 128), jnp.float32), jnp.zeros((8, 128), jnp.float32)
    device = place_ref[rows(DEVICE * 8), :]
    for block in range(devices // 8):
        here = lines_ref[rows(pad + 8 * block), :]
        below, above = lines_ref[rows(pad - trans + 8 * block), :], lines_ref[rows(pad + trans + 8 * block), :]
        share = pltpu.roll(jnp.where(lane < 48, below, above), 96, 1)
        own += jnp.where(row + 8 * block == device, share, 0.0)
        corner = here + share
        total += jnp.where(lane < 32, corner * corner, jnp.where(lane >= 64, here, 0.0))
    total = jnp.sum(jnp.sum(total, axis=0, keepdims=True), axis=1, keepdims=True)
    own = jnp.broadcast_to(jnp.sum(own, axis=0, keepdims=True), (8, 128))
    grad = grad_ref[...]
    edge = (lane < 2) | (lane >= 126)
    for i in (0, 1, 6, 7):
        grad += jnp.where((row == i) & edge, pltpu.roll(own, (126 - 4 * i) % 128, 1), 0.0)
    out_ref[...] = grad / jnp.sqrt(total / cells + 1e-06)


def f32(*shape):
    return jax.ShapeDtypeStruct(shape, jnp.float32)


def over_tiles(numbers):
    which = rows_of((8 * len(numbers), 128)) // 8
    held = jnp.full(which.shape, numbers[0], jnp.int32)
    for i, number in enumerate(numbers[1:], 1):
        held = jnp.where(which == i, number, held)
    return held


def in_hbm(array):
    return pltpu.with_memory_space_constraint(array, pltpu.HBM)


def call(kernel, *args, outs, scratch=(), hbm=None, out=VM):
    specs = [VM] * len(args)
    if hbm is not None:
        specs[hbm] = HB
    return pl.pallas_call(
        kernel,
        out_shape=outs,
        in_specs=specs,
        out_specs=tuple([out] * len(outs)),
        scratch_shapes=[pltpu.VMEM(shape, jnp.float32) if isinstance(shape, tuple) else shape for shape in scratch],
        compiler_params=PARAMS,
    )(*args)


def neighbours(axis):
    size = lax.axis_size(axis)
    up = [(i, i + 1) for i in range(size - 1)]
    return up, [(j, i) for i, j in up]


def exchange_rows(first, second):
    size = lax.axis_size("roll")
    inner = [(i, i ^ 1) for i in range(size) if i ^ 1 < size]
    outer = [pair for i in range(1, size - 1, 2) for pair in ((i, i + 1), (i + 1, i))]
    second = lax.ppermute(second, "roll", outer)
    return lax.ppermute(first, "roll", inner), second


def exchange_columns(cols):
    ahead, back = neighbours("trans")
    if lax.axis_size("trans") == 2:
        return lax.ppermute(cols, "trans", ahead + back)
    left, right = lax.ppermute(cols, "trans", ahead), lax.ppermute(cols, "trans", back)
    return jnp.where(lanes_of(cols.shape) % 4 < 2, left, right)


def on_device(adjoint, source, pressure, film, cavity, temp_index):
    components, cases, depth, width_x, width_y = adjoint.shape
    planes = components * cases * depth
    assert (components, width_x, width_y, 4 * depth) == (4, 8, 128, 128)
    state = adjoint.reshape(planes * 8, 128)
    forcing = source.reshape(planes * 8, 128)
    roll, trans, trans_size = lax.axis_index("roll"), lax.axis_index("trans"), lax.axis_size("trans")
    place = over_tiles([trans, trans_size, roll % 2, roll * trans_size + trans])
    level = jnp.broadcast_to(temp_index[:, None, None], (cases, 8, 128)).reshape(cases * 8, 128)
    devices = lax.axis_size("roll") * trans_size
    inner, part = f32(planes * 8, 128), f32(planes * 4 + 2 * PAD, 128)
    message, cols_shape = f32(planes * 2 + TAIL, 128), f32(components * cases * 8, 128)
    coef, packed, mask = call(
        functools.partial(coefficient_kernel, depth, cases),
        level,
        place,
        pressure.reshape(cases * 8, 128),
        film,
        cavity.reshape(cases * 8, 128),
        outs=(f32(cases * N_COEF * 8, 128), f32(cases * N_PACKED * 8, 128), f32(8, 128)),
    )
    state, first, second = call(
        functools.partial(send_kernel, depth, cases),
        place,
        in_hbm(state),
        outs=(inner, message, message),
        scratch=[pltpu.SemaphoreType.DMA((PIECES,))],
        hbm=1,
    )
    middle, outer, cols, forcing = call(
        functools.partial(pack_kernel, depth, cases),
        state,
        in_hbm(forcing),
        outs=(part, part, cols_shape, inner),
        scratch=[pltpu.SemaphoreType.DMA],
        hbm=1,
    )
    for index in range(SECTIONS):
        more = index < SECTIONS - 1
        first, second = exchange_rows(first, second)
        side = exchange_columns(cols)
        whole, *total = call(
            functools.partial(inner_kernel, depth, cases),
            middle,
            outer,
            forcing,
            coef,
            outs=(inner, f32(cases * 8, 128)) if more else (inner,),
            scratch=[(planes * 8, 256)],
        )
        middle, loose, sums, corr = call(
            functools.partial(sides_kernel, depth, cases, next_moments if more else wall_sums),
            whole,
            side,
            mask,
            packed,
            outs=(part, part, f32(cases * (5 if more else 2) * 8, 128), cols_shape),
        )
        if more:
            outer, second, first, moments = call(
                functools.partial(joined_kernel, depth, cases),
                place,
                loose,
                sums,
                *total,
                second,
                first,
                coef,
                outs=(part, message, message, f32(cases * 3 * 8, 128)),
                scratch=[(cases * 5 * 8, 128)],
            )
            (cols,) = call(functools.partial(columns_kernel, depth, cases), middle, outer, outs=(cols_shape,))
        else:
            early, grad, sums = call(
                functools.partial(final_kernel, depth, cases),
                place,
                loose,
                sums,
                corr,
                second,
                first,
                coef,
                moments,
                outs=(part, f32(8, 128), pltpu.VMEM((devices, 1, 128), jnp.float32)),
                scratch=[(cases * 2 * 8, 128)],
            )
            (state,) = call(
                functools.partial(rest_kernel, depth, cases),
                place,
                loose,
                middle,
                early,
                second,
                first,
                coef,
                outs=(pltpu.HBM(inner.shape, jnp.float32),),
                scratch=[inner.shape, pltpu.SemaphoreType.DMA((2,))],
                out=HB,
            )
    sums = lax.all_to_all(sums, ("roll", "trans"), 0, 0, tiled=True).reshape(devices, 128)
    pad = -(-trans_size // 8) * 8
    (wall_step,) = call(
        functools.partial(scale_kernel, devices * width_x * width_y, devices, trans_size),
        place,
        grad,
        sums,
        outs=(f32(8, 128),),
        scratch=[(devices + 2 * pad, 128)],
    )
    return (state.reshape(adjoint.shape), wall_step)


def solution(mesh):
    placed = (
        P(None, None, None, "roll", "trans"),
        P(None, None, None, "roll", "trans"),
        P(None, "roll", "trans"),
        P("roll", "trans"),
        P(None, "roll", "trans"),
        P(),
    )
    return jax.shard_map(
        on_device,
        mesh=mesh,
        in_specs=placed,
        out_specs=(P(None, None, None, "roll", "trans"), P("roll", "trans")),
        check_vma=False,
    )
```

```python
import functools

import jax
import jax.numpy as jnp
from jax import lax
from jax.experimental import pallas as pl
from jax.experimental.pallas import tpu as pltpu
from jax.sharding import PartitionSpec as P

SECTIONS = 2


VISCOSITY_PRESS = 0.3
VISCOSITY_TEMP = 0.5
THETA_STEP = 0.2
SOUND = 0.5
KAPPA = 0.6
HEATING = 0.3
ROLL_SPEED = 1.0
COURANT = 0.8

VM = pl.BlockSpec(memory_space=pltpu.VMEM)
HB = pl.BlockSpec(memory_space=pltpu.HBM)
PARAMS = pltpu.CompilerParams(vmem_limit_bytes=16 * 1024 * 1024)

PAD = 8
CENTER, SPREAD, ACROSS = (0, 3, 6)
CARRY, SOUND_STEP, STEP, HEAT, FLUX, BEND = range(9, 15)
N_COEF = 15
N_PACKED = 4
PIECES = 4
TAIL = 24
MIDDLE, OUTER = (2, 3, 4, 5), (0, 1, 6, 7)
TRANS, TRANS_SIZE, ODD, DEVICE = range(4)
WEIGHT = (0, 1, 1, 2)


def lanes_of(shape):
    return lax.broadcasted_iota(jnp.int32, shape, 1)


def rows_of(shape):
    return lax.broadcasted_iota(jnp.int32, shape, 0)


def rows(start, count=8):
    return pl.ds(start, count)


def strided(start):
    return pl.ds(start, 8, stride=8)


def coefficients(depth, cases, place_ref, level_ref, pressure_ref, film_ref, cavity_ref, coef_ref, packed_ref, mask_ref):
    lane, row = lanes_of((8, 128)), rows_of((8, 128))
    film = film_ref[...]
    for case in range(cases):
        theta = THETA_STEP * jnp.broadcast_to(level_ref[:, case : case + 1], (8, 128)).astype(jnp.float32)
        viscosity = jnp.exp(VISCOSITY_PRESS * pressure_ref[rows(case * 8), :] - VISCOSITY_TEMP * theta)
        film_coef = 4.0 * viscosity / (film * film)
        density = 1.0 - 0.6 * cavity_ref[rows(case * 8), :].astype(jnp.float32)
        step = COURANT / (32.0 / 3.0 * viscosity + 4.0 * film_coef + 2.0 * SOUND + 1.0)
        planes = [None] * N_COEF
        for i, weight in enumerate((0.5, 1.0, KAPPA)):
            planes[SPREAD + i] = (weight / 12.0) * step * viscosity
            planes[ACROSS + i] = weight * step * film_coef
            planes[CENTER + i] = 1.0 - 60.0 * planes[SPREAD + i] - 2.0 * planes[ACROSS + i]
        planes[CARRY] = (ROLL_SPEED / 12.0) * step * density
        planes[SOUND_STEP] = (SOUND / 12.0) * step
        planes[STEP] = step
        planes[HEAT] = HEATING * step * viscosity
        planes[FLUX] = (ROLL_SPEED / (24.0 * depth)) * density * film
        planes[BEND] = (8.0 / depth) * viscosity / (film * film * film)
        for i, plane in enumerate(planes):
            coef_ref[rows((case * N_COEF + i) * 8), :] = plane
        wanted = jnp.concatenate(planes[SPREAD : SPREAD + 3] + [planes[SOUND_STEP]], axis=0)
        packed = exact_dot(wanted, edge_columns())
        for i in range(N_PACKED):
            packed_ref[rows((case * N_PACKED + i) * 8), :] = packed[i * 8 : i * 8 + 8]
    trans = place_ref[rows(TRANS * 8), :]
    from_left = jnp.where(trans > 0, 1.0, 0.0)
    from_right = jnp.where(trans < place_ref[rows(TRANS_SIZE * 8), :] - 1, 1.0, 0.0)
    mask_ref[...] = jnp.where(lane % 4 < 2, from_left, from_right)


def edge_columns():
    source = lanes_of((128, 128)) % 4
    source = jnp.where(source < 2, 126 + source, source - 2)
    return jnp.where(rows_of((128, 128)) == source, 1.0, 0.0).astype(jnp.bfloat16)


def in_parts(value):
    high = value.astype(jnp.bfloat16)
    rest = value - high.astype(jnp.float32)
    middle = rest.astype(jnp.bfloat16)
    return jnp.concatenate([high, middle], axis=1), (rest - middle.astype(jnp.float32)).astype(jnp.bfloat16)


def exact_dot(value, weights):
    upper, low = in_parts(value)
    part = jnp.dot(upper, jnp.concatenate([weights, weights], axis=0), preferred_element_type=jnp.float32)
    return part + jnp.dot(low, weights, preferred_element_type=jnp.float32)


class Post:
    def __init__(self, place_ref, first_ref, second_ref):
        self.odd = place_ref[rows(ODD * 8), :] == 1
        self.refs = first_ref, second_ref

    def put(self, where, up, down):
        first, second = self.refs
        odd = self.odd[: where.size]
        first[where, :] = jnp.where(odd, down, up)
        second[where, :] = jnp.where(odd, up, down)

    def get(self, where):
        first, second = (ref[where, :] for ref in self.refs)
        odd = self.odd[: where.size]
        return jnp.where(odd, first, second), jnp.where(odd, second, first)

    def put_tiles(self, planes, first, tiles):
        for i in range(2):
            self.put(rows(i * planes + first), tiles[6 + i], tiles[i])


def row_place(refs, row, planes):
    if row in MIDDLE:
        return refs[0], PAD + MIDDLE.index(row) * planes
    return refs[1], PAD + OUTER.index(row) * planes


def send_kernel(depth, cases, place_ref, state_ref, copy_ref, first_ref, second_ref, sems):
    planes = 4 * cases * depth
    post = Post(place_ref, first_ref, second_ref)

    def piece(i):
        here = rows(i * (planes * 8 // PIECES), planes * 8 // PIECES)
        return pltpu.make_async_copy(state_ref.at[here, :], copy_ref.at[here, :], sems.at[i])

    for i in range(PIECES):
        piece(i).start()
    for i in range(PIECES):
        piece(i).wait()
        for first in range(i * planes // PIECES, (i + 1) * planes // PIECES, 8):
            post.put_tiles(planes, first, {row: copy_ref[strided(first * 8 + row), :] for row in (0, 1, 6, 7)})


def pack_kernel(depth, cases, state_ref, place_ref, *rest):
    (middle_ref, outer_ref, cols_ref), outs, held, sems = rest[4:7], rest[7:10], rest[10:14], rest[14]
    copies = [pltpu.make_async_copy(rest[i], held[i], sems.at[i]) for i in range(4)]
    for copy in copies:
        copy.start()
    planes = 4 * cases * depth
    lane = lanes_of((8, 128))

    def one(pair, _):
        held = jnp.zeros((8, 128), jnp.float32)
        for layer in range(depth):
            group = depth - 1 - layer
            plane = state_ref[rows(pl.multiple_of((pair * depth + layer) * 8, 8)), :]
            held = jnp.where(lane // 4 == group, pltpu.roll(plane, (4 * group + 2) % 128, 1), held)
        cols_ref[rows(pl.multiple_of(pair * 8, 8)), :] = held
        for row in range(8):
            for block in range(depth // 8):
                first = pl.multiple_of(pair * depth + 8 * block, 8)
                ref, place = row_place((middle_ref, outer_ref), row, planes)
                ref[rows(place + first), :] = state_ref[strided(first * 8 + row), :]
        return 0

    lax.fori_loop(0, 4 * cases, one, 0)
    for copy in copies:
        copy.wait()
    coefficients(depth, cases, place_ref, *held, *outs)


def columns_kernel(depth, cases, middle_ref, outer_ref, cols_ref):
    planes = 4 * cases * depth
    columns = edge_columns()
    mine = lanes_of((depth, 128)) // 4 == (depth - 1) - rows_of((depth, 128))
    for row in range(8):
        ref, place = row_place((middle_ref, outer_ref), row, planes)
        edges = exact_dot(ref[rows(place, planes), :], columns)
        for pair in range(4 * cases):
            kept = jnp.where(mine, edges[pair * depth : (pair + 1) * depth], 0.0)
            cols_ref[pl.ds(pair * 8 + row, 1), :] = jnp.sum(kept, axis=0, keepdims=True)


def inner_kernel(depth, cases, middle_ref, outer_ref, source_ref, coef_ref, *rest):
    out_ref, *more_refs, deriv_ref = rest
    planes = 4 * cases * depth
    lane, layer = lanes_of((8, 128)), rows_of((8, 128))
    gap = rows_of((128, 256)) - lanes_of((128, 256)) % 128
    second = jnp.where(jnp.abs(gap) == 1, 16.0, jnp.where(jnp.abs(gap) == 2, -1.0, 0.0))
    first = jnp.where(gap == 1, 8.0, jnp.where(gap == -1, -8.0, jnp.where(gap == 2, -1.0, jnp.where(gap == -2, 1.0, 0.0))))
    weights = jnp.where(lanes_of((128, 256)) < 128, second, first).astype(jnp.bfloat16)
    for row in range(8):
        ref, place = row_place((middle_ref, outer_ref), row, planes)
        value = ref[rows(place, planes), :]
        deriv_ref[rows(row * planes, planes), :] = exact_dot(value, weights)

    def one(index, _):
        case, block = index // (depth // 8), index % (depth // 8)
        k = layer + 8 * block
        height = (k.astype(jnp.float32) + 0.5) / depth
        offsets = [pl.multiple_of((c * cases + case) * depth + 8 * block, 8) for c in range(4)]
        places = [row_place((middle_ref, outer_ref), row, planes) for row in range(8)]
        tiles = [[ref[rows(place + offsets[c]), :] for ref, place in places] for c in range(4)]

        for row in range(8):

            def coef(i):
                return coef_ref[pl.ds((case * N_COEF + i) * 8 + row, 1), :]

            along = []
            for c in range(4):
                near = [tiles[c][row + by] if 0 <= row + by < 8 else None for by in (-2, -1, 1, 2)]
                along.append(near)

            def first_x(c):
                m2, m1, p1, p2 = along[c]
                ones = 8.0 * (p1 - m1) if m1 is not None and p1 is not None else 8.0 * p1 if m1 is None else -8.0 * m1
                if m2 is not None and p2 is not None:
                    return ones - (p2 - m2)
                return ones - p2 if m2 is None else ones + m2

            def second_x(c):
                m2, m1, p1, p2 = along[c]
                ones = 16.0 * (p1 + m1) if m1 is not None and p1 is not None else 16.0 * (p1 if m1 is None else m1)
                if m2 is not None and p2 is not None:
                    return ones - (p2 + m2)
                return ones - (p2 if m2 is None else m2)

            carry = coef(CARRY) * height
            sound = coef(SOUND_STEP)
            step = coef(STEP)
            slopes = [first_x(c) for c in range(4)]
            for c in range(4):
                here = row * planes + offsets[c]
                ref, place = places[row]
                behind = jnp.where(k > 0, ref[rows(place + offsets[c] - 1), :], 0.0)
                beyond = jnp.where(k < depth - 1, ref[rows(place + offsets[c] + 1), :], 0.0)
                source = source_ref[strided(offsets[c] * 8 + row), :]
                w = WEIGHT[c]
                value = coef(CENTER + w) * tiles[c][row] + coef(SPREAD + w) * (second_x(c) + deriv_ref[rows(here), 0:128])
                value += coef(ACROSS + w) * (behind + beyond) + step * source + carry * slopes[c]
                if c == 0:
                    other = row * planes + offsets[2]
                    value += sound * (slopes[1] + deriv_ref[rows(other), 128:256])
                elif c == 1:
                    value += sound * slopes[0]
                elif c == 2:
                    other = row * planes + offsets[0]
                    value += sound * deriv_ref[rows(other), 128:256]
                else:
                    value += coef(HEAT) * tiles[1][row]
                out_ref[rows(here), :] = value
        return 0

    lax.fori_loop(0, cases * (depth // 8), one, 0)

    if more_refs:
        (total_ref,) = more_refs
        for case in range(cases):
            for row in range(8):
                total = jnp.zeros((8, 128), jnp.float32)
                for block in range(depth // 8):
                    total += source_ref[strided((case * depth + 8 * block) * 8 + row), :]
                total_ref[pl.ds(case * 8 + row, 1), :] = jnp.sum(total, axis=0, keepdims=True)


def columns_beyond(cases, side_ref, mask_ref, packed_ref, corr_ref):
    slot = lanes_of((8, 128)) % 4
    for case in range(cases):
        coefs = [packed_ref[rows((case * N_PACKED + i) * 8), :] for i in range(N_PACKED)]
        second, first = [], []
        for c in range(4):
            side = side_ref[rows((c * cases + case) * 8), :] * mask_ref[...]
            p1 = jnp.where(slot == 1, pltpu.roll(side, 127, 1), 0.0)
            p2 = jnp.where(slot < 2, pltpu.roll(side, 126, 1), 0.0)
            m1 = jnp.where(slot == 2, pltpu.roll(side, 1, 1), 0.0)
            m2 = jnp.where(slot >= 2, pltpu.roll(side, 2, 1), 0.0)
            second.append(16.0 * (p1 + m1) - (p2 + m2))
            first.append(8.0 * (p1 - m1) - (p2 - m2))
        for c in range(4):
            value = coefs[WEIGHT[c]] * second[c]
            if c == 0:
                value += coefs[3] * first[2]
            elif c == 2:
                value += coefs[3] * first[0]
            corr_ref[rows((c * cases + case) * 8), :] = value


def depth_sum(tiles):
    total = tiles[0]
    for tile in tiles[1:]:
        total = total + tile
    return jnp.sum(total, axis=0, keepdims=True)


def next_moments(depth, tiles_of, layer):
    density = tiles_of(0)
    heights = [(layer + (8 * block + 0.5)).astype(jnp.float32) / depth for block in range(depth // 8)]
    return (
        depth_sum(density),
        depth_sum([tile * height for tile, height in zip(density, heights, strict=True)]),
        depth_sum(tiles_of(1)),
        depth_sum(tiles_of(2)),
        density[0][0:1] + density[-1][7:8],
    )


def wall_sums(depth, tiles_of, layer):
    momentum, before = tiles_of(1), tiles_of(1, -1)
    changes = [momentum[0] - jnp.where(layer > 0, before[0], 0.0)]
    changes += [here - there for here, there in zip(momentum[1:], before[1:], strict=True)]
    squares = [change * change for change in changes] + [jnp.where(layer == 7, momentum[-1] * momentum[-1], 0.0)]
    return depth_sum(tiles_of(0)), depth_sum(squares)


def line_sums(depth, cases, planes, sums, ref, which, out_ref, layer):
    for case in range(cases):
        for i, row in enumerate(which):

            def tiles_of(c, by=0):
                start = PAD + i * planes + (c * cases + case) * depth
                return [ref[rows(start + by + 8 * block), :] for block in range(depth // 8)]

            lines = sums(depth, tiles_of, layer)
            for n, line in enumerate(lines):
                out_ref[pl.ds((case * len(lines) + n) * 8 + row, 1), :] = line


def joined_sums(middle_ref, outer_ref, index, layer):
    return jnp.where((layer >= 2) & (layer < 6), middle_ref[rows(index * 8), :], outer_ref[rows(index * 8), :])


def sides_kernel(depth, cases, sums, inner_ref, side_ref, mask_ref, packed_ref, middle_ref, loose_ref, sums_ref, corr_ref):
    planes = 4 * cases * depth
    lane, layer = lanes_of((8, 128)), rows_of((8, 128))
    edge = (lane < 2) | (lane >= 126)
    columns_beyond(cases, side_ref, mask_ref, packed_ref, corr_ref)

    def one(case, _):
        for row in range(8):
            for c in range(4):
                line = jnp.broadcast_to(corr_ref[pl.ds((c * cases + case) * 8 + row, 1), :], (8, 128))
                for block in range(depth // 8):
                    offset = pl.multiple_of((c * cases + case) * depth + 8 * block, 8)
                    moved = pltpu.roll(line, 2 + 32 * block, 1, stride=4, stride_axis=0)
                    value = inner_ref[rows(row * planes + offset), :] + jnp.where(edge, moved, 0.0)
                    ref, place = row_place((middle_ref, loose_ref), row, planes)
                    ref[rows(place + offset), :] = value
        return 0

    lax.fori_loop(0, cases, one, 0)
    line_sums(depth, cases, planes, sums, middle_ref, MIDDLE, sums_ref, layer)


def outer_rows(depth, cases, planes, parts, loose_ref, post, coef_ref, store):
    layer = rows_of((8, 128))

    def one(case, _):
        for block in range(depth // 8):
            height = ((layer + 8 * block).astype(jnp.float32) + 0.5) / depth
            offsets = [pl.multiple_of((c * cases + case) * depth + 8 * block, 8) for c in range(4)]
            near = {c: [post.get(rows(i * planes + offsets[c])) for i in range(2)] for c in {*parts, *range(2)}}
            whole = {c: {} for c in parts}
            for i, row in enumerate(OUTER):

                def coef(n):
                    return coef_ref[pl.ds((case * N_COEF + n) * 8 + row, 1), :]

                second, first = {}, {}
                for c, ((m2, p1), (m1, p2)) in near.items():
                    if row == 0:
                        second[c], first[c] = 16.0 * m1 - m2, m2 - 8.0 * m1
                    elif row == 1:
                        second[c], first[c] = -m1, m1
                    elif row == 6:
                        second[c], first[c] = -p1, -p1
                    else:
                        second[c], first[c] = 16.0 * p1 - p2, 8.0 * p1 - p2
                for c in parts:
                    value = loose_ref[rows(PAD + i * planes + offsets[c]), :]
                    value += coef(SPREAD + WEIGHT[c]) * second[c] + coef(CARRY) * height * first[c]
                    if c < 2:
                        value += coef(SOUND_STEP) * first[1 - c]
                    whole[c][row] = value
            for c in parts:
                store(c, case, block, offsets[c], whole[c])
        return 0

    lax.fori_loop(0, cases, one, 0)


def joined_kernel(
    depth,
    cases,
    place_ref,
    loose_ref,
    middle_sums_ref,
    source_total_ref,
    second_in_ref,
    first_in_ref,
    coef_ref,
    outer_ref,
    second_ref,
    first_ref,
    moment_ref,
    outer_sums_ref,
):
    planes = 4 * cases * depth
    lane, layer = lanes_of((8, 128)), rows_of((8, 128))
    post, arrived = Post(place_ref, first_ref, second_ref), Post(place_ref, first_in_ref, second_in_ref)

    def store(c, case, block, offset, tiles):
        for i, row in enumerate(OUTER):
            outer_ref[rows(PAD + i * planes + offset), :] = tiles[row]
        post.put_tiles(planes, offset, tiles)

    outer_rows(depth, cases, planes, range(4), loose_ref, arrived, coef_ref, store)

    line_sums(depth, cases, planes, next_moments, outer_ref, OUTER, outer_sums_ref, layer)
    for case in range(cases):

        def coef(i):
            return coef_ref[rows((case * N_COEF + i) * 8), :]

        moments = [joined_sums(middle_sums_ref, outer_sums_ref, case * 5 + i, layer) for i in range(5)]
        total, lifted, along, across, walls = moments
        for i in range(3):
            moment_ref[rows((case * 3 + i) * 8), :] = moments[i]

        def x_parts(plane):
            m1, m2 = jnp.where(layer >= 1, pltpu.roll(plane, 1, 0), 0.0), jnp.where(layer >= 2, pltpu.roll(plane, 2, 0), 0.0)
            p1, p2 = jnp.where(layer < 7, pltpu.roll(plane, 7, 0), 0.0), jnp.where(layer < 6, pltpu.roll(plane, 6, 0), 0.0)
            return 16.0 * (p1 + m1) - (p2 + m2), 8.0 * (p1 - m1) - (p2 - m2)

        def y_parts(plane):
            m1, m2 = jnp.where(lane >= 1, pltpu.roll(plane, 1, 1), 0.0), jnp.where(lane >= 2, pltpu.roll(plane, 2, 1), 0.0)
            p1, p2 = jnp.where(lane < 127, pltpu.roll(plane, 127, 1), 0.0), jnp.where(lane < 126, pltpu.roll(plane, 126, 1), 0.0)
            return 16.0 * (p1 + m1) - (p2 + m2), 8.0 * (p1 - m1) - (p2 - m2)

        value = coef(CENTER) * total + coef(SPREAD) * (x_parts(total)[0] + y_parts(total)[0])
        value += coef(ACROSS) * (2.0 * total - walls) + coef(CARRY) * x_parts(lifted)[1]
        value += coef(SOUND_STEP) * (x_parts(along)[1] + y_parts(across)[1]) + coef(STEP) * source_total_ref[rows(case * 8), :]
        sent = (value, coef(SPREAD), coef(CARRY), coef(SOUND_STEP), coef(FLUX))
        for i, plane in enumerate(sent):
            post.put(pl.ds(2 * planes + (case * 5 + i) * 2, 2), plane[6:8], plane[0:2])


def edge_sums(tile):
    for by in (4, 8, 16, 32, 64):
        tile = tile + pltpu.roll(tile, by, 1)
    return pltpu.roll(tile, 2, 1)


def final_kernel(
    depth,
    cases,
    place_ref,
    loose_ref,
    middle_sums_ref,
    corr_ref,
    second_in_ref,
    first_in_ref,
    coef_ref,
    moment_ref,
    outer_ref,
    grad_ref,
    line_ref,
    outer_sums_ref,
):
    planes = 4 * cases * depth
    lane, layer = lanes_of((8, 128)), rows_of((8, 128))
    arrived = Post(place_ref, first_in_ref, second_in_ref)

    def store(c, case, block, offset, tiles):
        for i, row in enumerate(OUTER):
            outer_ref[rows(PAD + i * planes + offset), :] = tiles[row]

    outer_rows(depth, cases, planes, range(2), loose_ref, arrived, coef_ref, store)
    line_sums(depth, cases, planes, wall_sums, outer_ref, OUTER, outer_sums_ref, layer)

    zero = jnp.zeros((8, 128), jnp.float32)
    grad, missing = zero, zero
    for case in range(cases):

        def coef(i):
            return coef_ref[rows((case * N_COEF + i) * 8), :]

        pairs = [arrived.get(pl.ds(2 * planes + (case * 5 + i) * 2, 2)) for i in range(5)]
        below, above = [pair[0] for pair in pairs], [pair[1] for pair in pairs]
        total, lifted, along = (moment_ref[rows((case * 3 + i) * 8), :] for i in range(3))

        def beyond(plane):
            first, second, last, before = plane[0:1], plane[1:2], plane[7:8], plane[6:7]
            down = (jnp.concatenate([-first, 16.0 * first - second], 0), jnp.concatenate([-first, 8.0 * first - second], 0))
            up = (jnp.concatenate([16.0 * last - before, -last], 0), jnp.concatenate([before - 8.0 * last, last], 0))
            return down, up

        down, up = zip(beyond(total), beyond(lifted), beyond(along), strict=True)
        mean_below = below[0] + below[1] * down[0][0] + below[2] * down[1][1] + below[3] * down[2][1]
        mean_above = above[0] + above[1] * up[0][0] + above[2] * up[1][1] + above[3] * up[2][1]
        mean, bend = (joined_sums(middle_sums_ref, outer_sums_ref, case * 2 + i, layer) for i in range(2))
        halo = jnp.concatenate([mean_above, zero[0:4], mean_below], axis=0)
        m1 = pltpu.roll(jnp.where(layer == 7, halo, mean), 1, 0)
        m2 = pltpu.roll(jnp.where(layer >= 6, halo, mean), 2, 0)
        p1 = pltpu.roll(jnp.where(layer == 0, halo, mean), 7, 0)
        p2 = pltpu.roll(jnp.where(layer < 2, halo, mean), 6, 0)
        grad += coef(FLUX) * (8.0 * (p1 - m1) - (p2 - m2)) + coef(BEND) * bend
        change = edge_sums(corr_ref[rows(case * 8), :])
        down_rows = jnp.concatenate([change[6:7] - 8.0 * change[7:8], change[7:8]], axis=0)
        up_rows = jnp.concatenate([-change[0:1], 8.0 * change[0:1] - change[1:2]], axis=0)
        missing += jnp.concatenate([above[4] * down_rows, zero[0:4], below[4] * up_rows], axis=0)
    corner = ((lane < 2) | (lane >= 126)) & ((layer < 2) | (layer >= 6))
    grad_ref[...] = grad
    inside = jnp.where(corner, 0.0, grad)
    rest = jnp.sum(inside * inside, axis=0, keepdims=True)
    corners = pltpu.roll(jnp.where(corner, grad, 0.0), 2, 1, stride=4, stride_axis=0)
    shares = pltpu.roll(jnp.where(corner, missing, 0.0), 34, 1, stride=4, stride_axis=0)
    line = jnp.sum(corners + shares, axis=0, keepdims=True)
    line = jnp.where(lanes_of((1, 128)) < 64, line, rest + pltpu.roll(rest, 64, 1))
    line_ref[...] = jnp.broadcast_to(line[None], line_ref.shape)


def rest_kernel(
    depth,
    cases,
    place_ref,
    loose_ref,
    middle_ref,
    early_ref,
    second_in_ref,
    first_in_ref,
    coef_ref,
    out_ref,
    state_ref,
    sems,
):
    planes = 4 * cases * depth
    half = planes * 4
    copies = [pltpu.make_async_copy(state_ref.at[rows(i * half, half), :], out_ref.at[rows(i * half, half), :], sems.at[i]) for i in range(2)]

    def place_tiles(c, refs):
        def one(case, _):
            for block in range(depth // 8):
                offset = pl.multiple_of((c * cases + case) * depth + 8 * block, 8)
                for row in range(8):
                    if refs[row] is not None:
                        ref, place = row_place(refs[row], row, planes)
                        state_ref[strided(offset * 8 + row), :] = ref[rows(place + offset), :]
            return 0

        lax.fori_loop(0, cases, one, 0)

    both = (middle_ref, early_ref)
    for c in range(2):
        place_tiles(c, [both] * 8)
    copies[0].start()
    for c in range(2, 4):
        place_tiles(c, [both if row in MIDDLE else None for row in range(8)])

    def store(c, case, block, offset, tiles):
        for row, tile in tiles.items():
            state_ref[strided(offset * 8 + row), :] = tile

    arrived = Post(place_ref, first_in_ref, second_in_ref)
    outer_rows(depth, cases, planes, (2, 3), loose_ref, arrived, coef_ref, store)
    copies[1].start()
    copies[0].wait()
    copies[1].wait()


def scale_kernel(cells, devices, trans, place_ref, grad_ref, sums_ref, out_ref, lines_ref):
    pad = -(-trans // 8) * 8
    lane, row = lanes_of((8, 128)), rows_of((8, 128))
    zero = jnp.zeros((pad, 128), jnp.float32)
    lines_ref[rows(0, pad), :] = zero
    lines_ref[rows(pad + devices, pad), :] = zero
    lines_ref[rows(pad, devices), :] = sums_ref[...]
    total, own = jnp.zeros((8, 128), jnp.float32), jnp.zeros((8, 128), jnp.float32)
    device = place_ref[rows(DEVICE * 8), :]
    for block in range(devices // 8):
        here = lines_ref[rows(pad + 8 * block), :]
        below, above = lines_ref[rows(pad - trans + 8 * block), :], lines_ref[rows(pad + trans + 8 * block), :]
        share = pltpu.roll(jnp.where(lane < 48, below, above), 96, 1)
        own += jnp.where(row + 8 * block == device, share, 0.0)
        corner = here + share
        total += jnp.where(lane < 32, corner * corner, jnp.where(lane >= 64, here, 0.0))
    total = jnp.sum(jnp.sum(total, axis=0, keepdims=True), axis=1, keepdims=True)
    own = jnp.broadcast_to(jnp.sum(own, axis=0, keepdims=True), (8, 128))
    grad = grad_ref[...]
    edge = (lane < 2) | (lane >= 126)
    for i in (0, 1, 6, 7):
        grad += jnp.where((row == i) & edge, pltpu.roll(own, (126 - 4 * i) % 128, 1), 0.0)
    out_ref[...] = grad / jnp.sqrt(total / cells + 1e-06)


def f32(*shape):
    return jax.ShapeDtypeStruct(shape, jnp.float32)


def over_tiles(numbers):
    which = rows_of((8 * len(numbers), 128)) // 8
    held = jnp.full(which.shape, numbers[0], jnp.int32)
    for i, number in enumerate(numbers[1:], 1):
        held = jnp.where(which == i, number, held)
    return held


def in_hbm(array):
    return pltpu.with_memory_space_constraint(array, pltpu.HBM)


def call(kernel, *args, outs, scratch=(), hbm=(), out=VM):
    specs = [VM] * len(args)
    for i in hbm:
        specs[i] = HB
    return pl.pallas_call(
        kernel,
        out_shape=outs,
        in_specs=specs,
        out_specs=tuple([out] * len(outs)),
        scratch_shapes=[pltpu.VMEM(shape, jnp.float32) if isinstance(shape, tuple) else shape for shape in scratch],
        compiler_params=PARAMS,
    )(*args)


def neighbours(axis):
    size = lax.axis_size(axis)
    up = [(i, i + 1) for i in range(size - 1)]
    return up, [(j, i) for i, j in up]


def exchange_rows(first, second):
    size = lax.axis_size("roll")
    inner = [(i, i ^ 1) for i in range(size) if i ^ 1 < size]
    outer = [pair for i in range(1, size - 1, 2) for pair in ((i, i + 1), (i + 1, i))]
    second = lax.ppermute(second, "roll", outer)
    return lax.ppermute(first, "roll", inner), second


def exchange_columns(cols):
    ahead, back = neighbours("trans")
    if lax.axis_size("trans") == 2:
        return lax.ppermute(cols, "trans", ahead + back)
    left, right = lax.ppermute(cols, "trans", ahead), lax.ppermute(cols, "trans", back)
    return jnp.where(lanes_of(cols.shape) % 4 < 2, left, right)


def on_device(adjoint, source, pressure, film, cavity, temp_index):
    components, cases, depth, width_x, width_y = adjoint.shape
    planes = components * cases * depth
    assert (components, width_x, width_y, 4 * depth) == (4, 8, 128, 128)
    state = adjoint.reshape(planes * 8, 128)
    forcing = source.reshape(planes * 8, 128)
    roll, trans, trans_size = lax.axis_index("roll"), lax.axis_index("trans"), lax.axis_size("trans")
    place = over_tiles([trans, trans_size, roll % 2, roll * trans_size + trans])
    devices = lax.axis_size("roll") * trans_size
    inner, part = f32(planes * 8, 128), f32(planes * 4 + 2 * PAD, 128)
    message, tailed, cols_shape = f32(planes * 2, 128), f32(planes * 2 + TAIL, 128), f32(components * cases * 8, 128)
    state, first, second = call(
        functools.partial(send_kernel, depth, cases),
        place,
        in_hbm(state),
        outs=(inner, message, message),
        scratch=[pltpu.SemaphoreType.DMA((PIECES,))],
        hbm=(1,),
    )
    primal = (temp_index.reshape(1, cases), pressure.reshape(cases * 8, 128), film, cavity.reshape(cases * 8, 128))
    middle, outer, cols, coef, packed, mask = call(
        functools.partial(pack_kernel, depth, cases),
        state,
        place,
        *map(in_hbm, primal),
        outs=(part, part, cols_shape, f32(cases * N_COEF * 8, 128), f32(cases * N_PACKED * 8, 128), f32(8, 128)),
        scratch=[pltpu.VMEM(array.shape, array.dtype) for array in primal] + [pltpu.SemaphoreType.DMA((4,))],
        hbm=range(2, 6),
    )
    for index in range(SECTIONS):
        more = index < SECTIONS - 1
        first, second = exchange_rows(first, second)
        side = exchange_columns(cols)
        whole, *total = call(
            functools.partial(inner_kernel, depth, cases),
            middle,
            outer,
            forcing,
            coef,
            outs=(inner, f32(cases * 8, 128)) if more else (inner,),
            scratch=[(planes * 8, 256)],
        )
        middle, loose, sums, *corr = call(
            functools.partial(sides_kernel, depth, cases, next_moments if more else wall_sums),
            whole,
            side,
            mask,
            packed,
            outs=(part, part, f32(cases * (5 if more else 2) * 8, 128)) + (() if more else (cols_shape,)),
            scratch=[cols_shape.shape] if more else [],
        )
        if more:
            outer, second, first, moments = call(
                functools.partial(joined_kernel, depth, cases),
                place,
                loose,
                sums,
                *total,
                second,
                first,
                coef,
                outs=(part, tailed, tailed, f32(cases * 3 * 8, 128)),
                scratch=[(cases * 5 * 8, 128)],
            )
            (cols,) = call(functools.partial(columns_kernel, depth, cases), middle, outer, outs=(cols_shape,))
        else:
            early, grad, sums = call(
                functools.partial(final_kernel, depth, cases),
                place,
                loose,
                sums,
                *corr,
                second,
                first,
                coef,
                moments,
                outs=(part, f32(8, 128), pltpu.VMEM((devices, 1, 128), jnp.float32)),
                scratch=[(cases * 2 * 8, 128)],
            )
            (state,) = call(
                functools.partial(rest_kernel, depth, cases),
                place,
                loose,
                middle,
                early,
                second,
                first,
                coef,
                outs=(pltpu.HBM(inner.shape, jnp.float32),),
                scratch=[inner.shape, pltpu.SemaphoreType.DMA((2,))],
                out=HB,
            )
    sums = lax.all_to_all(sums, ("roll", "trans"), 0, 0, tiled=True).reshape(devices, 128)
    pad = -(-trans_size // 8) * 8
    (wall_step,) = call(
        functools.partial(scale_kernel, devices * width_x * width_y, devices, trans_size),
        place,
        grad,
        sums,
        outs=(f32(8, 128),),
        scratch=[(devices + 2 * pad, 128)],
    )
    return (state.reshape(adjoint.shape), wall_step)


def solution(mesh):
    placed = (
        P(None, None, None, "roll", "trans"),
        P(None, None, None, "roll", "trans"),
        P(None, "roll", "trans"),
        P("roll", "trans"),
        P(None, "roll", "trans"),
        P(),
    )
    return jax.shard_map(
        on_device,
        mesh=mesh,
        in_specs=placed,
        out_specs=(P(None, None, None, "roll", "trans"), P("roll", "trans")),
        check_vma=False,
    )
```

```python
import functools

import jax
import jax.numpy as jnp
from jax import lax
from jax.experimental import pallas as pl
from jax.experimental.pallas import tpu as pltpu
from jax.sharding import PartitionSpec as P

SECTIONS = 2


VISCOSITY_PRESS = 0.3
VISCOSITY_TEMP = 0.5
THETA_STEP = 0.2
SOUND = 0.5
KAPPA = 0.6
HEATING = 0.3
ROLL_SPEED = 1.0
COURANT = 0.8

VM = pl.BlockSpec(memory_space=pltpu.VMEM)
HB = pl.BlockSpec(memory_space=pltpu.HBM)
PARAMS = pltpu.CompilerParams(vmem_limit_bytes=16 * 1024 * 1024)

PAD = 8
CENTER, SPREAD, ACROSS = (0, 3, 6)
CARRY, SOUND_STEP, STEP, HEAT, FLUX, BEND = range(9, 15)
N_COEF = 15
N_PACKED = 4
PIECES = 4
TAIL = 24
MIDDLE, OUTER = (2, 3, 4, 5), (0, 1, 6, 7)
TRANS, TRANS_SIZE, ODD, DEVICE = range(4)
WEIGHT = (0, 1, 1, 2)


def lanes_of(shape):
    return lax.broadcasted_iota(jnp.int32, shape, 1)


def rows_of(shape):
    return lax.broadcasted_iota(jnp.int32, shape, 0)


def rows(start, count=8):
    return pl.ds(start, count)


def strided(start):
    return pl.ds(start, 8, stride=8)


def coefficients(depth, cases, place_ref, level_ref, pressure_ref, film_ref, cavity_ref, coef_ref, packed_ref, mask_ref):
    lane, row = lanes_of((8, 128)), rows_of((8, 128))
    film = film_ref[...]
    for case in range(cases):
        theta = THETA_STEP * jnp.broadcast_to(level_ref[:, case : case + 1], (8, 128)).astype(jnp.float32)
        viscosity = jnp.exp(VISCOSITY_PRESS * pressure_ref[rows(case * 8), :] - VISCOSITY_TEMP * theta)
        film_coef = 4.0 * viscosity / (film * film)
        density = 1.0 - 0.6 * cavity_ref[rows(case * 8), :].astype(jnp.float32)
        step = COURANT / (32.0 / 3.0 * viscosity + 4.0 * film_coef + 2.0 * SOUND + 1.0)
        planes = [None] * N_COEF
        for i, weight in enumerate((0.5, 1.0, KAPPA)):
            planes[SPREAD + i] = (weight / 12.0) * step * viscosity
            planes[ACROSS + i] = weight * step * film_coef
            planes[CENTER + i] = 1.0 - 60.0 * planes[SPREAD + i] - 2.0 * planes[ACROSS + i]
        planes[CARRY] = (ROLL_SPEED / 12.0) * step * density
        planes[SOUND_STEP] = (SOUND / 12.0) * step
        planes[STEP] = step
        planes[HEAT] = HEATING * step * viscosity
        planes[FLUX] = (ROLL_SPEED / (24.0 * depth)) * density * film
        planes[BEND] = (8.0 / depth) * viscosity / (film * film * film)
        for i, plane in enumerate(planes):
            coef_ref[rows((case * N_COEF + i) * 8), :] = plane
        wanted = jnp.concatenate(planes[SPREAD : SPREAD + 3] + [planes[SOUND_STEP]], axis=0)
        packed = exact_dot(wanted, edge_columns())
        for i in range(N_PACKED):
            packed_ref[rows((case * N_PACKED + i) * 8), :] = packed[i * 8 : i * 8 + 8]
    trans = place_ref[rows(TRANS * 8), :]
    from_left = jnp.where(trans > 0, 1.0, 0.0)
    from_right = jnp.where(trans < place_ref[rows(TRANS_SIZE * 8), :] - 1, 1.0, 0.0)
    mask_ref[...] = jnp.where(lane % 4 < 2, from_left, from_right)


def edge_columns():
    source = lanes_of((128, 128)) % 4
    source = jnp.where(source < 2, 126 + source, source - 2)
    return jnp.where(rows_of((128, 128)) == source, 1.0, 0.0).astype(jnp.bfloat16)


def in_parts(value):
    high = value.astype(jnp.bfloat16)
    rest = value - high.astype(jnp.float32)
    middle = rest.astype(jnp.bfloat16)
    return jnp.concatenate([high, middle], axis=1), (rest - middle.astype(jnp.float32)).astype(jnp.bfloat16)


def exact_dot(value, weights):
    upper, low = in_parts(value)
    part = jnp.dot(upper, jnp.concatenate([weights, weights], axis=0), preferred_element_type=jnp.float32)
    return part + jnp.dot(low, weights, preferred_element_type=jnp.float32)


class Post:
    def __init__(self, place_ref, first_ref, second_ref):
        self.odd = place_ref[rows(ODD * 8), :] == 1
        self.refs = first_ref, second_ref

    def put(self, where, up, down):
        first, second = self.refs
        odd = self.odd[: where.size]
        first[where, :] = jnp.where(odd, down, up)
        second[where, :] = jnp.where(odd, up, down)

    def get(self, where):
        first, second = (ref[where, :] for ref in self.refs)
        odd = self.odd[: where.size]
        return jnp.where(odd, first, second), jnp.where(odd, second, first)

    def put_tiles(self, planes, first, tiles):
        for i in range(2):
            self.put(rows(i * planes + first), tiles[6 + i], tiles[i])


def row_place(refs, row, planes):
    if row in MIDDLE:
        return refs[0], PAD + MIDDLE.index(row) * planes
    return refs[1], PAD + OUTER.index(row) * planes


def send_kernel(depth, cases, place_ref, state_ref, copy_ref, first_ref, second_ref, sems):
    planes = 4 * cases * depth
    post = Post(place_ref, first_ref, second_ref)

    def piece(i):
        here = rows(i * (planes * 8 // PIECES), planes * 8 // PIECES)
        return pltpu.make_async_copy(state_ref.at[here, :], copy_ref.at[here, :], sems.at[i])

    for i in range(PIECES):
        piece(i).start()
    for i in range(PIECES):
        piece(i).wait()
        for first in range(i * planes // PIECES, (i + 1) * planes // PIECES, 8):
            post.put_tiles(planes, first, {row: copy_ref[strided(first * 8 + row), :] for row in (0, 1, 6, 7)})


def pack_kernel(depth, cases, state_ref, cols_ref):
    lane = lanes_of((8, 128))

    def one(pair, _):
        held = jnp.zeros((8, 128), jnp.float32)
        for layer in range(depth):
            group = depth - 1 - layer
            plane = state_ref[rows(pl.multiple_of((pair * depth + layer) * 8, 8)), :]
            held = jnp.where(lane // 4 == group, pltpu.roll(plane, (4 * group + 2) % 128, 1), held)
        cols_ref[rows(pl.multiple_of(pair * 8, 8)), :] = held
        return 0

    lax.fori_loop(0, 4 * cases, one, 0, unroll=4)


def tile_kernel(depth, cases, state_ref, place_ref, *rest):
    planes = 4 * cases * depth
    (middle_ref, outer_ref), outs, held, sems = rest[4:6], rest[6:9], rest[9:13], rest[13]
    copies = [pltpu.make_async_copy(rest[i], held[i], sems.at[i]) for i in range(4)]
    for copy in copies:
        copy.start()

    def one(pair, _):
        for row in range(8):
            ref, place = row_place((middle_ref, outer_ref), row, planes)
            for block in range(depth // 8):
                first = pl.multiple_of(pair * depth + 8 * block, 8)
                ref[rows(place + first), :] = state_ref[strided(first * 8 + row), :]
        return 0

    lax.fori_loop(0, 4 * cases, one, 0)
    for copy in copies:
        copy.wait()
    coefficients(depth, cases, place_ref, *held, *outs)


def columns_kernel(depth, cases, middle_ref, outer_ref, cols_ref):
    planes = 4 * cases * depth
    columns = edge_columns()
    mine = lanes_of((depth, 128)) // 4 == (depth - 1) - rows_of((depth, 128))
    for row in range(8):
        ref, place = row_place((middle_ref, outer_ref), row, planes)
        edges = exact_dot(ref[rows(place, planes), :], columns)
        for pair in range(4 * cases):
            kept = jnp.where(mine, edges[pair * depth : (pair + 1) * depth], 0.0)
            cols_ref[pl.ds(pair * 8 + row, 1), :] = jnp.sum(kept, axis=0, keepdims=True)


def inner_kernel(depth, cases, middle_ref, outer_ref, source_ref, coef_ref, *rest):
    out_ref, *more_refs, deriv_ref = rest
    planes = 4 * cases * depth
    lane, layer = lanes_of((8, 128)), rows_of((8, 128))
    gap = rows_of((128, 256)) - lanes_of((128, 256)) % 128
    second = jnp.where(jnp.abs(gap) == 1, 16.0, jnp.where(jnp.abs(gap) == 2, -1.0, 0.0))
    first = jnp.where(gap == 1, 8.0, jnp.where(gap == -1, -8.0, jnp.where(gap == 2, -1.0, jnp.where(gap == -2, 1.0, 0.0))))
    weights = jnp.where(lanes_of((128, 256)) < 128, second, first).astype(jnp.bfloat16)
    for row in range(8):
        ref, place = row_place((middle_ref, outer_ref), row, planes)
        value = ref[rows(place, planes), :]
        deriv_ref[rows(row * planes, planes), :] = exact_dot(value, weights)

    def one(index, _):
        case, block = index // (depth // 8), index % (depth // 8)
        k = layer + 8 * block
        height = (k.astype(jnp.float32) + 0.5) / depth
        offsets = [pl.multiple_of((c * cases + case) * depth + 8 * block, 8) for c in range(4)]
        places = [row_place((middle_ref, outer_ref), row, planes) for row in range(8)]
        tiles = [[ref[rows(place + offsets[c]), :] for ref, place in places] for c in range(4)]

        for row in range(8):

            def coef(i):
                return coef_ref[pl.ds((case * N_COEF + i) * 8 + row, 1), :]

            along = []
            for c in range(4):
                near = [tiles[c][row + by] if 0 <= row + by < 8 else None for by in (-2, -1, 1, 2)]
                along.append(near)

            def first_x(c):
                m2, m1, p1, p2 = along[c]
                ones = 8.0 * (p1 - m1) if m1 is not None and p1 is not None else 8.0 * p1 if m1 is None else -8.0 * m1
                if m2 is not None and p2 is not None:
                    return ones - (p2 - m2)
                return ones - p2 if m2 is None else ones + m2

            def second_x(c):
                m2, m1, p1, p2 = along[c]
                ones = 16.0 * (p1 + m1) if m1 is not None and p1 is not None else 16.0 * (p1 if m1 is None else m1)
                if m2 is not None and p2 is not None:
                    return ones - (p2 + m2)
                return ones - (p2 if m2 is None else m2)

            carry = coef(CARRY) * height
            sound = coef(SOUND_STEP)
            step = coef(STEP)
            slopes = [first_x(c) for c in range(4)]
            for c in range(4):
                here = row * planes + offsets[c]
                ref, place = places[row]
                behind = jnp.where(k > 0, ref[rows(place + offsets[c] - 1), :], 0.0)
                beyond = jnp.where(k < depth - 1, ref[rows(place + offsets[c] + 1), :], 0.0)
                source = source_ref[strided(offsets[c] * 8 + row), :]
                w = WEIGHT[c]
                value = coef(CENTER + w) * tiles[c][row] + coef(SPREAD + w) * (second_x(c) + deriv_ref[rows(here), 0:128])
                value += coef(ACROSS + w) * (behind + beyond) + step * source + carry * slopes[c]
                if c == 0:
                    other = row * planes + offsets[2]
                    value += sound * (slopes[1] + deriv_ref[rows(other), 128:256])
                elif c == 1:
                    value += sound * slopes[0]
                elif c == 2:
                    other = row * planes + offsets[0]
                    value += sound * deriv_ref[rows(other), 128:256]
                else:
                    value += coef(HEAT) * tiles[1][row]
                out_ref[rows(here), :] = value
        return 0

    lax.fori_loop(0, cases * (depth // 8), one, 0)

    if more_refs:
        (total_ref,) = more_refs
        for case in range(cases):
            for row in range(8):
                total = jnp.zeros((8, 128), jnp.float32)
                for block in range(depth // 8):
                    total += source_ref[strided((case * depth + 8 * block) * 8 + row), :]
                total_ref[pl.ds(case * 8 + row, 1), :] = jnp.sum(total, axis=0, keepdims=True)


def columns_beyond(cases, side_ref, mask_ref, packed_ref, corr_ref):
    slot = lanes_of((8, 128)) % 4
    for case in range(cases):
        coefs = [packed_ref[rows((case * N_PACKED + i) * 8), :] for i in range(N_PACKED)]
        second, first = [], []
        for c in range(4):
            side = side_ref[rows((c * cases + case) * 8), :] * mask_ref[...]
            p1 = jnp.where(slot == 1, pltpu.roll(side, 127, 1), 0.0)
            p2 = jnp.where(slot < 2, pltpu.roll(side, 126, 1), 0.0)
            m1 = jnp.where(slot == 2, pltpu.roll(side, 1, 1), 0.0)
            m2 = jnp.where(slot >= 2, pltpu.roll(side, 2, 1), 0.0)
            second.append(16.0 * (p1 + m1) - (p2 + m2))
            first.append(8.0 * (p1 - m1) - (p2 - m2))
        for c in range(4):
            value = coefs[WEIGHT[c]] * second[c]
            if c == 0:
                value += coefs[3] * first[2]
            elif c == 2:
                value += coefs[3] * first[0]
            corr_ref[rows((c * cases + case) * 8), :] = value


def depth_sum(tiles):
    total = tiles[0]
    for tile in tiles[1:]:
        total = total + tile
    return jnp.sum(total, axis=0, keepdims=True)


def next_moments(depth, tiles_of, layer):
    density = tiles_of(0)
    heights = [(layer + (8 * block + 0.5)).astype(jnp.float32) / depth for block in range(depth // 8)]
    return (
        depth_sum(density),
        depth_sum([tile * height for tile, height in zip(density, heights, strict=True)]),
        depth_sum(tiles_of(1)),
        depth_sum(tiles_of(2)),
        density[0][0:1] + density[-1][7:8],
    )


def wall_sums(depth, tiles_of, layer):
    momentum, before = tiles_of(1), tiles_of(1, -1)
    changes = [momentum[0] - jnp.where(layer > 0, before[0], 0.0)]
    changes += [here - there for here, there in zip(momentum[1:], before[1:], strict=True)]
    squares = [change * change for change in changes] + [jnp.where(layer == 7, momentum[-1] * momentum[-1], 0.0)]
    return depth_sum(tiles_of(0)), depth_sum(squares)


def line_sums(depth, cases, planes, sums, ref, which, out_ref, layer):
    for case in range(cases):
        for i, row in enumerate(which):

            def tiles_of(c, by=0):
                start = PAD + i * planes + (c * cases + case) * depth
                return [ref[rows(start + by + 8 * block), :] for block in range(depth // 8)]

            lines = sums(depth, tiles_of, layer)
            for n, line in enumerate(lines):
                out_ref[pl.ds((case * len(lines) + n) * 8 + row, 1), :] = line


def joined_sums(middle_ref, outer_ref, index, layer):
    return jnp.where((layer >= 2) & (layer < 6), middle_ref[rows(index * 8), :], outer_ref[rows(index * 8), :])


def sides_kernel(depth, cases, sums, inner_ref, side_ref, mask_ref, packed_ref, middle_ref, loose_ref, sums_ref, corr_ref):
    planes = 4 * cases * depth
    lane, layer = lanes_of((8, 128)), rows_of((8, 128))
    edge = (lane < 2) | (lane >= 126)
    columns_beyond(cases, side_ref, mask_ref, packed_ref, corr_ref)

    def one(case, _):
        for row in range(8):
            for c in range(4):
                line = jnp.broadcast_to(corr_ref[pl.ds((c * cases + case) * 8 + row, 1), :], (8, 128))
                for block in range(depth // 8):
                    offset = pl.multiple_of((c * cases + case) * depth + 8 * block, 8)
                    moved = pltpu.roll(line, 2 + 32 * block, 1, stride=4, stride_axis=0)
                    value = inner_ref[rows(row * planes + offset), :] + jnp.where(edge, moved, 0.0)
                    ref, place = row_place((middle_ref, loose_ref), row, planes)
                    ref[rows(place + offset), :] = value
        return 0

    lax.fori_loop(0, cases, one, 0)
    line_sums(depth, cases, planes, sums, middle_ref, MIDDLE, sums_ref, layer)


def outer_rows(depth, cases, planes, parts, loose_ref, post, coef_ref, store):
    layer = rows_of((8, 128))

    def one(case, _):
        for block in range(depth // 8):
            height = ((layer + 8 * block).astype(jnp.float32) + 0.5) / depth
            offsets = [pl.multiple_of((c * cases + case) * depth + 8 * block, 8) for c in range(4)]
            near = {c: [post.get(rows(i * planes + offsets[c])) for i in range(2)] for c in {*parts, *range(2)}}
            whole = {c: {} for c in parts}
            for i, row in enumerate(OUTER):

                def coef(n):
                    return coef_ref[pl.ds((case * N_COEF + n) * 8 + row, 1), :]

                second, first = {}, {}
                for c, ((m2, p1), (m1, p2)) in near.items():
                    if row == 0:
                        second[c], first[c] = 16.0 * m1 - m2, m2 - 8.0 * m1
                    elif row == 1:
                        second[c], first[c] = -m1, m1
                    elif row == 6:
                        second[c], first[c] = -p1, -p1
                    else:
                        second[c], first[c] = 16.0 * p1 - p2, 8.0 * p1 - p2
                for c in parts:
                    value = loose_ref[rows(PAD + i * planes + offsets[c]), :]
                    value += coef(SPREAD + WEIGHT[c]) * second[c] + coef(CARRY) * height * first[c]
                    if c < 2:
                        value += coef(SOUND_STEP) * first[1 - c]
                    whole[c][row] = value
            for c in parts:
                store(c, case, block, offsets[c], whole[c])
        return 0

    lax.fori_loop(0, cases, one, 0)


def joined_kernel(
    depth,
    cases,
    place_ref,
    loose_ref,
    middle_sums_ref,
    source_total_ref,
    second_in_ref,
    first_in_ref,
    coef_ref,
    outer_ref,
    second_ref,
    first_ref,
    moment_ref,
    outer_sums_ref,
):
    planes = 4 * cases * depth
    lane, layer = lanes_of((8, 128)), rows_of((8, 128))
    post, arrived = Post(place_ref, first_ref, second_ref), Post(place_ref, first_in_ref, second_in_ref)

    def store(c, case, block, offset, tiles):
        for i, row in enumerate(OUTER):
            outer_ref[rows(PAD + i * planes + offset), :] = tiles[row]
        post.put_tiles(planes, offset, tiles)

    outer_rows(depth, cases, planes, range(4), loose_ref, arrived, coef_ref, store)

    line_sums(depth, cases, planes, next_moments, outer_ref, OUTER, outer_sums_ref, layer)
    for case in range(cases):

        def coef(i):
            return coef_ref[rows((case * N_COEF + i) * 8), :]

        moments = [joined_sums(middle_sums_ref, outer_sums_ref, case * 5 + i, layer) for i in range(5)]
        total, lifted, along, across, walls = moments
        for i in range(3):
            moment_ref[rows((case * 3 + i) * 8), :] = moments[i]

        def x_parts(plane):
            m1, m2 = jnp.where(layer >= 1, pltpu.roll(plane, 1, 0), 0.0), jnp.where(layer >= 2, pltpu.roll(plane, 2, 0), 0.0)
            p1, p2 = jnp.where(layer < 7, pltpu.roll(plane, 7, 0), 0.0), jnp.where(layer < 6, pltpu.roll(plane, 6, 0), 0.0)
            return 16.0 * (p1 + m1) - (p2 + m2), 8.0 * (p1 - m1) - (p2 - m2)

        def y_parts(plane):
            m1, m2 = jnp.where(lane >= 1, pltpu.roll(plane, 1, 1), 0.0), jnp.where(lane >= 2, pltpu.roll(plane, 2, 1), 0.0)
            p1, p2 = jnp.where(lane < 127, pltpu.roll(plane, 127, 1), 0.0), jnp.where(lane < 126, pltpu.roll(plane, 126, 1), 0.0)
            return 16.0 * (p1 + m1) - (p2 + m2), 8.0 * (p1 - m1) - (p2 - m2)

        value = coef(CENTER) * total + coef(SPREAD) * (x_parts(total)[0] + y_parts(total)[0])
        value += coef(ACROSS) * (2.0 * total - walls) + coef(CARRY) * x_parts(lifted)[1]
        value += coef(SOUND_STEP) * (x_parts(along)[1] + y_parts(across)[1]) + coef(STEP) * source_total_ref[rows(case * 8), :]
        sent = (value, coef(SPREAD), coef(CARRY), coef(SOUND_STEP), coef(FLUX))
        for i, plane in enumerate(sent):
            post.put(pl.ds(2 * planes + (case * 5 + i) * 2, 2), plane[6:8], plane[0:2])


def edge_sums(tile):
    for by in (4, 8, 16, 32, 64):
        tile = tile + pltpu.roll(tile, by, 1)
    return pltpu.roll(tile, 2, 1)


def final_kernel(
    depth,
    cases,
    place_ref,
    loose_ref,
    middle_sums_ref,
    corr_ref,
    second_in_ref,
    first_in_ref,
    coef_ref,
    moment_ref,
    outer_ref,
    grad_ref,
    line_ref,
    outer_sums_ref,
):
    planes = 4 * cases * depth
    lane, layer = lanes_of((8, 128)), rows_of((8, 128))
    arrived = Post(place_ref, first_in_ref, second_in_ref)

    def store(c, case, block, offset, tiles):
        for i, row in enumerate(OUTER):
            outer_ref[rows(PAD + i * planes + offset), :] = tiles[row]

    outer_rows(depth, cases, planes, range(2), loose_ref, arrived, coef_ref, store)
    line_sums(depth, cases, planes, wall_sums, outer_ref, OUTER, outer_sums_ref, layer)

    zero = jnp.zeros((8, 128), jnp.float32)
    grad, missing = zero, zero
    for case in range(cases):

        def coef(i):
            return coef_ref[rows((case * N_COEF + i) * 8), :]

        pairs = [arrived.get(pl.ds(2 * planes + (case * 5 + i) * 2, 2)) for i in range(5)]
        below, above = [pair[0] for pair in pairs], [pair[1] for pair in pairs]
        total, lifted, along = (moment_ref[rows((case * 3 + i) * 8), :] for i in range(3))

        def beyond(plane):
            first, second, last, before = plane[0:1], plane[1:2], plane[7:8], plane[6:7]
            down = (jnp.concatenate([-first, 16.0 * first - second], 0), jnp.concatenate([-first, 8.0 * first - second], 0))
            up = (jnp.concatenate([16.0 * last - before, -last], 0), jnp.concatenate([before - 8.0 * last, last], 0))
            return down, up

        down, up = zip(beyond(total), beyond(lifted), beyond(along), strict=True)
        mean_below = below[0] + below[1] * down[0][0] + below[2] * down[1][1] + below[3] * down[2][1]
        mean_above = above[0] + above[1] * up[0][0] + above[2] * up[1][1] + above[3] * up[2][1]
        mean, bend = (joined_sums(middle_sums_ref, outer_sums_ref, case * 2 + i, layer) for i in range(2))
        halo = jnp.concatenate([mean_above, zero[0:4], mean_below], axis=0)
        m1 = pltpu.roll(jnp.where(layer == 7, halo, mean), 1, 0)
        m2 = pltpu.roll(jnp.where(layer >= 6, halo, mean), 2, 0)
        p1 = pltpu.roll(jnp.where(layer == 0, halo, mean), 7, 0)
        p2 = pltpu.roll(jnp.where(layer < 2, halo, mean), 6, 0)
        grad += coef(FLUX) * (8.0 * (p1 - m1) - (p2 - m2)) + coef(BEND) * bend
        change = edge_sums(corr_ref[rows(case * 8), :])
        down_rows = jnp.concatenate([change[6:7] - 8.0 * change[7:8], change[7:8]], axis=0)
        up_rows = jnp.concatenate([-change[0:1], 8.0 * change[0:1] - change[1:2]], axis=0)
        missing += jnp.concatenate([above[4] * down_rows, zero[0:4], below[4] * up_rows], axis=0)
    corner = ((lane < 2) | (lane >= 126)) & ((layer < 2) | (layer >= 6))
    grad_ref[...] = grad
    inside = jnp.where(corner, 0.0, grad)
    rest = jnp.sum(inside * inside, axis=0, keepdims=True)
    corners = pltpu.roll(jnp.where(corner, grad, 0.0), 2, 1, stride=4, stride_axis=0)
    shares = pltpu.roll(jnp.where(corner, missing, 0.0), 34, 1, stride=4, stride_axis=0)
    line = jnp.sum(corners + shares, axis=0, keepdims=True)
    line = jnp.where(lanes_of((1, 128)) < 64, line, rest + pltpu.roll(rest, 64, 1))
    line_ref[...] = jnp.broadcast_to(line[None], line_ref.shape)


def rest_kernel(
    depth,
    cases,
    place_ref,
    loose_ref,
    middle_ref,
    early_ref,
    second_in_ref,
    first_in_ref,
    coef_ref,
    out_ref,
    state_ref,
    sems,
):
    planes = 4 * cases * depth
    half = planes * 4
    copies = [pltpu.make_async_copy(state_ref.at[rows(i * half, half), :], out_ref.at[rows(i * half, half), :], sems.at[i]) for i in range(2)]

    def place_tiles(c, refs):
        def one(case, _):
            for block in range(depth // 8):
                offset = pl.multiple_of((c * cases + case) * depth + 8 * block, 8)
                for row in range(8):
                    if refs[row] is not None:
                        ref, place = row_place(refs[row], row, planes)
                        state_ref[strided(offset * 8 + row), :] = ref[rows(place + offset), :]
            return 0

        lax.fori_loop(0, cases, one, 0)

    both = (middle_ref, early_ref)
    for c in range(2):
        place_tiles(c, [both] * 8)
    copies[0].start()
    for c in range(2, 4):
        place_tiles(c, [both if row in MIDDLE else None for row in range(8)])

    def store(c, case, block, offset, tiles):
        for row, tile in tiles.items():
            state_ref[strided(offset * 8 + row), :] = tile

    arrived = Post(place_ref, first_in_ref, second_in_ref)
    outer_rows(depth, cases, planes, (2, 3), loose_ref, arrived, coef_ref, store)
    copies[1].start()
    copies[0].wait()
    copies[1].wait()


def scale_kernel(cells, devices, trans, place_ref, grad_ref, sums_ref, out_ref, lines_ref):
    pad = -(-trans // 8) * 8
    lane, row = lanes_of((8, 128)), rows_of((8, 128))
    zero = jnp.zeros((pad, 128), jnp.float32)
    lines_ref[rows(0, pad), :] = zero
    lines_ref[rows(pad + devices, pad), :] = zero
    lines_ref[rows(pad, devices), :] = sums_ref[...]
    total, own = jnp.zeros((8, 128), jnp.float32), jnp.zeros((8, 128), jnp.float32)
    device = place_ref[rows(DEVICE * 8), :]
    for block in range(devices // 8):
        here = lines_ref[rows(pad + 8 * block), :]
        below, above = lines_ref[rows(pad - trans + 8 * block), :], lines_ref[rows(pad + trans + 8 * block), :]
        share = pltpu.roll(jnp.where(lane < 48, below, above), 96, 1)
        own += jnp.where(row + 8 * block == device, share, 0.0)
        corner = here + share
        total += jnp.where(lane < 32, corner * corner, jnp.where(lane >= 64, here, 0.0))
    total = jnp.sum(jnp.sum(total, axis=0, keepdims=True), axis=1, keepdims=True)
    own = jnp.broadcast_to(jnp.sum(own, axis=0, keepdims=True), (8, 128))
    grad = grad_ref[...]
    edge = (lane < 2) | (lane >= 126)
    for i in (0, 1, 6, 7):
        grad += jnp.where((row == i) & edge, pltpu.roll(own, (126 - 4 * i) % 128, 1), 0.0)
    out_ref[...] = grad / jnp.sqrt(total / cells + 1e-06)


def f32(*shape):
    return jax.ShapeDtypeStruct(shape, jnp.float32)


def over_tiles(numbers):
    which = rows_of((8 * len(numbers), 128)) // 8
    held = jnp.full(which.shape, numbers[0], jnp.int32)
    for i, number in enumerate(numbers[1:], 1):
        held = jnp.where(which == i, number, held)
    return held


def in_hbm(array):
    return pltpu.with_memory_space_constraint(array, pltpu.HBM)


def call(kernel, *args, outs, scratch=(), hbm=(), out=VM):
    specs = [VM] * len(args)
    for i in hbm:
        specs[i] = HB
    return pl.pallas_call(
        kernel,
        out_shape=outs,
        in_specs=specs,
        out_specs=tuple([out] * len(outs)),
        scratch_shapes=[pltpu.VMEM(shape, jnp.float32) if isinstance(shape, tuple) else shape for shape in scratch],
        compiler_params=PARAMS,
    )(*args)


def neighbours(axis):
    size = lax.axis_size(axis)
    up = [(i, i + 1) for i in range(size - 1)]
    return up, [(j, i) for i, j in up]


def exchange_rows(first, second):
    size = lax.axis_size("roll")
    inner = [(i, i ^ 1) for i in range(size) if i ^ 1 < size]
    outer = [pair for i in range(1, size - 1, 2) for pair in ((i, i + 1), (i + 1, i))]
    second = lax.ppermute(second, "roll", outer)
    return lax.ppermute(first, "roll", inner), second


def exchange_columns(cols):
    ahead, back = neighbours("trans")
    if lax.axis_size("trans") == 2:
        return lax.ppermute(cols, "trans", ahead + back)
    left, right = lax.ppermute(cols, "trans", ahead), lax.ppermute(cols, "trans", back)
    return jnp.where(lanes_of(cols.shape) % 4 < 2, left, right)


def on_device(adjoint, source, pressure, film, cavity, temp_index):
    components, cases, depth, width_x, width_y = adjoint.shape
    planes = components * cases * depth
    assert (components, width_x, width_y, 4 * depth) == (4, 8, 128, 128)
    state = adjoint.reshape(planes * 8, 128)
    forcing = source.reshape(planes * 8, 128)
    roll, trans, trans_size = lax.axis_index("roll"), lax.axis_index("trans"), lax.axis_size("trans")
    place = over_tiles([trans, trans_size, roll % 2, roll * trans_size + trans])
    devices = lax.axis_size("roll") * trans_size
    inner, part = f32(planes * 8, 128), f32(planes * 4 + 2 * PAD, 128)
    message, tailed, cols_shape = f32(planes * 2, 128), f32(planes * 2 + TAIL, 128), f32(components * cases * 8, 128)
    state, first, second = call(
        functools.partial(send_kernel, depth, cases),
        place,
        in_hbm(state),
        outs=(inner, message, message),
        scratch=[pltpu.SemaphoreType.DMA((PIECES,))],
        hbm=(1,),
    )
    primal = (temp_index.reshape(1, cases), pressure.reshape(cases * 8, 128), film, cavity.reshape(cases * 8, 128))
    (cols,) = call(functools.partial(pack_kernel, depth, cases), state, outs=(cols_shape,))
    middle, outer, coef, packed, mask = call(
        functools.partial(tile_kernel, depth, cases),
        state,
        place,
        *map(in_hbm, primal),
        outs=(part, part, f32(cases * N_COEF * 8, 128), f32(cases * N_PACKED * 8, 128), f32(8, 128)),
        scratch=[pltpu.VMEM(array.shape, array.dtype) for array in primal] + [pltpu.SemaphoreType.DMA((4,))],
        hbm=range(2, 6),
    )
    for index in range(SECTIONS):
        more = index < SECTIONS - 1
        first, second = exchange_rows(first, second)
        side = exchange_columns(cols)
        whole, *total = call(
            functools.partial(inner_kernel, depth, cases),
            middle,
            outer,
            forcing,
            coef,
            outs=(inner, f32(cases * 8, 128)) if more else (inner,),
            scratch=[(planes * 8, 256)],
        )
        middle, loose, sums, *corr = call(
            functools.partial(sides_kernel, depth, cases, next_moments if more else wall_sums),
            whole,
            side,
            mask,
            packed,
            outs=(part, part, f32(cases * (5 if more else 2) * 8, 128)) + (() if more else (cols_shape,)),
            scratch=[cols_shape.shape] if more else [],
        )
        if more:
            outer, second, first, moments = call(
                functools.partial(joined_kernel, depth, cases),
                place,
                loose,
                sums,
                *total,
                second,
                first,
                coef,
                outs=(part, tailed, tailed, f32(cases * 3 * 8, 128)),
                scratch=[(cases * 5 * 8, 128)],
            )
            (cols,) = call(functools.partial(columns_kernel, depth, cases), middle, outer, outs=(cols_shape,))
        else:
            early, grad, sums = call(
                functools.partial(final_kernel, depth, cases),
                place,
                loose,
                sums,
                *corr,
                second,
                first,
                coef,
                moments,
                outs=(part, f32(8, 128), pltpu.VMEM((devices, 1, 128), jnp.float32)),
                scratch=[(cases * 2 * 8, 128)],
            )
            (state,) = call(
                functools.partial(rest_kernel, depth, cases),
                place,
                loose,
                middle,
                early,
                second,
                first,
                coef,
                outs=(pltpu.HBM(inner.shape, jnp.float32),),
                scratch=[inner.shape, pltpu.SemaphoreType.DMA((2,))],
                out=HB,
            )
    sums = lax.all_to_all(sums, ("roll", "trans"), 0, 0, tiled=True).reshape(devices, 128)
    pad = -(-trans_size // 8) * 8
    (wall_step,) = call(
        functools.partial(scale_kernel, devices * width_x * width_y, devices, trans_size),
        place,
        grad,
        sums,
        outs=(f32(8, 128),),
        scratch=[(devices + 2 * pad, 128)],
    )
    return (state.reshape(adjoint.shape), wall_step)


def solution(mesh):
    placed = (
        P(None, None, None, "roll", "trans"),
        P(None, None, None, "roll", "trans"),
        P(None, "roll", "trans"),
        P("roll", "trans"),
        P(None, "roll", "trans"),
        P(),
    )
    return jax.shard_map(
        on_device,
        mesh=mesh,
        in_specs=placed,
        out_specs=(P(None, None, None, "roll", "trans"), P("roll", "trans")),
        check_vma=False,
    )
```

```python
import functools

import jax
import jax.numpy as jnp
from jax import lax
from jax.experimental import pallas as pl
from jax.experimental.pallas import tpu as pltpu
from jax.sharding import PartitionSpec as P

SECTIONS = 2


VISCOSITY_PRESS = 0.3
VISCOSITY_TEMP = 0.5
THETA_STEP = 0.2
SOUND = 0.5
KAPPA = 0.6
HEATING = 0.3
ROLL_SPEED = 1.0
COURANT = 0.8

VM = pl.BlockSpec(memory_space=pltpu.VMEM)
HB = pl.BlockSpec(memory_space=pltpu.HBM)
PARAMS = pltpu.CompilerParams(vmem_limit_bytes=16 * 1024 * 1024)

PAD = 8
CENTER, SPREAD, ACROSS = (0, 3, 6)
CARRY, SOUND_STEP, STEP, HEAT, FLUX, BEND = range(9, 15)
N_COEF = 15
N_PACKED = 4
PIECES = 4
TAIL = 24
MIDDLE, OUTER = (2, 3, 4, 5), (0, 1, 6, 7)
TRANS, TRANS_SIZE, ODD, DEVICE = range(4)
WEIGHT = (0, 1, 1, 2)


def lanes_of(shape):
    return lax.broadcasted_iota(jnp.int32, shape, 1)


def rows_of(shape):
    return lax.broadcasted_iota(jnp.int32, shape, 0)


def rows(start, count=8):
    return pl.ds(start, count)


def strided(start):
    return pl.ds(start, 8, stride=8)


def coefficients(depth, cases, place_ref, level_ref, pressure_ref, film_ref, cavity_ref, coef_ref, packed_ref, mask_ref):
    lane, row = lanes_of((8, 128)), rows_of((8, 128))
    film = film_ref[...]
    for case in range(cases):
        theta = THETA_STEP * jnp.broadcast_to(level_ref[:, case : case + 1], (8, 128)).astype(jnp.float32)
        viscosity = jnp.exp(VISCOSITY_PRESS * pressure_ref[rows(case * 8), :] - VISCOSITY_TEMP * theta)
        film_coef = 4.0 * viscosity / (film * film)
        density = 1.0 - 0.6 * cavity_ref[rows(case * 8), :].astype(jnp.float32)
        step = COURANT / (32.0 / 3.0 * viscosity + 4.0 * film_coef + 2.0 * SOUND + 1.0)
        planes = [None] * N_COEF
        for i, weight in enumerate((0.5, 1.0, KAPPA)):
            planes[SPREAD + i] = (weight / 12.0) * step * viscosity
            planes[ACROSS + i] = weight * step * film_coef
            planes[CENTER + i] = 1.0 - 60.0 * planes[SPREAD + i] - 2.0 * planes[ACROSS + i]
        planes[CARRY] = (ROLL_SPEED / 12.0) * step * density
        planes[SOUND_STEP] = (SOUND / 12.0) * step
        planes[STEP] = step
        planes[HEAT] = HEATING * step * viscosity
        planes[FLUX] = (ROLL_SPEED / (24.0 * depth)) * density * film
        planes[BEND] = (8.0 / depth) * viscosity / (film * film * film)
        for i, plane in enumerate(planes):
            coef_ref[rows((case * N_COEF + i) * 8), :] = plane
        wanted = jnp.concatenate(planes[SPREAD : SPREAD + 3] + [planes[SOUND_STEP]], axis=0)
        packed = exact_dot(wanted, edge_columns())
        for i in range(N_PACKED):
            packed_ref[rows((case * N_PACKED + i) * 8), :] = packed[i * 8 : i * 8 + 8]
    trans = place_ref[rows(TRANS * 8), :]
    from_left = jnp.where(trans > 0, 1.0, 0.0)
    from_right = jnp.where(trans < place_ref[rows(TRANS_SIZE * 8), :] - 1, 1.0, 0.0)
    mask_ref[...] = jnp.where(lane % 4 < 2, from_left, from_right)


def edge_columns():
    source = lanes_of((128, 128)) % 4
    source = jnp.where(source < 2, 126 + source, source - 2)
    return jnp.where(rows_of((128, 128)) == source, 1.0, 0.0).astype(jnp.bfloat16)


def in_parts(value):
    high = value.astype(jnp.bfloat16)
    rest = value - high.astype(jnp.float32)
    middle = rest.astype(jnp.bfloat16)
    return jnp.concatenate([high, middle], axis=1), (rest - middle.astype(jnp.float32)).astype(jnp.bfloat16)


def exact_dot(value, weights):
    upper, low = in_parts(value)
    part = jnp.dot(upper, jnp.concatenate([weights, weights], axis=0), preferred_element_type=jnp.float32)
    return part + jnp.dot(low, weights, preferred_element_type=jnp.float32)


class Post:
    def __init__(self, place_ref, first_ref, second_ref):
        self.odd = place_ref[rows(ODD * 8), :] == 1
        self.refs = first_ref, second_ref

    def put(self, where, up, down):
        first, second = self.refs
        odd = self.odd[: where.size]
        first[where, :] = jnp.where(odd, down, up)
        second[where, :] = jnp.where(odd, up, down)

    def get(self, where):
        first, second = (ref[where, :] for ref in self.refs)
        odd = self.odd[: where.size]
        return jnp.where(odd, first, second), jnp.where(odd, second, first)

    def put_tiles(self, planes, first, tiles):
        for i in range(2):
            self.put(rows(i * planes + first), tiles[6 + i], tiles[i])


def row_place(refs, row, planes):
    if row in MIDDLE:
        return refs[0], PAD + MIDDLE.index(row) * planes
    return refs[1], PAD + OUTER.index(row) * planes


def send_kernel(depth, cases, place_ref, state_ref, copy_ref, first_ref, second_ref, sems):
    planes = 4 * cases * depth
    post = Post(place_ref, first_ref, second_ref)

    def piece(i):
        here = rows(i * (planes * 8 // PIECES), planes * 8 // PIECES)
        return pltpu.make_async_copy(state_ref.at[here, :], copy_ref.at[here, :], sems.at[i])

    for i in range(PIECES):
        piece(i).start()
    for i in range(PIECES):
        piece(i).wait()
        for first in range(i * planes // PIECES, (i + 1) * planes // PIECES, 8):
            post.put_tiles(planes, first, {row: copy_ref[strided(first * 8 + row), :] for row in (0, 1, 6, 7)})


def pack_kernel(depth, cases, state_ref, cols_ref):
    lane = lanes_of((8, 128))

    def one(pair, _):
        held = jnp.zeros((8, 128), jnp.float32)
        for layer in range(depth):
            group = depth - 1 - layer
            plane = state_ref[rows(pl.multiple_of((pair * depth + layer) * 8, 8)), :]
            held = jnp.where(lane // 4 == group, pltpu.roll(plane, (4 * group + 2) % 128, 1), held)
        cols_ref[rows(pl.multiple_of(pair * 8, 8)), :] = held
        return 0

    lax.fori_loop(0, 4 * cases, one, 0, unroll=4)


def tile_kernel(depth, cases, state_ref, place_ref, *rest):
    planes = 4 * cases * depth
    (middle_ref, outer_ref), outs, held, sems = rest[4:6], rest[6:9], rest[9:13], rest[13]
    copies = [pltpu.make_async_copy(rest[i], held[i], sems.at[i]) for i in range(4)]
    for copy in copies:
        copy.start()

    def one(pair, _):
        for row in range(8):
            ref, place = row_place((middle_ref, outer_ref), row, planes)
            for block in range(depth // 8):
                first = pl.multiple_of(pair * depth + 8 * block, 8)
                ref[rows(place + first), :] = state_ref[strided(first * 8 + row), :]
        return 0

    lax.fori_loop(0, 4 * cases, one, 0)
    for copy in copies:
        copy.wait()
    coefficients(depth, cases, place_ref, *held, *outs)


def columns_kernel(depth, cases, middle_ref, outer_ref, cols_ref):
    planes = 4 * cases * depth
    columns = edge_columns()
    mine = lanes_of((depth, 128)) // 4 == (depth - 1) - rows_of((depth, 128))
    for row in range(8):
        ref, place = row_place((middle_ref, outer_ref), row, planes)
        edges = exact_dot(ref[rows(place, planes), :], columns)
        for pair in range(4 * cases):
            kept = jnp.where(mine, edges[pair * depth : (pair + 1) * depth], 0.0)
            cols_ref[pl.ds(pair * 8 + row, 1), :] = jnp.sum(kept, axis=0, keepdims=True)


def inner_kernel(depth, cases, middle_ref, outer_ref, source_ref, coef_ref, *rest):
    out_ref, *more_refs, deriv_ref = rest
    planes = 4 * cases * depth
    lane, layer = lanes_of((8, 128)), rows_of((8, 128))
    gap = rows_of((128, 256)) - lanes_of((128, 256)) % 128
    second = jnp.where(jnp.abs(gap) == 1, 16.0, jnp.where(jnp.abs(gap) == 2, -1.0, 0.0))
    first = jnp.where(gap == 1, 8.0, jnp.where(gap == -1, -8.0, jnp.where(gap == 2, -1.0, jnp.where(gap == -2, 1.0, 0.0))))
    weights = jnp.where(lanes_of((128, 256)) < 128, second, first).astype(jnp.bfloat16)
    for row in range(8):
        ref, place = row_place((middle_ref, outer_ref), row, planes)
        value = ref[rows(place, planes), :]
        deriv_ref[rows(row * planes, planes), :] = exact_dot(value, weights)

    def one(index, _):
        case, block = index // (depth // 8), index % (depth // 8)
        k = layer + 8 * block
        height = (k.astype(jnp.float32) + 0.5) / depth
        offsets = [pl.multiple_of((c * cases + case) * depth + 8 * block, 8) for c in range(4)]
        places = [row_place((middle_ref, outer_ref), row, planes) for row in range(8)]
        tiles = [[ref[rows(place + offsets[c]), :] for ref, place in places] for c in range(4)]

        for row in range(8):

            def coef(i):
                return coef_ref[pl.ds((case * N_COEF + i) * 8 + row, 1), :]

            along = []
            for c in range(4):
                near = [tiles[c][row + by] if 0 <= row + by < 8 else None for by in (-2, -1, 1, 2)]
                along.append(near)

            def first_x(c):
                m2, m1, p1, p2 = along[c]
                ones = 8.0 * (p1 - m1) if m1 is not None and p1 is not None else 8.0 * p1 if m1 is None else -8.0 * m1
                if m2 is not None and p2 is not None:
                    return ones - (p2 - m2)
                return ones - p2 if m2 is None else ones + m2

            def second_x(c):
                m2, m1, p1, p2 = along[c]
                ones = 16.0 * (p1 + m1) if m1 is not None and p1 is not None else 16.0 * (p1 if m1 is None else m1)
                if m2 is not None and p2 is not None:
                    return ones - (p2 + m2)
                return ones - (p2 if m2 is None else m2)

            carry = coef(CARRY) * height
            sound = coef(SOUND_STEP)
            step = coef(STEP)
            slopes = [first_x(c) for c in range(4)]
            for c in range(4):
                here = row * planes + offsets[c]
                ref, place = places[row]
                behind = jnp.where(k > 0, ref[rows(place + offsets[c] - 1), :], 0.0)
                beyond = jnp.where(k < depth - 1, ref[rows(place + offsets[c] + 1), :], 0.0)
                source = source_ref[strided(offsets[c] * 8 + row), :]
                w = WEIGHT[c]
                value = coef(CENTER + w) * tiles[c][row] + coef(SPREAD + w) * (second_x(c) + deriv_ref[rows(here), 0:128])
                value += coef(ACROSS + w) * (behind + beyond) + step * source + carry * slopes[c]
                if c == 0:
                    other = row * planes + offsets[2]
                    value += sound * (slopes[1] + deriv_ref[rows(other), 128:256])
                elif c == 1:
                    value += sound * slopes[0]
                elif c == 2:
                    other = row * planes + offsets[0]
                    value += sound * deriv_ref[rows(other), 128:256]
                else:
                    value += coef(HEAT) * tiles[1][row]
                out_ref[rows(here), :] = value
        return 0

    lax.fori_loop(0, cases * (depth // 8), one, 0)

    if more_refs:
        (total_ref,) = more_refs
        for case in range(cases):
            for row in range(8):
                total = jnp.zeros((8, 128), jnp.float32)
                for block in range(depth // 8):
                    total += source_ref[strided((case * depth + 8 * block) * 8 + row), :]
                total_ref[pl.ds(case * 8 + row, 1), :] = jnp.sum(total, axis=0, keepdims=True)


def columns_beyond(cases, side_ref, mask_ref, packed_ref, corr_ref):
    slot = lanes_of((8, 128)) % 4
    for case in range(cases):
        coefs = [packed_ref[rows((case * N_PACKED + i) * 8), :] for i in range(N_PACKED)]
        second, first = [], []
        for c in range(4):
            side = side_ref[rows((c * cases + case) * 8), :] * mask_ref[...]
            p1 = jnp.where(slot == 1, pltpu.roll(side, 127, 1), 0.0)
            p2 = jnp.where(slot < 2, pltpu.roll(side, 126, 1), 0.0)
            m1 = jnp.where(slot == 2, pltpu.roll(side, 1, 1), 0.0)
            m2 = jnp.where(slot >= 2, pltpu.roll(side, 2, 1), 0.0)
            second.append(16.0 * (p1 + m1) - (p2 + m2))
            first.append(8.0 * (p1 - m1) - (p2 - m2))
        for c in range(4):
            value = coefs[WEIGHT[c]] * second[c]
            if c == 0:
                value += coefs[3] * first[2]
            elif c == 2:
                value += coefs[3] * first[0]
            corr_ref[rows((c * cases + case) * 8), :] = value


def depth_sum(tiles):
    total = tiles[0]
    for tile in tiles[1:]:
        total = total + tile
    return jnp.sum(total, axis=0, keepdims=True)


def next_moments(depth, tiles_of, layer):
    density = tiles_of(0)
    heights = [(layer + (8 * block + 0.5)).astype(jnp.float32) / depth for block in range(depth // 8)]
    return (
        depth_sum(density),
        depth_sum([tile * height for tile, height in zip(density, heights, strict=True)]),
        depth_sum(tiles_of(1)),
        depth_sum(tiles_of(2)),
        density[0][0:1] + density[-1][7:8],
    )


def wall_sums(depth, tiles_of, layer):
    momentum, before = tiles_of(1), tiles_of(1, -1)
    changes = [momentum[0] - jnp.where(layer > 0, before[0], 0.0)]
    changes += [here - there for here, there in zip(momentum[1:], before[1:], strict=True)]
    squares = [change * change for change in changes] + [jnp.where(layer == 7, momentum[-1] * momentum[-1], 0.0)]
    return depth_sum(tiles_of(0)), depth_sum(squares)


def line_sums(depth, cases, planes, sums, ref, which, out_ref, layer):
    for case in range(cases):
        for i, row in enumerate(which):

            def tiles_of(c, by=0):
                start = PAD + i * planes + (c * cases + case) * depth
                return [ref[rows(start + by + 8 * block), :] for block in range(depth // 8)]

            lines = sums(depth, tiles_of, layer)
            for n, line in enumerate(lines):
                out_ref[pl.ds((case * len(lines) + n) * 8 + row, 1), :] = line


def joined_sums(middle_ref, outer_ref, index, layer):
    return jnp.where((layer >= 2) & (layer < 6), middle_ref[rows(index * 8), :], outer_ref[rows(index * 8), :])


def sides_kernel(depth, cases, sums, inner_ref, side_ref, mask_ref, packed_ref, middle_ref, loose_ref, sums_ref, corr_ref):
    planes = 4 * cases * depth
    lane, layer = lanes_of((8, 128)), rows_of((8, 128))
    edge = (lane < 2) | (lane >= 126)
    columns_beyond(cases, side_ref, mask_ref, packed_ref, corr_ref)

    def one(case, _):
        for row in range(8):
            for c in range(4):
                line = jnp.broadcast_to(corr_ref[pl.ds((c * cases + case) * 8 + row, 1), :], (8, 128))
                for block in range(depth // 8):
                    offset = pl.multiple_of((c * cases + case) * depth + 8 * block, 8)
                    moved = pltpu.roll(line, 2 + 32 * block, 1, stride=4, stride_axis=0)
                    value = inner_ref[rows(row * planes + offset), :] + jnp.where(edge, moved, 0.0)
                    ref, place = row_place((middle_ref, loose_ref), row, planes)
                    ref[rows(place + offset), :] = value
        return 0

    lax.fori_loop(0, cases, one, 0)
    line_sums(depth, cases, planes, sums, middle_ref, MIDDLE, sums_ref, layer)


def outer_rows(depth, cases, planes, parts, loose_ref, post, coef_ref, store):
    layer = rows_of((8, 128))

    def one(case, _):
        for block in range(depth // 8):
            height = ((layer + 8 * block).astype(jnp.float32) + 0.5) / depth
            offsets = [pl.multiple_of((c * cases + case) * depth + 8 * block, 8) for c in range(4)]
            near = {c: [post.get(rows(i * planes + offsets[c])) for i in range(2)] for c in {*parts, *range(2)}}
            whole = {c: {} for c in parts}
            for i, row in enumerate(OUTER):

                def coef(n):
                    return coef_ref[pl.ds((case * N_COEF + n) * 8 + row, 1), :]

                second, first = {}, {}
                for c, ((m2, p1), (m1, p2)) in near.items():
                    if row == 0:
                        second[c], first[c] = 16.0 * m1 - m2, m2 - 8.0 * m1
                    elif row == 1:
                        second[c], first[c] = -m1, m1
                    elif row == 6:
                        second[c], first[c] = -p1, -p1
                    else:
                        second[c], first[c] = 16.0 * p1 - p2, 8.0 * p1 - p2
                for c in parts:
                    value = loose_ref[rows(PAD + i * planes + offsets[c]), :]
                    value += coef(SPREAD + WEIGHT[c]) * second[c] + coef(CARRY) * height * first[c]
                    if c < 2:
                        value += coef(SOUND_STEP) * first[1 - c]
                    whole[c][row] = value
            for c in parts:
                store(c, case, block, offsets[c], whole[c])
        return 0

    lax.fori_loop(0, cases, one, 0)


def joined_kernel(
    depth,
    cases,
    place_ref,
    loose_ref,
    middle_sums_ref,
    source_total_ref,
    second_in_ref,
    first_in_ref,
    coef_ref,
    outer_ref,
    second_ref,
    first_ref,
    moment_ref,
    outer_sums_ref,
):
    planes = 4 * cases * depth
    lane, layer = lanes_of((8, 128)), rows_of((8, 128))
    post, arrived = Post(place_ref, first_ref, second_ref), Post(place_ref, first_in_ref, second_in_ref)

    def store(c, case, block, offset, tiles):
        for i, row in enumerate(OUTER):
            outer_ref[rows(PAD + i * planes + offset), :] = tiles[row]
        post.put_tiles(planes, offset, tiles)

    outer_rows(depth, cases, planes, range(4), loose_ref, arrived, coef_ref, store)

    line_sums(depth, cases, planes, next_moments, outer_ref, OUTER, outer_sums_ref, layer)
    for case in range(cases):

        def coef(i):
            return coef_ref[rows((case * N_COEF + i) * 8), :]

        moments = [joined_sums(middle_sums_ref, outer_sums_ref, case * 5 + i, layer) for i in range(5)]
        total, lifted, along, across, walls = moments
        for i in range(3):
            moment_ref[rows((case * 3 + i) * 8), :] = moments[i]

        def x_parts(plane):
            m1, m2 = jnp.where(layer >= 1, pltpu.roll(plane, 1, 0), 0.0), jnp.where(layer >= 2, pltpu.roll(plane, 2, 0), 0.0)
            p1, p2 = jnp.where(layer < 7, pltpu.roll(plane, 7, 0), 0.0), jnp.where(layer < 6, pltpu.roll(plane, 6, 0), 0.0)
            return 16.0 * (p1 + m1) - (p2 + m2), 8.0 * (p1 - m1) - (p2 - m2)

        def y_parts(plane):
            m1, m2 = jnp.where(lane >= 1, pltpu.roll(plane, 1, 1), 0.0), jnp.where(lane >= 2, pltpu.roll(plane, 2, 1), 0.0)
            p1, p2 = jnp.where(lane < 127, pltpu.roll(plane, 127, 1), 0.0), jnp.where(lane < 126, pltpu.roll(plane, 126, 1), 0.0)
            return 16.0 * (p1 + m1) - (p2 + m2), 8.0 * (p1 - m1) - (p2 - m2)

        value = coef(CENTER) * total + coef(SPREAD) * (x_parts(total)[0] + y_parts(total)[0])
        value += coef(ACROSS) * (2.0 * total - walls) + coef(CARRY) * x_parts(lifted)[1]
        value += coef(SOUND_STEP) * (x_parts(along)[1] + y_parts(across)[1]) + coef(STEP) * source_total_ref[rows(case * 8), :]
        sent = (value, coef(SPREAD), coef(CARRY), coef(SOUND_STEP), coef(FLUX))
        for i, plane in enumerate(sent):
            post.put(pl.ds(2 * planes + (case * 5 + i) * 2, 2), plane[6:8], plane[0:2])


def edge_sums(tile):
    for by in (4, 8, 16, 32, 64):
        tile = tile + pltpu.roll(tile, by, 1)
    return pltpu.roll(tile, 2, 1)


def final_kernel(
    depth,
    cases,
    place_ref,
    loose_ref,
    middle_sums_ref,
    corr_ref,
    second_in_ref,
    first_in_ref,
    coef_ref,
    moment_ref,
    outer_ref,
    grad_ref,
    line_ref,
    outer_sums_ref,
):
    planes = 4 * cases * depth
    lane, layer = lanes_of((8, 128)), rows_of((8, 128))
    arrived = Post(place_ref, first_in_ref, second_in_ref)

    def store(c, case, block, offset, tiles):
        for i, row in enumerate(OUTER):
            outer_ref[rows(PAD + i * planes + offset), :] = tiles[row]

    outer_rows(depth, cases, planes, range(2), loose_ref, arrived, coef_ref, store)
    line_sums(depth, cases, planes, wall_sums, outer_ref, OUTER, outer_sums_ref, layer)

    zero = jnp.zeros((8, 128), jnp.float32)
    grad, missing = zero, zero
    for case in range(cases):

        def coef(i):
            return coef_ref[rows((case * N_COEF + i) * 8), :]

        pairs = [arrived.get(pl.ds(2 * planes + (case * 5 + i) * 2, 2)) for i in range(5)]
        below, above = [pair[0] for pair in pairs], [pair[1] for pair in pairs]
        total, lifted, along = (moment_ref[rows((case * 3 + i) * 8), :] for i in range(3))

        def beyond(plane):
            first, second, last, before = plane[0:1], plane[1:2], plane[7:8], plane[6:7]
            down = (jnp.concatenate([-first, 16.0 * first - second], 0), jnp.concatenate([-first, 8.0 * first - second], 0))
            up = (jnp.concatenate([16.0 * last - before, -last], 0), jnp.concatenate([before - 8.0 * last, last], 0))
            return down, up

        down, up = zip(beyond(total), beyond(lifted), beyond(along), strict=True)
        mean_below = below[0] + below[1] * down[0][0] + below[2] * down[1][1] + below[3] * down[2][1]
        mean_above = above[0] + above[1] * up[0][0] + above[2] * up[1][1] + above[3] * up[2][1]
        mean, bend = (joined_sums(middle_sums_ref, outer_sums_ref, case * 2 + i, layer) for i in range(2))
        halo = jnp.concatenate([mean_above, zero[0:4], mean_below], axis=0)
        m1 = pltpu.roll(jnp.where(layer == 7, halo, mean), 1, 0)
        m2 = pltpu.roll(jnp.where(layer >= 6, halo, mean), 2, 0)
        p1 = pltpu.roll(jnp.where(layer == 0, halo, mean), 7, 0)
        p2 = pltpu.roll(jnp.where(layer < 2, halo, mean), 6, 0)
        grad += coef(FLUX) * (8.0 * (p1 - m1) - (p2 - m2)) + coef(BEND) * bend
        change = edge_sums(corr_ref[rows(case * 8), :])
        down_rows = jnp.concatenate([change[6:7] - 8.0 * change[7:8], change[7:8]], axis=0)
        up_rows = jnp.concatenate([-change[0:1], 8.0 * change[0:1] - change[1:2]], axis=0)
        missing += jnp.concatenate([above[4] * down_rows, zero[0:4], below[4] * up_rows], axis=0)
    corner = ((lane < 2) | (lane >= 126)) & ((layer < 2) | (layer >= 6))
    grad_ref[...] = grad
    inside = jnp.where(corner, 0.0, grad)
    rest = jnp.sum(inside * inside, axis=0, keepdims=True)
    corners = pltpu.roll(jnp.where(corner, grad, 0.0), 2, 1, stride=4, stride_axis=0)
    shares = pltpu.roll(jnp.where(corner, missing, 0.0), 34, 1, stride=4, stride_axis=0)
    line = jnp.sum(corners + shares, axis=0, keepdims=True)
    line = jnp.where(lanes_of((1, 128)) < 64, line, rest + pltpu.roll(rest, 64, 1))
    line_ref[...] = jnp.broadcast_to(line[None], line_ref.shape)


def scaled(cells, devices, trans, place_ref, grad_ref, sums_ref, lines_ref):
    pad = -(-trans // 8) * 8
    lane, row = lanes_of((8, 128)), rows_of((8, 128))
    zero = jnp.zeros((pad, 128), jnp.float32)
    lines_ref[rows(0, pad), :] = zero
    lines_ref[rows(pad + devices, pad), :] = zero
    lines_ref[rows(pad, devices), :] = sums_ref[...]
    total, own = jnp.zeros((8, 128), jnp.float32), jnp.zeros((8, 128), jnp.float32)
    device = place_ref[rows(DEVICE * 8), :]
    for block in range(devices // 8):
        here = lines_ref[rows(pad + 8 * block), :]
        below, above = lines_ref[rows(pad - trans + 8 * block), :], lines_ref[rows(pad + trans + 8 * block), :]
        share = pltpu.roll(jnp.where(lane < 48, below, above), 96, 1)
        own += jnp.where(row + 8 * block == device, share, 0.0)
        corner = here + share
        total += jnp.where(lane < 32, corner * corner, jnp.where(lane >= 64, here, 0.0))
    total = jnp.sum(jnp.sum(total, axis=0, keepdims=True), axis=1, keepdims=True)
    own = jnp.broadcast_to(jnp.sum(own, axis=0, keepdims=True), (8, 128))
    grad = grad_ref[...]
    edge = (lane < 2) | (lane >= 126)
    for i in (0, 1, 6, 7):
        grad += jnp.where((row == i) & edge, pltpu.roll(own, (126 - 4 * i) % 128, 1), 0.0)
    return grad / jnp.sqrt(total / cells + 1e-06)


def rest_kernel(
    depth,
    cases,
    cells,
    devices,
    trans,
    place_ref,
    loose_ref,
    middle_ref,
    early_ref,
    second_in_ref,
    first_in_ref,
    coef_ref,
    grad_ref,
    sums_ref,
    out_ref,
    wall_out_ref,
    state_ref,
    wall_ref,
    lines_ref,
    sems,
):
    wall_ref[...] = scaled(cells, devices, trans, place_ref, grad_ref, sums_ref, lines_ref)
    wall_copy = pltpu.make_async_copy(wall_ref, wall_out_ref, sems.at[2])
    wall_copy.start()
    planes = 4 * cases * depth
    half = planes * 4
    copies = [pltpu.make_async_copy(state_ref.at[rows(i * half, half), :], out_ref.at[rows(i * half, half), :], sems.at[i]) for i in range(2)]

    def place_tiles(c, refs):
        def one(case, _):
            for block in range(depth // 8):
                offset = pl.multiple_of((c * cases + case) * depth + 8 * block, 8)
                for row in range(8):
                    if refs[row] is not None:
                        ref, place = row_place(refs[row], row, planes)
                        state_ref[strided(offset * 8 + row), :] = ref[rows(place + offset), :]
            return 0

        lax.fori_loop(0, cases, one, 0)

    both = (middle_ref, early_ref)
    for c in range(2):
        place_tiles(c, [both] * 8)
    copies[0].start()
    for c in range(2, 4):
        place_tiles(c, [both if row in MIDDLE else None for row in range(8)])

    def store(c, case, block, offset, tiles):
        for row, tile in tiles.items():
            state_ref[strided(offset * 8 + row), :] = tile

    arrived = Post(place_ref, first_in_ref, second_in_ref)
    outer_rows(depth, cases, planes, (2, 3), loose_ref, arrived, coef_ref, store)
    copies[1].start()
    wall_copy.wait()
    copies[0].wait()
    copies[1].wait()


def f32(*shape):
    return jax.ShapeDtypeStruct(shape, jnp.float32)


def over_tiles(numbers):
    which = rows_of((8 * len(numbers), 128)) // 8
    held = jnp.full(which.shape, numbers[0], jnp.int32)
    for i, number in enumerate(numbers[1:], 1):
        held = jnp.where(which == i, number, held)
    return held


def in_hbm(array):
    return pltpu.with_memory_space_constraint(array, pltpu.HBM)


def call(kernel, *args, outs, scratch=(), hbm=(), out=VM):
    specs = [VM] * len(args)
    for i in hbm:
        specs[i] = HB
    return pl.pallas_call(
        kernel,
        out_shape=outs,
        in_specs=specs,
        out_specs=tuple([out] * len(outs)),
        scratch_shapes=[pltpu.VMEM(shape, jnp.float32) if isinstance(shape, tuple) else shape for shape in scratch],
        compiler_params=PARAMS,
    )(*args)


def neighbours(axis):
    size = lax.axis_size(axis)
    up = [(i, i + 1) for i in range(size - 1)]
    return up, [(j, i) for i, j in up]


def exchange_rows(first, second):
    size = lax.axis_size("roll")
    inner = [(i, i ^ 1) for i in range(size) if i ^ 1 < size]
    outer = [pair for i in range(1, size - 1, 2) for pair in ((i, i + 1), (i + 1, i))]
    second = lax.ppermute(second, "roll", outer)
    return lax.ppermute(first, "roll", inner), second


def exchange_columns(cols):
    ahead, back = neighbours("trans")
    if lax.axis_size("trans") == 2:
        return lax.ppermute(cols, "trans", ahead + back)
    left, right = lax.ppermute(cols, "trans", ahead), lax.ppermute(cols, "trans", back)
    return jnp.where(lanes_of(cols.shape) % 4 < 2, left, right)


def on_device(adjoint, source, pressure, film, cavity, temp_index):
    components, cases, depth, width_x, width_y = adjoint.shape
    planes = components * cases * depth
    assert (components, width_x, width_y, 4 * depth) == (4, 8, 128, 128)
    state = adjoint.reshape(planes * 8, 128)
    forcing = source.reshape(planes * 8, 128)
    roll, trans, trans_size = lax.axis_index("roll"), lax.axis_index("trans"), lax.axis_size("trans")
    place = over_tiles([trans, trans_size, roll % 2, roll * trans_size + trans])
    devices = lax.axis_size("roll") * trans_size
    inner, part = f32(planes * 8, 128), f32(planes * 4 + 2 * PAD, 128)
    message, tailed, cols_shape = f32(planes * 2, 128), f32(planes * 2 + TAIL, 128), f32(components * cases * 8, 128)
    state, first, second = call(
        functools.partial(send_kernel, depth, cases),
        place,
        in_hbm(state),
        outs=(inner, message, message),
        scratch=[pltpu.SemaphoreType.DMA((PIECES,))],
        hbm=(1,),
    )
    primal = (temp_index.reshape(1, cases), pressure.reshape(cases * 8, 128), film, cavity.reshape(cases * 8, 128))
    (cols,) = call(functools.partial(pack_kernel, depth, cases), state, outs=(cols_shape,))
    middle, outer, coef, packed, mask = call(
        functools.partial(tile_kernel, depth, cases),
        state,
        place,
        *map(in_hbm, primal),
        outs=(part, part, f32(cases * N_COEF * 8, 128), f32(cases * N_PACKED * 8, 128), f32(8, 128)),
        scratch=[pltpu.VMEM(array.shape, array.dtype) for array in primal] + [pltpu.SemaphoreType.DMA((4,))],
        hbm=range(2, 6),
    )
    for index in range(SECTIONS):
        more = index < SECTIONS - 1
        first, second = exchange_rows(first, second)
        side = exchange_columns(cols)
        whole, *total = call(
            functools.partial(inner_kernel, depth, cases),
            middle,
            outer,
            forcing,
            coef,
            outs=(inner, f32(cases * 8, 128)) if more else (inner,),
            scratch=[(planes * 8, 256)],
        )
        middle, loose, sums, *corr = call(
            functools.partial(sides_kernel, depth, cases, next_moments if more else wall_sums),
            whole,
            side,
            mask,
            packed,
            outs=(part, part, f32(cases * (5 if more else 2) * 8, 128)) + (() if more else (cols_shape,)),
            scratch=[cols_shape.shape] if more else [],
        )
        if more:
            outer, second, first, moments = call(
                functools.partial(joined_kernel, depth, cases),
                place,
                loose,
                sums,
                *total,
                second,
                first,
                coef,
                outs=(part, tailed, tailed, f32(cases * 3 * 8, 128)),
                scratch=[(cases * 5 * 8, 128)],
            )
            (cols,) = call(functools.partial(columns_kernel, depth, cases), middle, outer, outs=(cols_shape,))
        else:
            early, grad, sums = call(
                functools.partial(final_kernel, depth, cases),
                place,
                loose,
                sums,
                *corr,
                second,
                first,
                coef,
                moments,
                outs=(part, f32(8, 128), pltpu.VMEM((devices, 1, 128), jnp.float32)),
                scratch=[(cases * 2 * 8, 128)],
            )
    sums = lax.all_to_all(sums, ("roll", "trans"), 0, 0, tiled=True).reshape(devices, 128)
    pad = -(-trans_size // 8) * 8
    state, wall_step = call(
        functools.partial(rest_kernel, depth, cases, devices * width_x * width_y, devices, trans_size),
        place,
        loose,
        middle,
        early,
        second,
        first,
        coef,
        grad,
        sums,
        outs=(pltpu.HBM(inner.shape, jnp.float32), pltpu.HBM((8, 128), jnp.float32)),
        scratch=[inner.shape, (8, 128), (devices + 2 * pad, 128), pltpu.SemaphoreType.DMA((3,))],
        out=HB,
    )
    return (state.reshape(adjoint.shape), wall_step)


def solution(mesh):
    placed = (
        P(None, None, None, "roll", "trans"),
        P(None, None, None, "roll", "trans"),
        P(None, "roll", "trans"),
        P("roll", "trans"),
        P(None, "roll", "trans"),
        P(),
    )
    return jax.shard_map(
        on_device,
        mesh=mesh,
        in_specs=placed,
        out_specs=(P(None, None, None, "roll", "trans"), P("roll", "trans")),
        check_vma=False,
    )
```

```python
import functools

import jax
import jax.numpy as jnp
from jax import lax
from jax.experimental import pallas as pl
from jax.experimental.pallas import tpu as pltpu
from jax.sharding import PartitionSpec as P

SECTIONS = 2


VISCOSITY_PRESS = 0.3
VISCOSITY_TEMP = 0.5
THETA_STEP = 0.2
SOUND = 0.5
KAPPA = 0.6
HEATING = 0.3
ROLL_SPEED = 1.0
COURANT = 0.8

VM = pl.BlockSpec(memory_space=pltpu.VMEM)
HB = pl.BlockSpec(memory_space=pltpu.HBM)
PARAMS = pltpu.CompilerParams(vmem_limit_bytes=16 * 1024 * 1024)

PAD = 8
CENTER, SPREAD, ACROSS = (0, 3, 6)
CARRY, SOUND_STEP, STEP, HEAT, FLUX, BEND = range(9, 15)
N_COEF = 15
N_PACKED = 4
PIECES = 4
TAIL = 24
MIDDLE, OUTER = (2, 3, 4, 5), (0, 1, 6, 7)
TRANS, TRANS_SIZE, ODD, DEVICE = range(4)
WEIGHT = (0, 1, 1, 2)


def lanes_of(shape):
    return lax.broadcasted_iota(jnp.int32, shape, 1)


def rows_of(shape):
    return lax.broadcasted_iota(jnp.int32, shape, 0)


def rows(start, count=8):
    return pl.ds(start, count)


def strided(start):
    return pl.ds(start, 8, stride=8)


def coefficients(depth, cases, place_ref, level_ref, pressure_ref, film_ref, cavity_ref, coef_ref, packed_ref, mask_ref):
    lane, row = lanes_of((8, 128)), rows_of((8, 128))
    film = film_ref[...]
    for case in range(cases):
        theta = THETA_STEP * jnp.broadcast_to(level_ref[:, case : case + 1], (8, 128)).astype(jnp.float32)
        viscosity = jnp.exp(VISCOSITY_PRESS * pressure_ref[rows(case * 8), :] - VISCOSITY_TEMP * theta)
        film_coef = 4.0 * viscosity / (film * film)
        density = 1.0 - 0.6 * cavity_ref[rows(case * 8), :].astype(jnp.float32)
        step = COURANT / (32.0 / 3.0 * viscosity + 4.0 * film_coef + 2.0 * SOUND + 1.0)
        planes = [None] * N_COEF
        for i, weight in enumerate((0.5, 1.0, KAPPA)):
            planes[SPREAD + i] = (weight / 12.0) * step * viscosity
            planes[ACROSS + i] = weight * step * film_coef
            planes[CENTER + i] = 1.0 - 60.0 * planes[SPREAD + i] - 2.0 * planes[ACROSS + i]
        planes[CARRY] = (ROLL_SPEED / 12.0) * step * density
        planes[SOUND_STEP] = (SOUND / 12.0) * step
        planes[STEP] = step
        planes[HEAT] = HEATING * step * viscosity
        planes[FLUX] = (ROLL_SPEED / (24.0 * depth)) * density * film
        planes[BEND] = (8.0 / depth) * viscosity / (film * film * film)
        for i, plane in enumerate(planes):
            coef_ref[rows((case * N_COEF + i) * 8), :] = plane
        wanted = jnp.concatenate(planes[SPREAD : SPREAD + 3] + [planes[SOUND_STEP]], axis=0)
        packed = exact_dot(wanted, edge_columns())
        for i in range(N_PACKED):
            packed_ref[rows((case * N_PACKED + i) * 8), :] = packed[i * 8 : i * 8 + 8]
    trans = place_ref[rows(TRANS * 8), :]
    from_left = jnp.where(trans > 0, 1.0, 0.0)
    from_right = jnp.where(trans < place_ref[rows(TRANS_SIZE * 8), :] - 1, 1.0, 0.0)
    mask_ref[...] = jnp.where(lane % 4 < 2, from_left, from_right)


def edge_columns():
    source = lanes_of((128, 128)) % 4
    source = jnp.where(source < 2, 126 + source, source - 2)
    return jnp.where(rows_of((128, 128)) == source, 1.0, 0.0).astype(jnp.bfloat16)


def in_parts(value):
    high = value.astype(jnp.bfloat16)
    rest = value - high.astype(jnp.float32)
    middle = rest.astype(jnp.bfloat16)
    return jnp.concatenate([high, middle], axis=1), (rest - middle.astype(jnp.float32)).astype(jnp.bfloat16)


def exact_dot(value, weights):
    upper, low = in_parts(value)
    part = jnp.dot(upper, jnp.concatenate([weights, weights], axis=0), preferred_element_type=jnp.float32)
    return part + jnp.dot(low, weights, preferred_element_type=jnp.float32)


class Post:
    def __init__(self, place_ref, first_ref, second_ref):
        self.odd = place_ref[rows(ODD * 8), :] == 1
        self.refs = first_ref, second_ref

    def put(self, where, up, down):
        first, second = self.refs
        odd = self.odd[: where.size]
        first[where, :] = jnp.where(odd, down, up)
        second[where, :] = jnp.where(odd, up, down)

    def get(self, where):
        first, second = (ref[where, :] for ref in self.refs)
        odd = self.odd[: where.size]
        return jnp.where(odd, first, second), jnp.where(odd, second, first)

    def put_tiles(self, planes, first, tiles):
        for i in range(2):
            self.put(rows(i * planes + first), tiles[6 + i], tiles[i])


def row_place(refs, row, planes):
    if row in MIDDLE:
        return refs[0], PAD + MIDDLE.index(row) * planes
    return refs[1], PAD + OUTER.index(row) * planes


def send_kernel(depth, cases, place_ref, state_ref, copy_ref, first_ref, second_ref, sems):
    planes = 4 * cases * depth
    post = Post(place_ref, first_ref, second_ref)

    def piece(i):
        here = rows(i * (planes * 8 // PIECES), planes * 8 // PIECES)
        return pltpu.make_async_copy(state_ref.at[here, :], copy_ref.at[here, :], sems.at[i])

    for i in range(PIECES):
        piece(i).start()
    for i in range(PIECES):
        piece(i).wait()
        for first in range(i * planes // PIECES, (i + 1) * planes // PIECES, 8):
            post.put_tiles(planes, first, {row: copy_ref[strided(first * 8 + row), :] for row in (0, 1, 6, 7)})


def pack_kernel(depth, cases, state_ref, cols_ref):
    lane = lanes_of((8, 128))

    def one(pair, _):
        held = jnp.zeros((8, 128), jnp.float32)
        for layer in range(depth):
            group = depth - 1 - layer
            plane = state_ref[rows(pl.multiple_of((pair * depth + layer) * 8, 8)), :]
            held = jnp.where(lane // 4 == group, pltpu.roll(plane, (4 * group + 2) % 128, 1), held)
        cols_ref[rows(pl.multiple_of(pair * 8, 8)), :] = held
        return 0

    lax.fori_loop(0, 4 * cases, one, 0, unroll=4)


def tile_kernel(depth, cases, state_ref, place_ref, *rest):
    planes = 4 * cases * depth
    (middle_ref, outer_ref), outs, held, sems = rest[4:6], rest[6:9], rest[9:13], rest[13]
    copies = [pltpu.make_async_copy(rest[i], held[i], sems.at[i]) for i in range(4)]
    for copy in copies:
        copy.start()

    def one(pair, _):
        for row in range(8):
            ref, place = row_place((middle_ref, outer_ref), row, planes)
            for block in range(depth // 8):
                first = pl.multiple_of(pair * depth + 8 * block, 8)
                ref[rows(place + first), :] = state_ref[strided(first * 8 + row), :]
        return 0

    lax.fori_loop(0, 4 * cases, one, 0)
    for copy in copies:
        copy.wait()
    coefficients(depth, cases, place_ref, *held, *outs)


def columns_kernel(depth, cases, middle_ref, outer_ref, cols_ref):
    planes = 4 * cases * depth
    columns = edge_columns()
    mine = lanes_of((depth, 128)) // 4 == (depth - 1) - rows_of((depth, 128))
    for row in range(8):
        ref, place = row_place((middle_ref, outer_ref), row, planes)
        edges = exact_dot(ref[rows(place, planes), :], columns)
        for pair in range(4 * cases):
            kept = jnp.where(mine, edges[pair * depth : (pair + 1) * depth], 0.0)
            cols_ref[pl.ds(pair * 8 + row, 1), :] = jnp.sum(kept, axis=0, keepdims=True)


def inner_kernel(depth, cases, middle_ref, outer_ref, source_ref, coef_ref, *rest):
    out_ref, *more_refs, deriv_ref = rest
    planes = 4 * cases * depth
    lane, layer = lanes_of((8, 128)), rows_of((8, 128))
    gap = rows_of((128, 256)) - lanes_of((128, 256)) % 128
    second = jnp.where(jnp.abs(gap) == 1, 16.0, jnp.where(jnp.abs(gap) == 2, -1.0, 0.0))
    first = jnp.where(gap == 1, 8.0, jnp.where(gap == -1, -8.0, jnp.where(gap == 2, -1.0, jnp.where(gap == -2, 1.0, 0.0))))
    weights = jnp.where(lanes_of((128, 256)) < 128, second, first).astype(jnp.bfloat16)
    for row in range(8):
        ref, place = row_place((middle_ref, outer_ref), row, planes)
        value = ref[rows(place, planes), :]
        deriv_ref[rows(row * planes, planes), :] = exact_dot(value, weights)

    def one(index, _):
        case, block = index // (depth // 8), index % (depth // 8)
        k = layer + 8 * block
        height = (k.astype(jnp.float32) + 0.5) / depth
        offsets = [pl.multiple_of((c * cases + case) * depth + 8 * block, 8) for c in range(4)]
        places = [row_place((middle_ref, outer_ref), row, planes) for row in range(8)]
        tiles = [[ref[rows(place + offsets[c]), :] for ref, place in places] for c in range(4)]

        for row in range(8):

            def coef(i):
                return coef_ref[pl.ds((case * N_COEF + i) * 8 + row, 1), :]

            along = []
            for c in range(4):
                near = [tiles[c][row + by] if 0 <= row + by < 8 else None for by in (-2, -1, 1, 2)]
                along.append(near)

            def first_x(c):
                m2, m1, p1, p2 = along[c]
                ones = 8.0 * (p1 - m1) if m1 is not None and p1 is not None else 8.0 * p1 if m1 is None else -8.0 * m1
                if m2 is not None and p2 is not None:
                    return ones - (p2 - m2)
                return ones - p2 if m2 is None else ones + m2

            def second_x(c):
                m2, m1, p1, p2 = along[c]
                ones = 16.0 * (p1 + m1) if m1 is not None and p1 is not None else 16.0 * (p1 if m1 is None else m1)
                if m2 is not None and p2 is not None:
                    return ones - (p2 + m2)
                return ones - (p2 if m2 is None else m2)

            carry = coef(CARRY) * height
            sound = coef(SOUND_STEP)
            step = coef(STEP)
            slopes = [first_x(c) for c in range(4)]
            for c in range(4):
                here = row * planes + offsets[c]
                ref, place = places[row]
                behind = jnp.where(k > 0, ref[rows(place + offsets[c] - 1), :], 0.0)
                beyond = jnp.where(k < depth - 1, ref[rows(place + offsets[c] + 1), :], 0.0)
                source = source_ref[strided(offsets[c] * 8 + row), :]
                w = WEIGHT[c]
                value = coef(CENTER + w) * tiles[c][row] + coef(SPREAD + w) * (second_x(c) + deriv_ref[rows(here), 0:128])
                value += coef(ACROSS + w) * (behind + beyond) + step * source + carry * slopes[c]
                if c == 0:
                    other = row * planes + offsets[2]
                    value += sound * (slopes[1] + deriv_ref[rows(other), 128:256])
                elif c == 1:
                    value += sound * slopes[0]
                elif c == 2:
                    other = row * planes + offsets[0]
                    value += sound * deriv_ref[rows(other), 128:256]
                else:
                    value += coef(HEAT) * tiles[1][row]
                out_ref[rows(here), :] = value
        return 0

    lax.fori_loop(0, cases * (depth // 8), one, 0)

    if more_refs:
        (total_ref,) = more_refs
        for case in range(cases):
            for row in range(8):
                total = jnp.zeros((8, 128), jnp.float32)
                for block in range(depth // 8):
                    total += source_ref[strided((case * depth + 8 * block) * 8 + row), :]
                total_ref[pl.ds(case * 8 + row, 1), :] = jnp.sum(total, axis=0, keepdims=True)


def columns_beyond(cases, side_ref, mask_ref, packed_ref, corr_ref):
    slot = lanes_of((8, 128)) % 4
    for case in range(cases):
        coefs = [packed_ref[rows((case * N_PACKED + i) * 8), :] for i in range(N_PACKED)]
        second, first = [], []
        for c in range(4):
            side = side_ref[rows((c * cases + case) * 8), :] * mask_ref[...]
            p1 = jnp.where(slot == 1, pltpu.roll(side, 127, 1), 0.0)
            p2 = jnp.where(slot < 2, pltpu.roll(side, 126, 1), 0.0)
            m1 = jnp.where(slot == 2, pltpu.roll(side, 1, 1), 0.0)
            m2 = jnp.where(slot >= 2, pltpu.roll(side, 2, 1), 0.0)
            second.append(16.0 * (p1 + m1) - (p2 + m2))
            first.append(8.0 * (p1 - m1) - (p2 - m2))
        for c in range(4):
            value = coefs[WEIGHT[c]] * second[c]
            if c == 0:
                value += coefs[3] * first[2]
            elif c == 2:
                value += coefs[3] * first[0]
            corr_ref[rows((c * cases + case) * 8), :] = value


def depth_sum(tiles):
    total = tiles[0]
    for tile in tiles[1:]:
        total = total + tile
    return jnp.sum(total, axis=0, keepdims=True)


def next_moments(depth, tiles_of, layer):
    density = tiles_of(0)
    heights = [(layer + (8 * block + 0.5)).astype(jnp.float32) / depth for block in range(depth // 8)]
    return (
        depth_sum(density),
        depth_sum([tile * height for tile, height in zip(density, heights, strict=True)]),
        depth_sum(tiles_of(1)),
        depth_sum(tiles_of(2)),
        density[0][0:1] + density[-1][7:8],
    )


def wall_sums(depth, tiles_of, layer):
    momentum, before = tiles_of(1), tiles_of(1, -1)
    changes = [momentum[0] - jnp.where(layer > 0, before[0], 0.0)]
    changes += [here - there for here, there in zip(momentum[1:], before[1:], strict=True)]
    squares = [change * change for change in changes] + [jnp.where(layer == 7, momentum[-1] * momentum[-1], 0.0)]
    return depth_sum(tiles_of(0)), depth_sum(squares)


def line_sums(depth, cases, planes, sums, ref, which, out_ref, layer):
    for case in range(cases):
        for i, row in enumerate(which):

            def tiles_of(c, by=0):
                start = PAD + i * planes + (c * cases + case) * depth
                return [ref[rows(start + by + 8 * block), :] for block in range(depth // 8)]

            lines = sums(depth, tiles_of, layer)
            for n, line in enumerate(lines):
                out_ref[pl.ds((case * len(lines) + n) * 8 + row, 1), :] = line


def joined_sums(middle_ref, outer_ref, index, layer):
    return jnp.where((layer >= 2) & (layer < 6), middle_ref[rows(index * 8), :], outer_ref[rows(index * 8), :])


def sides_kernel(depth, cases, sums, inner_ref, side_ref, mask_ref, packed_ref, middle_ref, loose_ref, sums_ref, corr_ref):
    planes = 4 * cases * depth
    lane, layer = lanes_of((8, 128)), rows_of((8, 128))
    edge = (lane < 2) | (lane >= 126)
    columns_beyond(cases, side_ref, mask_ref, packed_ref, corr_ref)

    def one(case, _):
        for row in range(8):
            for c in range(4):
                line = jnp.broadcast_to(corr_ref[pl.ds((c * cases + case) * 8 + row, 1), :], (8, 128))
                for block in range(depth // 8):
                    offset = pl.multiple_of((c * cases + case) * depth + 8 * block, 8)
                    moved = pltpu.roll(line, 2 + 32 * block, 1, stride=4, stride_axis=0)
                    value = inner_ref[rows(row * planes + offset), :] + jnp.where(edge, moved, 0.0)
                    ref, place = row_place((middle_ref, loose_ref), row, planes)
                    ref[rows(place + offset), :] = value
        return 0

    lax.fori_loop(0, cases, one, 0)
    line_sums(depth, cases, planes, sums, middle_ref, MIDDLE, sums_ref, layer)


def outer_rows(depth, cases, planes, parts, loose_ref, post, coef_ref, store):
    layer = rows_of((8, 128))

    def one(case, _):
        for block in range(depth // 8):
            height = ((layer + 8 * block).astype(jnp.float32) + 0.5) / depth
            offsets = [pl.multiple_of((c * cases + case) * depth + 8 * block, 8) for c in range(4)]
            near = {c: [post.get(rows(i * planes + offsets[c])) for i in range(2)] for c in {*parts, *range(2)}}
            whole = {c: {} for c in parts}
            for i, row in enumerate(OUTER):

                def coef(n):
                    return coef_ref[pl.ds((case * N_COEF + n) * 8 + row, 1), :]

                second, first = {}, {}
                for c, ((m2, p1), (m1, p2)) in near.items():
                    if row == 0:
                        second[c], first[c] = 16.0 * m1 - m2, m2 - 8.0 * m1
                    elif row == 1:
                        second[c], first[c] = -m1, m1
                    elif row == 6:
                        second[c], first[c] = -p1, -p1
                    else:
                        second[c], first[c] = 16.0 * p1 - p2, 8.0 * p1 - p2
                for c in parts:
                    value = loose_ref[rows(PAD + i * planes + offsets[c]), :]
                    value += coef(SPREAD + WEIGHT[c]) * second[c] + coef(CARRY) * height * first[c]
                    if c < 2:
                        value += coef(SOUND_STEP) * first[1 - c]
                    whole[c][row] = value
            for c in parts:
                store(c, case, block, offsets[c], whole[c])
        return 0

    lax.fori_loop(0, cases, one, 0)


def joined_kernel(
    depth,
    cases,
    place_ref,
    loose_ref,
    middle_sums_ref,
    source_total_ref,
    second_in_ref,
    first_in_ref,
    coef_ref,
    outer_ref,
    second_ref,
    first_ref,
    moment_ref,
    outer_sums_ref,
):
    planes = 4 * cases * depth
    lane, layer = lanes_of((8, 128)), rows_of((8, 128))
    post, arrived = Post(place_ref, first_ref, second_ref), Post(place_ref, first_in_ref, second_in_ref)

    def store(c, case, block, offset, tiles):
        for i, row in enumerate(OUTER):
            outer_ref[rows(PAD + i * planes + offset), :] = tiles[row]
        post.put_tiles(planes, offset, tiles)

    outer_rows(depth, cases, planes, range(4), loose_ref, arrived, coef_ref, store)

    line_sums(depth, cases, planes, next_moments, outer_ref, OUTER, outer_sums_ref, layer)
    for case in range(cases):

        def coef(i):
            return coef_ref[rows((case * N_COEF + i) * 8), :]

        moments = [joined_sums(middle_sums_ref, outer_sums_ref, case * 5 + i, layer) for i in range(5)]
        total, lifted, along, across, walls = moments
        for i in range(3):
            moment_ref[rows((case * 3 + i) * 8), :] = moments[i]

        def x_parts(plane):
            m1, m2 = jnp.where(layer >= 1, pltpu.roll(plane, 1, 0), 0.0), jnp.where(layer >= 2, pltpu.roll(plane, 2, 0), 0.0)
            p1, p2 = jnp.where(layer < 7, pltpu.roll(plane, 7, 0), 0.0), jnp.where(layer < 6, pltpu.roll(plane, 6, 0), 0.0)
            return 16.0 * (p1 + m1) - (p2 + m2), 8.0 * (p1 - m1) - (p2 - m2)

        def y_parts(plane):
            m1, m2 = jnp.where(lane >= 1, pltpu.roll(plane, 1, 1), 0.0), jnp.where(lane >= 2, pltpu.roll(plane, 2, 1), 0.0)
            p1, p2 = jnp.where(lane < 127, pltpu.roll(plane, 127, 1), 0.0), jnp.where(lane < 126, pltpu.roll(plane, 126, 1), 0.0)
            return 16.0 * (p1 + m1) - (p2 + m2), 8.0 * (p1 - m1) - (p2 - m2)

        value = coef(CENTER) * total + coef(SPREAD) * (x_parts(total)[0] + y_parts(total)[0])
        value += coef(ACROSS) * (2.0 * total - walls) + coef(CARRY) * x_parts(lifted)[1]
        value += coef(SOUND_STEP) * (x_parts(along)[1] + y_parts(across)[1]) + coef(STEP) * source_total_ref[rows(case * 8), :]
        sent = (value, coef(SPREAD), coef(CARRY), coef(SOUND_STEP), coef(FLUX))
        for i, plane in enumerate(sent):
            post.put(pl.ds(2 * planes + (case * 5 + i) * 2, 2), plane[6:8], plane[0:2])


def edge_sums(tile):
    for by in (4, 8, 16, 32, 64):
        tile = tile + pltpu.roll(tile, by, 1)
    return pltpu.roll(tile, 2, 1)


def final_kernel(
    depth,
    cases,
    place_ref,
    loose_ref,
    middle_sums_ref,
    corr_ref,
    second_in_ref,
    first_in_ref,
    coef_ref,
    moment_ref,
    outer_ref,
    grad_ref,
    line_ref,
    outer_sums_ref,
):
    planes = 4 * cases * depth
    lane, layer = lanes_of((8, 128)), rows_of((8, 128))
    arrived = Post(place_ref, first_in_ref, second_in_ref)

    def store(c, case, block, offset, tiles):
        for i, row in enumerate(OUTER):
            outer_ref[rows(PAD + i * planes + offset), :] = tiles[row]

    outer_rows(depth, cases, planes, range(2), loose_ref, arrived, coef_ref, store)
    line_sums(depth, cases, planes, wall_sums, outer_ref, OUTER, outer_sums_ref, layer)

    zero = jnp.zeros((8, 128), jnp.float32)
    grad, missing = zero, zero
    for case in range(cases):

        def coef(i):
            return coef_ref[rows((case * N_COEF + i) * 8), :]

        pairs = [arrived.get(pl.ds(2 * planes + (case * 5 + i) * 2, 2)) for i in range(5)]
        below, above = [pair[0] for pair in pairs], [pair[1] for pair in pairs]
        total, lifted, along = (moment_ref[rows((case * 3 + i) * 8), :] for i in range(3))

        def beyond(plane):
            first, second, last, before = plane[0:1], plane[1:2], plane[7:8], plane[6:7]
            down = (jnp.concatenate([-first, 16.0 * first - second], 0), jnp.concatenate([-first, 8.0 * first - second], 0))
            up = (jnp.concatenate([16.0 * last - before, -last], 0), jnp.concatenate([before - 8.0 * last, last], 0))
            return down, up

        down, up = zip(beyond(total), beyond(lifted), beyond(along), strict=True)
        mean_below = below[0] + below[1] * down[0][0] + below[2] * down[1][1] + below[3] * down[2][1]
        mean_above = above[0] + above[1] * up[0][0] + above[2] * up[1][1] + above[3] * up[2][1]
        mean, bend = (joined_sums(middle_sums_ref, outer_sums_ref, case * 2 + i, layer) for i in range(2))
        halo = jnp.concatenate([mean_above, zero[0:4], mean_below], axis=0)
        m1 = pltpu.roll(jnp.where(layer == 7, halo, mean), 1, 0)
        m2 = pltpu.roll(jnp.where(layer >= 6, halo, mean), 2, 0)
        p1 = pltpu.roll(jnp.where(layer == 0, halo, mean), 7, 0)
        p2 = pltpu.roll(jnp.where(layer < 2, halo, mean), 6, 0)
        grad += coef(FLUX) * (8.0 * (p1 - m1) - (p2 - m2)) + coef(BEND) * bend
        change = edge_sums(corr_ref[rows(case * 8), :])
        down_rows = jnp.concatenate([change[6:7] - 8.0 * change[7:8], change[7:8]], axis=0)
        up_rows = jnp.concatenate([-change[0:1], 8.0 * change[0:1] - change[1:2]], axis=0)
        missing += jnp.concatenate([above[4] * down_rows, zero[0:4], below[4] * up_rows], axis=0)
    corner = ((lane < 2) | (lane >= 126)) & ((layer < 2) | (layer >= 6))
    grad_ref[...] = grad
    inside = jnp.where(corner, 0.0, grad)
    rest = jnp.sum(inside * inside, axis=0, keepdims=True)
    corners = pltpu.roll(jnp.where(corner, grad, 0.0), 2, 1, stride=4, stride_axis=0)
    shares = pltpu.roll(jnp.where(corner, missing, 0.0), 34, 1, stride=4, stride_axis=0)
    line = jnp.sum(corners + shares, axis=0, keepdims=True)
    line = jnp.where(lanes_of((1, 128)) < 64, line, rest + pltpu.roll(rest, 64, 1))
    line_ref[...] = jnp.broadcast_to(line[None], line_ref.shape)


def scaled(cells, devices, trans, place_ref, grad_ref, sums_ref, lines_ref):
    pad = -(-trans // 8) * 8
    lane, row = lanes_of((8, 128)), rows_of((8, 128))
    zero = jnp.zeros((pad, 128), jnp.float32)
    lines_ref[rows(0, pad), :] = zero
    lines_ref[rows(pad + devices, pad), :] = zero
    lines_ref[rows(pad, devices), :] = sums_ref[...]
    total, own = jnp.zeros((8, 128), jnp.float32), jnp.zeros((8, 128), jnp.float32)
    device = place_ref[rows(DEVICE * 8), :]
    for block in range(devices // 8):
        here = lines_ref[rows(pad + 8 * block), :]
        below, above = lines_ref[rows(pad - trans + 8 * block), :], lines_ref[rows(pad + trans + 8 * block), :]
        share = pltpu.roll(jnp.where(lane < 48, below, above), 96, 1)
        own += jnp.where(row + 8 * block == device, share, 0.0)
        corner = here + share
        total += jnp.where(lane < 32, corner * corner, jnp.where(lane >= 64, here, 0.0))
    total = jnp.sum(jnp.sum(total, axis=0, keepdims=True), axis=1, keepdims=True)
    own = jnp.broadcast_to(jnp.sum(own, axis=0, keepdims=True), (8, 128))
    grad = grad_ref[...]
    edge = (lane < 2) | (lane >= 126)
    for i in (0, 1, 6, 7):
        grad += jnp.where((row == i) & edge, pltpu.roll(own, (126 - 4 * i) % 128, 1), 0.0)
    return grad / jnp.sqrt(total / cells + 1e-06)


def rest_kernel(
    depth,
    cases,
    cells,
    devices,
    trans,
    place_ref,
    loose_ref,
    middle_ref,
    early_ref,
    second_in_ref,
    first_in_ref,
    coef_ref,
    grad_ref,
    sums_ref,
    out_ref,
    wall_out_ref,
    state_ref,
    wall_ref,
    lines_ref,
    sems,
):
    planes = 4 * cases * depth
    part = planes * 2

    def copy(first, count, sem):
        here = rows(first * part, count * part)
        return pltpu.make_async_copy(state_ref.at[here, :], out_ref.at[here, :], sems.at[sem])

    copies = [copy(2, 2, 0), copy(0, 1, 1), copy(1, 1, 2), pltpu.make_async_copy(wall_ref, wall_out_ref, sems.at[3])]

    def place_tiles(c, refs):
        def one(case, _):
            for block in range(depth // 8):
                offset = pl.multiple_of((c * cases + case) * depth + 8 * block, 8)
                for row in range(8):
                    if refs[row] is not None:
                        ref, place = row_place(refs[row], row, planes)
                        state_ref[strided(offset * 8 + row), :] = ref[rows(place + offset), :]
            return 0

        lax.fori_loop(0, cases, one, 0)

    both = (middle_ref, early_ref)
    for c in range(2, 4):
        place_tiles(c, [both if row in MIDDLE else None for row in range(8)])

    def store(c, case, block, offset, tiles):
        for row, tile in tiles.items():
            state_ref[strided(offset * 8 + row), :] = tile

    arrived = Post(place_ref, first_in_ref, second_in_ref)
    outer_rows(depth, cases, planes, (2, 3), loose_ref, arrived, coef_ref, store)
    copies[0].start()
    for c in range(2):
        place_tiles(c, [both] * 8)
        copies[1 + c].start()
    wall_ref[...] = scaled(cells, devices, trans, place_ref, grad_ref, sums_ref, lines_ref)
    copies[3].start()
    for each in copies:
        each.wait()


def f32(*shape):
    return jax.ShapeDtypeStruct(shape, jnp.float32)


def over_tiles(numbers):
    which = rows_of((8 * len(numbers), 128)) // 8
    held = jnp.full(which.shape, numbers[0], jnp.int32)
    for i, number in enumerate(numbers[1:], 1):
        held = jnp.where(which == i, number, held)
    return held


def in_hbm(array):
    return pltpu.with_memory_space_constraint(array, pltpu.HBM)


def call(kernel, *args, outs, scratch=(), hbm=(), out=VM):
    specs = [VM] * len(args)
    for i in hbm:
        specs[i] = HB
    return pl.pallas_call(
        kernel,
        out_shape=outs,
        in_specs=specs,
        out_specs=tuple([out] * len(outs)),
        scratch_shapes=[pltpu.VMEM(shape, jnp.float32) if isinstance(shape, tuple) else shape for shape in scratch],
        compiler_params=PARAMS,
    )(*args)


def neighbours(axis):
    size = lax.axis_size(axis)
    up = [(i, i + 1) for i in range(size - 1)]
    return up, [(j, i) for i, j in up]


def exchange_rows(first, second):
    size = lax.axis_size("roll")
    inner = [(i, i ^ 1) for i in range(size) if i ^ 1 < size]
    outer = [pair for i in range(1, size - 1, 2) for pair in ((i, i + 1), (i + 1, i))]
    second = lax.ppermute(second, "roll", outer)
    return lax.ppermute(first, "roll", inner), second


def exchange_columns(cols):
    ahead, back = neighbours("trans")
    if lax.axis_size("trans") == 2:
        return lax.ppermute(cols, "trans", ahead + back)
    left, right = lax.ppermute(cols, "trans", ahead), lax.ppermute(cols, "trans", back)
    return jnp.where(lanes_of(cols.shape) % 4 < 2, left, right)


def on_device(adjoint, source, pressure, film, cavity, temp_index):
    components, cases, depth, width_x, width_y = adjoint.shape
    planes = components * cases * depth
    assert (components, width_x, width_y, 4 * depth) == (4, 8, 128, 128)
    state = adjoint.reshape(planes * 8, 128)
    forcing = source.reshape(planes * 8, 128)
    roll, trans, trans_size = lax.axis_index("roll"), lax.axis_index("trans"), lax.axis_size("trans")
    place = over_tiles([trans, trans_size, roll % 2, roll * trans_size + trans])
    devices = lax.axis_size("roll") * trans_size
    inner, part = f32(planes * 8, 128), f32(planes * 4 + 2 * PAD, 128)
    message, tailed, cols_shape = f32(planes * 2, 128), f32(planes * 2 + TAIL, 128), f32(components * cases * 8, 128)
    state, first, second = call(
        functools.partial(send_kernel, depth, cases),
        place,
        in_hbm(state),
        outs=(inner, message, message),
        scratch=[pltpu.SemaphoreType.DMA((PIECES,))],
        hbm=(1,),
    )
    primal = (temp_index.reshape(1, cases), pressure.reshape(cases * 8, 128), film, cavity.reshape(cases * 8, 128))
    (cols,) = call(functools.partial(pack_kernel, depth, cases), state, outs=(cols_shape,))
    middle, outer, coef, packed, mask = call(
        functools.partial(tile_kernel, depth, cases),
        state,
        place,
        *map(in_hbm, primal),
        outs=(part, part, f32(cases * N_COEF * 8, 128), f32(cases * N_PACKED * 8, 128), f32(8, 128)),
        scratch=[pltpu.VMEM(array.shape, array.dtype) for array in primal] + [pltpu.SemaphoreType.DMA((4,))],
        hbm=range(2, 6),
    )
    for index in range(SECTIONS):
        more = index < SECTIONS - 1
        first, second = exchange_rows(first, second)
        side = exchange_columns(cols)
        whole, *total = call(
            functools.partial(inner_kernel, depth, cases),
            middle,
            outer,
            forcing,
            coef,
            outs=(inner, f32(cases * 8, 128)) if more else (inner,),
            scratch=[(planes * 8, 256)],
        )
        middle, loose, sums, *corr = call(
            functools.partial(sides_kernel, depth, cases, next_moments if more else wall_sums),
            whole,
            side,
            mask,
            packed,
            outs=(part, part, f32(cases * (5 if more else 2) * 8, 128)) + (() if more else (cols_shape,)),
            scratch=[cols_shape.shape] if more else [],
        )
        if more:
            outer, second, first, moments = call(
                functools.partial(joined_kernel, depth, cases),
                place,
                loose,
                sums,
                *total,
                second,
                first,
                coef,
                outs=(part, tailed, tailed, f32(cases * 3 * 8, 128)),
                scratch=[(cases * 5 * 8, 128)],
            )
            (cols,) = call(functools.partial(columns_kernel, depth, cases), middle, outer, outs=(cols_shape,))
        else:
            early, grad, sums = call(
                functools.partial(final_kernel, depth, cases),
                place,
                loose,
                sums,
                *corr,
                second,
                first,
                coef,
                moments,
                outs=(part, f32(8, 128), pltpu.VMEM((devices, 1, 128), jnp.float32)),
                scratch=[(cases * 2 * 8, 128)],
            )
    sums = lax.all_to_all(sums, ("roll", "trans"), 0, 0, tiled=True).reshape(devices, 128)
    pad = -(-trans_size // 8) * 8
    state, wall_step = call(
        functools.partial(rest_kernel, depth, cases, devices * width_x * width_y, devices, trans_size),
        place,
        loose,
        middle,
        early,
        second,
        first,
        coef,
        grad,
        sums,
        outs=(pltpu.HBM(inner.shape, jnp.float32), pltpu.HBM((8, 128), jnp.float32)),
        scratch=[inner.shape, (8, 128), (devices + 2 * pad, 128), pltpu.SemaphoreType.DMA((4,))],
        out=HB,
    )
    return (state.reshape(adjoint.shape), wall_step)


def solution(mesh):
    placed = (
        P(None, None, None, "roll", "trans"),
        P(None, None, None, "roll", "trans"),
        P(None, "roll", "trans"),
        P("roll", "trans"),
        P(None, "roll", "trans"),
        P(),
    )
    return jax.shard_map(
        on_device,
        mesh=mesh,
        in_specs=placed,
        out_specs=(P(None, None, None, "roll", "trans"), P("roll", "trans")),
        check_vma=False,
    )
```

```python
import functools

import jax
import jax.numpy as jnp
from jax import lax
from jax.experimental import pallas as pl
from jax.experimental.pallas import tpu as pltpu
from jax.sharding import PartitionSpec as P

SECTIONS = 2


VISCOSITY_PRESS = 0.3
VISCOSITY_TEMP = 0.5
THETA_STEP = 0.2
SOUND = 0.5
KAPPA = 0.6
HEATING = 0.3
ROLL_SPEED = 1.0
COURANT = 0.8

VM = pl.BlockSpec(memory_space=pltpu.VMEM)
HB = pl.BlockSpec(memory_space=pltpu.HBM)
PARAMS = pltpu.CompilerParams(vmem_limit_bytes=16 * 1024 * 1024)

PAD = 8
CENTER, SPREAD, ACROSS = (0, 3, 6)
CARRY, SOUND_STEP, STEP, HEAT, FLUX, BEND = range(9, 15)
N_COEF = 15
N_PACKED = 4
PIECES = 4
TAIL = 24
MIDDLE, OUTER = (2, 3, 4, 5), (0, 1, 6, 7)
TRANS, TRANS_SIZE, ODD, DEVICE = range(4)
WEIGHT = (0, 1, 1, 2)


def lanes_of(shape):
    return lax.broadcasted_iota(jnp.int32, shape, 1)


def rows_of(shape):
    return lax.broadcasted_iota(jnp.int32, shape, 0)


def rows(start, count=8):
    return pl.ds(start, count)


def strided(start):
    return pl.ds(start, 8, stride=8)


def coefficients(depth, cases, place_ref, level_ref, pressure_ref, film_ref, cavity_ref, coef_ref, packed_ref, mask_ref):
    lane, row = lanes_of((8, 128)), rows_of((8, 128))
    film = film_ref[...]
    for case in range(cases):
        theta = THETA_STEP * jnp.broadcast_to(level_ref[:, case : case + 1], (8, 128)).astype(jnp.float32)
        viscosity = jnp.exp(VISCOSITY_PRESS * pressure_ref[rows(case * 8), :] - VISCOSITY_TEMP * theta)
        film_coef = 4.0 * viscosity / (film * film)
        density = 1.0 - 0.6 * cavity_ref[rows(case * 8), :].astype(jnp.float32)
        step = COURANT / (32.0 / 3.0 * viscosity + 4.0 * film_coef + 2.0 * SOUND + 1.0)
        planes = [None] * N_COEF
        for i, weight in enumerate((0.5, 1.0, KAPPA)):
            planes[SPREAD + i] = (weight / 12.0) * step * viscosity
            planes[ACROSS + i] = weight * step * film_coef
            planes[CENTER + i] = 1.0 - 60.0 * planes[SPREAD + i] - 2.0 * planes[ACROSS + i]
        planes[CARRY] = (ROLL_SPEED / 12.0) * step * density
        planes[SOUND_STEP] = (SOUND / 12.0) * step
        planes[STEP] = step
        planes[HEAT] = HEATING * step * viscosity
        planes[FLUX] = (ROLL_SPEED / (24.0 * depth)) * density * film
        planes[BEND] = (8.0 / depth) * viscosity / (film * film * film)
        for i, plane in enumerate(planes):
            coef_ref[rows((case * N_COEF + i) * 8), :] = plane
        wanted = jnp.concatenate(planes[SPREAD : SPREAD + 3] + [planes[SOUND_STEP]], axis=0)
        packed = exact_dot(wanted, edge_columns())
        for i in range(N_PACKED):
            packed_ref[rows((case * N_PACKED + i) * 8), :] = packed[i * 8 : i * 8 + 8]
    trans = place_ref[rows(TRANS * 8), :]
    from_left = jnp.where(trans > 0, 1.0, 0.0)
    from_right = jnp.where(trans < place_ref[rows(TRANS_SIZE * 8), :] - 1, 1.0, 0.0)
    mask_ref[...] = jnp.where(lane % 4 < 2, from_left, from_right)


def edge_columns():
    source = lanes_of((128, 128)) % 4
    source = jnp.where(source < 2, 126 + source, source - 2)
    return jnp.where(rows_of((128, 128)) == source, 1.0, 0.0).astype(jnp.bfloat16)


def in_parts(value):
    high = value.astype(jnp.bfloat16)
    rest = value - high.astype(jnp.float32)
    middle = rest.astype(jnp.bfloat16)
    return jnp.concatenate([high, middle], axis=1), (rest - middle.astype(jnp.float32)).astype(jnp.bfloat16)


def exact_dot(value, weights):
    upper, low = in_parts(value)
    part = jnp.dot(upper, jnp.concatenate([weights, weights], axis=0), preferred_element_type=jnp.float32)
    return part + jnp.dot(low, weights, preferred_element_type=jnp.float32)


class Post:
    def __init__(self, place_ref, first_ref, second_ref):
        self.odd = place_ref[rows(ODD * 8), :] == 1
        self.refs = first_ref, second_ref

    def put(self, where, up, down):
        first, second = self.refs
        odd = self.odd[: where.size]
        first[where, :] = jnp.where(odd, down, up)
        second[where, :] = jnp.where(odd, up, down)

    def get(self, where):
        first, second = (ref[where, :] for ref in self.refs)
        odd = self.odd[: where.size]
        return jnp.where(odd, first, second), jnp.where(odd, second, first)

    def put_tiles(self, planes, first, tiles):
        for i in range(2):
            self.put(rows(i * planes + first), tiles[6 + i], tiles[i])


def row_place(refs, row, planes):
    if row in MIDDLE:
        return refs[0], PAD + MIDDLE.index(row) * planes
    return refs[1], PAD + OUTER.index(row) * planes


def send_kernel(depth, cases, place_ref, state_ref, copy_ref, first_ref, second_ref, sems):
    planes = 4 * cases * depth
    post = Post(place_ref, first_ref, second_ref)

    def piece(i):
        here = rows(i * (planes * 8 // PIECES), planes * 8 // PIECES)
        return pltpu.make_async_copy(state_ref.at[here, :], copy_ref.at[here, :], sems.at[i])

    for i in range(PIECES):
        piece(i).start()
    for i in range(PIECES):
        piece(i).wait()
        for first in range(i * planes // PIECES, (i + 1) * planes // PIECES, 8):
            post.put_tiles(planes, first, {row: copy_ref[strided(first * 8 + row), :] for row in (0, 1, 6, 7)})


def pack_kernel(depth, cases, state_ref, cols_ref):
    lane = lanes_of((8, 128))

    def one(pair, _):
        held = jnp.zeros((8, 128), jnp.float32)
        for layer in range(depth):
            group = depth - 1 - layer
            plane = state_ref[rows(pl.multiple_of((pair * depth + layer) * 8, 8)), :]
            held = jnp.where(lane // 4 == group, pltpu.roll(plane, (4 * group + 2) % 128, 1), held)
        cols_ref[rows(pl.multiple_of(pair * 8, 8)), :] = held
        return 0

    lax.fori_loop(0, 4 * cases, one, 0, unroll=4)


def tile_kernel(depth, cases, state_ref, place_ref, *rest):
    planes = 4 * cases * depth
    (middle_ref, outer_ref), outs, held, sems = rest[4:6], rest[6:9], rest[9:13], rest[13]
    copies = [pltpu.make_async_copy(rest[i], held[i], sems.at[i]) for i in range(4)]
    for copy in copies:
        copy.start()

    def one(pair, _):
        for row in range(8):
            ref, place = row_place((middle_ref, outer_ref), row, planes)
            for block in range(depth // 8):
                first = pl.multiple_of(pair * depth + 8 * block, 8)
                ref[rows(place + first), :] = state_ref[strided(first * 8 + row), :]
        return 0

    lax.fori_loop(0, 4 * cases, one, 0)
    for copy in copies:
        copy.wait()
    coefficients(depth, cases, place_ref, *held, *outs)


def columns_kernel(depth, cases, middle_ref, outer_ref, cols_ref):
    planes = 4 * cases * depth
    columns = edge_columns()
    mine = lanes_of((depth, 128)) // 4 == (depth - 1) - rows_of((depth, 128))
    for row in range(8):
        ref, place = row_place((middle_ref, outer_ref), row, planes)
        edges = exact_dot(ref[rows(place, planes), :], columns)
        for pair in range(4 * cases):
            kept = jnp.where(mine, edges[pair * depth : (pair + 1) * depth], 0.0)
            cols_ref[pl.ds(pair * 8 + row, 1), :] = jnp.sum(kept, axis=0, keepdims=True)


def inner_kernel(depth, cases, middle_ref, outer_ref, source_ref, coef_ref, *rest):
    out_ref, *more_refs, deriv_ref = rest
    planes = 4 * cases * depth
    lane, layer = lanes_of((8, 128)), rows_of((8, 128))
    gap = rows_of((128, 256)) - lanes_of((128, 256)) % 128
    second = jnp.where(jnp.abs(gap) == 1, 16.0, jnp.where(jnp.abs(gap) == 2, -1.0, 0.0))
    first = jnp.where(gap == 1, 8.0, jnp.where(gap == -1, -8.0, jnp.where(gap == 2, -1.0, jnp.where(gap == -2, 1.0, 0.0))))
    weights = jnp.where(lanes_of((128, 256)) < 128, second, first).astype(jnp.bfloat16)
    for row in range(8):
        ref, place = row_place((middle_ref, outer_ref), row, planes)
        value = ref[rows(place, planes), :]
        deriv_ref[rows(row * planes, planes), :] = exact_dot(value, weights)

    def one(index, _):
        case, block = index // (depth // 8), index % (depth // 8)
        k = layer + 8 * block
        height = (k.astype(jnp.float32) + 0.5) / depth
        offsets = [pl.multiple_of((c * cases + case) * depth + 8 * block, 8) for c in range(4)]
        places = [row_place((middle_ref, outer_ref), row, planes) for row in range(8)]
        tiles = [[ref[rows(place + offsets[c]), :] for ref, place in places] for c in range(4)]

        for row in range(8):

            def coef(i):
                return coef_ref[pl.ds((case * N_COEF + i) * 8 + row, 1), :]

            along = []
            for c in range(4):
                near = [tiles[c][row + by] if 0 <= row + by < 8 else None for by in (-2, -1, 1, 2)]
                along.append(near)

            def first_x(c):
                m2, m1, p1, p2 = along[c]
                ones = 8.0 * (p1 - m1) if m1 is not None and p1 is not None else 8.0 * p1 if m1 is None else -8.0 * m1
                if m2 is not None and p2 is not None:
                    return ones - (p2 - m2)
                return ones - p2 if m2 is None else ones + m2

            def second_x(c):
                m2, m1, p1, p2 = along[c]
                ones = 16.0 * (p1 + m1) if m1 is not None and p1 is not None else 16.0 * (p1 if m1 is None else m1)
                if m2 is not None and p2 is not None:
                    return ones - (p2 + m2)
                return ones - (p2 if m2 is None else m2)

            carry = coef(CARRY) * height
            sound = coef(SOUND_STEP)
            step = coef(STEP)
            slopes = [first_x(c) for c in range(4)]
            for c in range(4):
                here = row * planes + offsets[c]
                ref, place = places[row]
                behind = jnp.where(k > 0, ref[rows(place + offsets[c] - 1), :], 0.0)
                beyond = jnp.where(k < depth - 1, ref[rows(place + offsets[c] + 1), :], 0.0)
                source = source_ref[strided(offsets[c] * 8 + row), :]
                w = WEIGHT[c]
                value = coef(CENTER + w) * tiles[c][row] + coef(SPREAD + w) * (second_x(c) + deriv_ref[rows(here), 0:128])
                value += coef(ACROSS + w) * (behind + beyond) + step * source + carry * slopes[c]
                if c == 0:
                    other = row * planes + offsets[2]
                    value += sound * (slopes[1] + deriv_ref[rows(other), 128:256])
                elif c == 1:
                    value += sound * slopes[0]
                elif c == 2:
                    other = row * planes + offsets[0]
                    value += sound * deriv_ref[rows(other), 128:256]
                else:
                    value += coef(HEAT) * tiles[1][row]
                out_ref[rows(here), :] = value
        return 0

    lax.fori_loop(0, cases * (depth // 8), one, 0)

    if more_refs:
        (total_ref,) = more_refs
        for case in range(cases):
            for row in range(8):
                total = jnp.zeros((8, 128), jnp.float32)
                for block in range(depth // 8):
                    total += source_ref[strided((case * depth + 8 * block) * 8 + row), :]
                total_ref[pl.ds(case * 8 + row, 1), :] = jnp.sum(total, axis=0, keepdims=True)


def columns_beyond(cases, side_ref, mask_ref, packed_ref, corr_ref):
    slot = lanes_of((8, 128)) % 4
    for case in range(cases):
        coefs = [packed_ref[rows((case * N_PACKED + i) * 8), :] for i in range(N_PACKED)]
        second, first = [], []
        for c in range(4):
            side = side_ref[rows((c * cases + case) * 8), :] * mask_ref[...]
            p1 = jnp.where(slot == 1, pltpu.roll(side, 127, 1), 0.0)
            p2 = jnp.where(slot < 2, pltpu.roll(side, 126, 1), 0.0)
            m1 = jnp.where(slot == 2, pltpu.roll(side, 1, 1), 0.0)
            m2 = jnp.where(slot >= 2, pltpu.roll(side, 2, 1), 0.0)
            second.append(16.0 * (p1 + m1) - (p2 + m2))
            first.append(8.0 * (p1 - m1) - (p2 - m2))
        for c in range(4):
            value = coefs[WEIGHT[c]] * second[c]
            if c == 0:
                value += coefs[3] * first[2]
            elif c == 2:
                value += coefs[3] * first[0]
            corr_ref[rows((c * cases + case) * 8), :] = value


def depth_sum(tiles):
    total = tiles[0]
    for tile in tiles[1:]:
        total = total + tile
    return jnp.sum(total, axis=0, keepdims=True)


def next_moments(depth, tiles_of, layer):
    density = tiles_of(0)
    heights = [(layer + (8 * block + 0.5)).astype(jnp.float32) / depth for block in range(depth // 8)]
    return (
        depth_sum(density),
        depth_sum([tile * height for tile, height in zip(density, heights, strict=True)]),
        depth_sum(tiles_of(1)),
        depth_sum(tiles_of(2)),
        density[0][0:1] + density[-1][7:8],
    )


def wall_sums(depth, tiles_of, layer):
    momentum, before = tiles_of(1), tiles_of(1, -1)
    changes = [momentum[0] - jnp.where(layer > 0, before[0], 0.0)]
    changes += [here - there for here, there in zip(momentum[1:], before[1:], strict=True)]
    squares = [change * change for change in changes] + [jnp.where(layer == 7, momentum[-1] * momentum[-1], 0.0)]
    return depth_sum(tiles_of(0)), depth_sum(squares)


def line_sums(depth, cases, planes, sums, ref, which, out_ref, layer):
    for case in range(cases):
        for i, row in enumerate(which):

            def tiles_of(c, by=0):
                start = PAD + i * planes + (c * cases + case) * depth
                return [ref[rows(start + by + 8 * block), :] for block in range(depth // 8)]

            lines = sums(depth, tiles_of, layer)
            for n, line in enumerate(lines):
                out_ref[pl.ds((case * len(lines) + n) * 8 + row, 1), :] = line


def joined_sums(middle_ref, outer_ref, index, layer):
    return jnp.where((layer >= 2) & (layer < 6), middle_ref[rows(index * 8), :], outer_ref[rows(index * 8), :])


def sides_kernel(depth, cases, sums, inner_ref, side_ref, mask_ref, packed_ref, middle_ref, loose_ref, sums_ref, corr_ref):
    planes = 4 * cases * depth
    lane, layer = lanes_of((8, 128)), rows_of((8, 128))
    edge = (lane < 2) | (lane >= 126)
    columns_beyond(cases, side_ref, mask_ref, packed_ref, corr_ref)

    def one(case, _):
        for row in range(8):
            for c in range(4):
                line = jnp.broadcast_to(corr_ref[pl.ds((c * cases + case) * 8 + row, 1), :], (8, 128))
                for block in range(depth // 8):
                    offset = pl.multiple_of((c * cases + case) * depth + 8 * block, 8)
                    moved = pltpu.roll(line, 2 + 32 * block, 1, stride=4, stride_axis=0)
                    value = inner_ref[rows(row * planes + offset), :] + jnp.where(edge, moved, 0.0)
                    ref, place = row_place((middle_ref, loose_ref), row, planes)
                    ref[rows(place + offset), :] = value
        return 0

    lax.fori_loop(0, cases, one, 0, unroll=True)
    line_sums(depth, cases, planes, sums, middle_ref, MIDDLE, sums_ref, layer)


def outer_rows(depth, cases, planes, parts, loose_ref, post, coef_ref, store):
    layer = rows_of((8, 128))

    def one(case, _):
        for block in range(depth // 8):
            height = ((layer + 8 * block).astype(jnp.float32) + 0.5) / depth
            offsets = [pl.multiple_of((c * cases + case) * depth + 8 * block, 8) for c in range(4)]
            near = {c: [post.get(rows(i * planes + offsets[c])) for i in range(2)] for c in {*parts, *range(2)}}
            whole = {c: {} for c in parts}
            for i, row in enumerate(OUTER):

                def coef(n):
                    return coef_ref[pl.ds((case * N_COEF + n) * 8 + row, 1), :]

                second, first = {}, {}
                for c, ((m2, p1), (m1, p2)) in near.items():
                    if row == 0:
                        second[c], first[c] = 16.0 * m1 - m2, m2 - 8.0 * m1
                    elif row == 1:
                        second[c], first[c] = -m1, m1
                    elif row == 6:
                        second[c], first[c] = -p1, -p1
                    else:
                        second[c], first[c] = 16.0 * p1 - p2, 8.0 * p1 - p2
                for c in parts:
                    value = loose_ref[rows(PAD + i * planes + offsets[c]), :]
                    value += coef(SPREAD + WEIGHT[c]) * second[c] + coef(CARRY) * height * first[c]
                    if c < 2:
                        value += coef(SOUND_STEP) * first[1 - c]
                    whole[c][row] = value
            for c in parts:
                store(c, case, block, offsets[c], whole[c])
        return 0

    lax.fori_loop(0, cases, one, 0, unroll=True)


def joined_kernel(
    depth,
    cases,
    place_ref,
    loose_ref,
    middle_sums_ref,
    source_total_ref,
    second_in_ref,
    first_in_ref,
    coef_ref,
    outer_ref,
    second_ref,
    first_ref,
    moment_ref,
    outer_sums_ref,
):
    planes = 4 * cases * depth
    lane, layer = lanes_of((8, 128)), rows_of((8, 128))
    post, arrived = Post(place_ref, first_ref, second_ref), Post(place_ref, first_in_ref, second_in_ref)

    def store(c, case, block, offset, tiles):
        for i, row in enumerate(OUTER):
            outer_ref[rows(PAD + i * planes + offset), :] = tiles[row]
        post.put_tiles(planes, offset, tiles)

    outer_rows(depth, cases, planes, range(4), loose_ref, arrived, coef_ref, store)

    line_sums(depth, cases, planes, next_moments, outer_ref, OUTER, outer_sums_ref, layer)
    for case in range(cases):

        def coef(i):
            return coef_ref[rows((case * N_COEF + i) * 8), :]

        moments = [joined_sums(middle_sums_ref, outer_sums_ref, case * 5 + i, layer) for i in range(5)]
        total, lifted, along, across, walls = moments
        for i in range(3):
            moment_ref[rows((case * 3 + i) * 8), :] = moments[i]

        def x_parts(plane):
            m1, m2 = jnp.where(layer >= 1, pltpu.roll(plane, 1, 0), 0.0), jnp.where(layer >= 2, pltpu.roll(plane, 2, 0), 0.0)
            p1, p2 = jnp.where(layer < 7, pltpu.roll(plane, 7, 0), 0.0), jnp.where(layer < 6, pltpu.roll(plane, 6, 0), 0.0)
            return 16.0 * (p1 + m1) - (p2 + m2), 8.0 * (p1 - m1) - (p2 - m2)

        def y_parts(plane):
            m1, m2 = jnp.where(lane >= 1, pltpu.roll(plane, 1, 1), 0.0), jnp.where(lane >= 2, pltpu.roll(plane, 2, 1), 0.0)
            p1, p2 = jnp.where(lane < 127, pltpu.roll(plane, 127, 1), 0.0), jnp.where(lane < 126, pltpu.roll(plane, 126, 1), 0.0)
            return 16.0 * (p1 + m1) - (p2 + m2), 8.0 * (p1 - m1) - (p2 - m2)

        value = coef(CENTER) * total + coef(SPREAD) * (x_parts(total)[0] + y_parts(total)[0])
        value += coef(ACROSS) * (2.0 * total - walls) + coef(CARRY) * x_parts(lifted)[1]
        value += coef(SOUND_STEP) * (x_parts(along)[1] + y_parts(across)[1]) + coef(STEP) * source_total_ref[rows(case * 8), :]
        sent = (value, coef(SPREAD), coef(CARRY), coef(SOUND_STEP), coef(FLUX))
        for i, plane in enumerate(sent):
            post.put(pl.ds(2 * planes + (case * 5 + i) * 2, 2), plane[6:8], plane[0:2])


def edge_sums(tile):
    for by in (4, 8, 16, 32, 64):
        tile = tile + pltpu.roll(tile, by, 1)
    return pltpu.roll(tile, 2, 1)


def final_kernel(
    depth,
    cases,
    place_ref,
    loose_ref,
    middle_sums_ref,
    corr_ref,
    second_in_ref,
    first_in_ref,
    coef_ref,
    moment_ref,
    outer_ref,
    grad_ref,
    line_ref,
    outer_sums_ref,
):
    planes = 4 * cases * depth
    lane, layer = lanes_of((8, 128)), rows_of((8, 128))
    arrived = Post(place_ref, first_in_ref, second_in_ref)

    def store(c, case, block, offset, tiles):
        for i, row in enumerate(OUTER):
            outer_ref[rows(PAD + i * planes + offset), :] = tiles[row]

    outer_rows(depth, cases, planes, range(2), loose_ref, arrived, coef_ref, store)
    line_sums(depth, cases, planes, wall_sums, outer_ref, OUTER, outer_sums_ref, layer)

    zero = jnp.zeros((8, 128), jnp.float32)
    grad, missing = zero, zero
    for case in range(cases):

        def coef(i):
            return coef_ref[rows((case * N_COEF + i) * 8), :]

        pairs = [arrived.get(pl.ds(2 * planes + (case * 5 + i) * 2, 2)) for i in range(5)]
        below, above = [pair[0] for pair in pairs], [pair[1] for pair in pairs]
        total, lifted, along = (moment_ref[rows((case * 3 + i) * 8), :] for i in range(3))

        def beyond(plane):
            first, second, last, before = plane[0:1], plane[1:2], plane[7:8], plane[6:7]
            down = (jnp.concatenate([-first, 16.0 * first - second], 0), jnp.concatenate([-first, 8.0 * first - second], 0))
            up = (jnp.concatenate([16.0 * last - before, -last], 0), jnp.concatenate([before - 8.0 * last, last], 0))
            return down, up

        down, up = zip(beyond(total), beyond(lifted), beyond(along), strict=True)
        mean_below = below[0] + below[1] * down[0][0] + below[2] * down[1][1] + below[3] * down[2][1]
        mean_above = above[0] + above[1] * up[0][0] + above[2] * up[1][1] + above[3] * up[2][1]
        mean, bend = (joined_sums(middle_sums_ref, outer_sums_ref, case * 2 + i, layer) for i in range(2))
        halo = jnp.concatenate([mean_above, zero[0:4], mean_below], axis=0)
        m1 = pltpu.roll(jnp.where(layer == 7, halo, mean), 1, 0)
        m2 = pltpu.roll(jnp.where(layer >= 6, halo, mean), 2, 0)
        p1 = pltpu.roll(jnp.where(layer == 0, halo, mean), 7, 0)
        p2 = pltpu.roll(jnp.where(layer < 2, halo, mean), 6, 0)
        grad += coef(FLUX) * (8.0 * (p1 - m1) - (p2 - m2)) + coef(BEND) * bend
        change = edge_sums(corr_ref[rows(case * 8), :])
        down_rows = jnp.concatenate([change[6:7] - 8.0 * change[7:8], change[7:8]], axis=0)
        up_rows = jnp.concatenate([-change[0:1], 8.0 * change[0:1] - change[1:2]], axis=0)
        missing += jnp.concatenate([above[4] * down_rows, zero[0:4], below[4] * up_rows], axis=0)
    corner = ((lane < 2) | (lane >= 126)) & ((layer < 2) | (layer >= 6))
    grad_ref[...] = grad
    inside = jnp.where(corner, 0.0, grad)
    rest = jnp.sum(inside * inside, axis=0, keepdims=True)
    corners = pltpu.roll(jnp.where(corner, grad, 0.0), 2, 1, stride=4, stride_axis=0)
    shares = pltpu.roll(jnp.where(corner, missing, 0.0), 34, 1, stride=4, stride_axis=0)
    line = jnp.sum(corners + shares, axis=0, keepdims=True)
    line = jnp.where(lanes_of((1, 128)) < 64, line, rest + pltpu.roll(rest, 64, 1))
    line_ref[...] = jnp.broadcast_to(line[None], line_ref.shape)


def scaled(cells, devices, trans, place_ref, grad_ref, sums_ref, lines_ref):
    pad = -(-trans // 8) * 8
    lane, row = lanes_of((8, 128)), rows_of((8, 128))
    zero = jnp.zeros((pad, 128), jnp.float32)
    lines_ref[rows(0, pad), :] = zero
    lines_ref[rows(pad + devices, pad), :] = zero
    lines_ref[rows(pad, devices), :] = sums_ref[...]
    total, own = jnp.zeros((8, 128), jnp.float32), jnp.zeros((8, 128), jnp.float32)
    device = place_ref[rows(DEVICE * 8), :]
    for block in range(devices // 8):
        here = lines_ref[rows(pad + 8 * block), :]
        below, above = lines_ref[rows(pad - trans + 8 * block), :], lines_ref[rows(pad + trans + 8 * block), :]
        share = pltpu.roll(jnp.where(lane < 48, below, above), 96, 1)
        own += jnp.where(row + 8 * block == device, share, 0.0)
        corner = here + share
        total += jnp.where(lane < 32, corner * corner, jnp.where(lane >= 64, here, 0.0))
    total = jnp.sum(jnp.sum(total, axis=0, keepdims=True), axis=1, keepdims=True)
    own = jnp.broadcast_to(jnp.sum(own, axis=0, keepdims=True), (8, 128))
    grad = grad_ref[...]
    edge = (lane < 2) | (lane >= 126)
    for i in (0, 1, 6, 7):
        grad += jnp.where((row == i) & edge, pltpu.roll(own, (126 - 4 * i) % 128, 1), 0.0)
    return grad / jnp.sqrt(total / cells + 1e-06)


def rest_kernel(
    depth,
    cases,
    cells,
    devices,
    trans,
    place_ref,
    loose_ref,
    middle_ref,
    early_ref,
    second_in_ref,
    first_in_ref,
    coef_ref,
    grad_ref,
    sums_ref,
    out_ref,
    wall_out_ref,
    state_ref,
    wall_ref,
    lines_ref,
    sems,
):
    planes = 4 * cases * depth
    part = planes * 2

    def copy(first, count, sem):
        here = rows(first * part, count * part)
        return pltpu.make_async_copy(state_ref.at[here, :], out_ref.at[here, :], sems.at[sem])

    copies = [copy(2, 2, 0), copy(0, 1, 1), copy(1, 1, 2), pltpu.make_async_copy(wall_ref, wall_out_ref, sems.at[3])]

    def place_tiles(c, refs):
        def one(case, _):
            for block in range(depth // 8):
                offset = pl.multiple_of((c * cases + case) * depth + 8 * block, 8)
                for row in range(8):
                    if refs[row] is not None:
                        ref, place = row_place(refs[row], row, planes)
                        state_ref[strided(offset * 8 + row), :] = ref[rows(place + offset), :]
            return 0

        lax.fori_loop(0, cases, one, 0)

    both = (middle_ref, early_ref)
    for c in range(2, 4):
        place_tiles(c, [both if row in MIDDLE else None for row in range(8)])

    def store(c, case, block, offset, tiles):
        for row, tile in tiles.items():
            state_ref[strided(offset * 8 + row), :] = tile

    arrived = Post(place_ref, first_in_ref, second_in_ref)
    outer_rows(depth, cases, planes, (2, 3), loose_ref, arrived, coef_ref, store)
    copies[0].start()
    for c in range(2):
        place_tiles(c, [both] * 8)
        copies[1 + c].start()
    wall_ref[...] = scaled(cells, devices, trans, place_ref, grad_ref, sums_ref, lines_ref)
    copies[3].start()
    for each in copies:
        each.wait()


def f32(*shape):
    return jax.ShapeDtypeStruct(shape, jnp.float32)


def over_tiles(numbers):
    which = rows_of((8 * len(numbers), 128)) // 8
    held = jnp.full(which.shape, numbers[0], jnp.int32)
    for i, number in enumerate(numbers[1:], 1):
        held = jnp.where(which == i, number, held)
    return held


def in_hbm(array):
    return pltpu.with_memory_space_constraint(array, pltpu.HBM)


def call(kernel, *args, outs, scratch=(), hbm=(), out=VM):
    specs = [VM] * len(args)
    for i in hbm:
        specs[i] = HB
    return pl.pallas_call(
        kernel,
        out_shape=outs,
        in_specs=specs,
        out_specs=tuple([out] * len(outs)),
        scratch_shapes=[pltpu.VMEM(shape, jnp.float32) if isinstance(shape, tuple) else shape for shape in scratch],
        compiler_params=PARAMS,
    )(*args)


def neighbours(axis):
    size = lax.axis_size(axis)
    up = [(i, i + 1) for i in range(size - 1)]
    return up, [(j, i) for i, j in up]


def exchange_rows(first, second):
    size = lax.axis_size("roll")
    inner = [(i, i ^ 1) for i in range(size) if i ^ 1 < size]
    outer = [pair for i in range(1, size - 1, 2) for pair in ((i, i + 1), (i + 1, i))]
    second = lax.ppermute(second, "roll", outer)
    return lax.ppermute(first, "roll", inner), second


def exchange_columns(cols):
    ahead, back = neighbours("trans")
    if lax.axis_size("trans") == 2:
        return lax.ppermute(cols, "trans", ahead + back)
    left, right = lax.ppermute(cols, "trans", ahead), lax.ppermute(cols, "trans", back)
    return jnp.where(lanes_of(cols.shape) % 4 < 2, left, right)


def on_device(adjoint, source, pressure, film, cavity, temp_index):
    components, cases, depth, width_x, width_y = adjoint.shape
    planes = components * cases * depth
    assert (components, width_x, width_y, 4 * depth) == (4, 8, 128, 128)
    state = adjoint.reshape(planes * 8, 128)
    forcing = source.reshape(planes * 8, 128)
    roll, trans, trans_size = lax.axis_index("roll"), lax.axis_index("trans"), lax.axis_size("trans")
    place = over_tiles([trans, trans_size, roll % 2, roll * trans_size + trans])
    devices = lax.axis_size("roll") * trans_size
    inner, part = f32(planes * 8, 128), f32(planes * 4 + 2 * PAD, 128)
    message, tailed, cols_shape = f32(planes * 2, 128), f32(planes * 2 + TAIL, 128), f32(components * cases * 8, 128)
    state, first, second = call(
        functools.partial(send_kernel, depth, cases),
        place,
        in_hbm(state),
        outs=(inner, message, message),
        scratch=[pltpu.SemaphoreType.DMA((PIECES,))],
        hbm=(1,),
    )
    primal = (temp_index.reshape(1, cases), pressure.reshape(cases * 8, 128), film, cavity.reshape(cases * 8, 128))
    (cols,) = call(functools.partial(pack_kernel, depth, cases), state, outs=(cols_shape,))
    middle, outer, coef, packed, mask = call(
        functools.partial(tile_kernel, depth, cases),
        state,
        place,
        *map(in_hbm, primal),
        outs=(part, part, f32(cases * N_COEF * 8, 128), f32(cases * N_PACKED * 8, 128), f32(8, 128)),
        scratch=[pltpu.VMEM(array.shape, array.dtype) for array in primal] + [pltpu.SemaphoreType.DMA((4,))],
        hbm=range(2, 6),
    )
    for index in range(SECTIONS):
        more = index < SECTIONS - 1
        first, second = exchange_rows(first, second)
        side = exchange_columns(cols)
        whole, *total = call(
            functools.partial(inner_kernel, depth, cases),
            middle,
            outer,
            forcing,
            coef,
            outs=(inner, f32(cases * 8, 128)) if more else (inner,),
            scratch=[(planes * 8, 256)],
        )
        middle, loose, sums, *corr = call(
            functools.partial(sides_kernel, depth, cases, next_moments if more else wall_sums),
            whole,
            side,
            mask,
            packed,
            outs=(part, part, f32(cases * (5 if more else 2) * 8, 128)) + (() if more else (cols_shape,)),
            scratch=[cols_shape.shape] if more else [],
        )
        if more:
            outer, second, first, moments = call(
                functools.partial(joined_kernel, depth, cases),
                place,
                loose,
                sums,
                *total,
                second,
                first,
                coef,
                outs=(part, tailed, tailed, f32(cases * 3 * 8, 128)),
                scratch=[(cases * 5 * 8, 128)],
            )
            (cols,) = call(functools.partial(columns_kernel, depth, cases), middle, outer, outs=(cols_shape,))
        else:
            early, grad, sums = call(
                functools.partial(final_kernel, depth, cases),
                place,
                loose,
                sums,
                *corr,
                second,
                first,
                coef,
                moments,
                outs=(part, f32(8, 128), pltpu.VMEM((devices, 1, 128), jnp.float32)),
                scratch=[(cases * 2 * 8, 128)],
            )
    sums = lax.all_to_all(sums, ("roll", "trans"), 0, 0, tiled=True).reshape(devices, 128)
    pad = -(-trans_size // 8) * 8
    state, wall_step = call(
        functools.partial(rest_kernel, depth, cases, devices * width_x * width_y, devices, trans_size),
        place,
        loose,
        middle,
        early,
        second,
        first,
        coef,
        grad,
        sums,
        outs=(pltpu.HBM(inner.shape, jnp.float32), pltpu.HBM((8, 128), jnp.float32)),
        scratch=[inner.shape, (8, 128), (devices + 2 * pad, 128), pltpu.SemaphoreType.DMA((4,))],
        out=HB,
    )
    return (state.reshape(adjoint.shape), wall_step)


def solution(mesh):
    placed = (
        P(None, None, None, "roll", "trans"),
        P(None, None, None, "roll", "trans"),
        P(None, "roll", "trans"),
        P("roll", "trans"),
        P(None, "roll", "trans"),
        P(),
    )
    return jax.shard_map(
        on_device,
        mesh=mesh,
        in_specs=placed,
        out_specs=(P(None, None, None, "roll", "trans"), P("roll", "trans")),
        check_vma=False,
    )
```

```python
import functools

import jax
import jax.numpy as jnp
from jax import lax
from jax.experimental import pallas as pl
from jax.experimental.pallas import tpu as pltpu
from jax.sharding import PartitionSpec as P

SECTIONS = 2


VISCOSITY_PRESS = 0.3
VISCOSITY_TEMP = 0.5
THETA_STEP = 0.2
SOUND = 0.5
KAPPA = 0.6
HEATING = 0.3
ROLL_SPEED = 1.0
COURANT = 0.8

VM = pl.BlockSpec(memory_space=pltpu.VMEM)
HB = pl.BlockSpec(memory_space=pltpu.HBM)
PARAMS = pltpu.CompilerParams(vmem_limit_bytes=16 * 1024 * 1024)

PAD = 8
CENTER, SPREAD, ACROSS = (0, 3, 6)
CARRY, SOUND_STEP, STEP, HEAT, FLUX, BEND = range(9, 15)
N_COEF = 15
N_PACKED = 4
PIECES = 2
TAIL = 24
MIDDLE, OUTER = (2, 3, 4, 5), (0, 1, 6, 7)
TRANS, TRANS_SIZE, ODD, DEVICE = range(4)
WEIGHT = (0, 1, 1, 2)


def lanes_of(shape):
    return lax.broadcasted_iota(jnp.int32, shape, 1)


def rows_of(shape):
    return lax.broadcasted_iota(jnp.int32, shape, 0)


def rows(start, count=8):
    return pl.ds(start, count)


def strided(start):
    return pl.ds(start, 8, stride=8)


def coefficients(depth, cases, place_ref, level_ref, pressure_ref, film_ref, cavity_ref, coef_ref, packed_ref, mask_ref):
    lane, row = lanes_of((8, 128)), rows_of((8, 128))
    film = film_ref[...]
    for case in range(cases):
        theta = THETA_STEP * jnp.broadcast_to(level_ref[:, case : case + 1], (8, 128)).astype(jnp.float32)
        viscosity = jnp.exp(VISCOSITY_PRESS * pressure_ref[rows(case * 8), :] - VISCOSITY_TEMP * theta)
        film_coef = 4.0 * viscosity / (film * film)
        density = 1.0 - 0.6 * cavity_ref[rows(case * 8), :].astype(jnp.float32)
        step = COURANT / (32.0 / 3.0 * viscosity + 4.0 * film_coef + 2.0 * SOUND + 1.0)
        planes = [None] * N_COEF
        for i, weight in enumerate((0.5, 1.0, KAPPA)):
            planes[SPREAD + i] = (weight / 12.0) * step * viscosity
            planes[ACROSS + i] = weight * step * film_coef
            planes[CENTER + i] = 1.0 - 60.0 * planes[SPREAD + i] - 2.0 * planes[ACROSS + i]
        planes[CARRY] = (ROLL_SPEED / 12.0) * step * density
        planes[SOUND_STEP] = (SOUND / 12.0) * step
        planes[STEP] = step
        planes[HEAT] = HEATING * step * viscosity
        planes[FLUX] = (ROLL_SPEED / (24.0 * depth)) * density * film
        planes[BEND] = (8.0 / depth) * viscosity / (film * film * film)
        for i, plane in enumerate(planes):
            coef_ref[rows((case * N_COEF + i) * 8), :] = plane
        wanted = jnp.concatenate(planes[SPREAD : SPREAD + 3] + [planes[SOUND_STEP]], axis=0)
        packed = exact_dot(wanted, edge_columns())
        for i in range(N_PACKED):
            packed_ref[rows((case * N_PACKED + i) * 8), :] = packed[i * 8 : i * 8 + 8]
    trans = place_ref[rows(TRANS * 8), :]
    from_left = jnp.where(trans > 0, 1.0, 0.0)
    from_right = jnp.where(trans < place_ref[rows(TRANS_SIZE * 8), :] - 1, 1.0, 0.0)
    mask_ref[...] = jnp.where(lane % 4 < 2, from_left, from_right)


def edge_columns():
    source = lanes_of((128, 128)) % 4
    source = jnp.where(source < 2, 126 + source, source - 2)
    return jnp.where(rows_of((128, 128)) == source, 1.0, 0.0).astype(jnp.bfloat16)


def in_parts(value):
    high = value.astype(jnp.bfloat16)
    rest = value - high.astype(jnp.float32)
    middle = rest.astype(jnp.bfloat16)
    return jnp.concatenate([high, middle], axis=1), (rest - middle.astype(jnp.float32)).astype(jnp.bfloat16)


def exact_dot(value, weights):
    upper, low = in_parts(value)
    part = jnp.dot(upper, jnp.concatenate([weights, weights], axis=0), preferred_element_type=jnp.float32)
    return part + jnp.dot(low, weights, preferred_element_type=jnp.float32)


class Post:
    def __init__(self, place_ref, first_ref, second_ref):
        self.odd = place_ref[rows(ODD * 8), :] == 1
        self.refs = first_ref, second_ref

    def put(self, where, up, down):
        first, second = self.refs
        odd = self.odd[: where.size]
        first[where, :] = jnp.where(odd, down, up)
        second[where, :] = jnp.where(odd, up, down)

    def get(self, where):
        first, second = (ref[where, :] for ref in self.refs)
        odd = self.odd[: where.size]
        return jnp.where(odd, first, second), jnp.where(odd, second, first)

    def put_tiles(self, planes, first, tiles):
        for i in range(2):
            self.put(rows(i * planes + first), tiles[6 + i], tiles[i])


def row_place(refs, row, planes):
    if row in MIDDLE:
        return refs[0], PAD + MIDDLE.index(row) * planes
    return refs[1], PAD + OUTER.index(row) * planes


def send_kernel(depth, cases, place_ref, state_ref, copy_ref, first_ref, second_ref, sems):
    planes = 4 * cases * depth
    post = Post(place_ref, first_ref, second_ref)

    def piece(i):
        here = rows(i * (planes * 8 // PIECES), planes * 8 // PIECES)
        return pltpu.make_async_copy(state_ref.at[here, :], copy_ref.at[here, :], sems.at[i])

    for i in range(PIECES):
        piece(i).start()
    for i in range(PIECES):
        piece(i).wait()
        for first in range(i * planes // PIECES, (i + 1) * planes // PIECES, 8):
            post.put_tiles(planes, first, {row: copy_ref[strided(first * 8 + row), :] for row in (0, 1, 6, 7)})


def pack_kernel(depth, cases, state_ref, cols_ref):
    lane = lanes_of((8, 128))

    def one(pair, _):
        held = jnp.zeros((8, 128), jnp.float32)
        for layer in range(depth):
            group = depth - 1 - layer
            plane = state_ref[rows(pl.multiple_of((pair * depth + layer) * 8, 8)), :]
            held = jnp.where(lane // 4 == group, pltpu.roll(plane, (4 * group + 2) % 128, 1), held)
        cols_ref[rows(pl.multiple_of(pair * 8, 8)), :] = held
        return 0

    lax.fori_loop(0, 4 * cases, one, 0, unroll=4)


def tile_kernel(depth, cases, state_ref, place_ref, *rest):
    planes = 4 * cases * depth
    (middle_ref, outer_ref), outs, held, sems = rest[4:6], rest[6:9], rest[9:13], rest[13]
    copies = [pltpu.make_async_copy(rest[i], held[i], sems.at[i]) for i in range(4)]
    for copy in copies:
        copy.start()

    def one(pair, _):
        for row in range(8):
            ref, place = row_place((middle_ref, outer_ref), row, planes)
            for block in range(depth // 8):
                first = pl.multiple_of(pair * depth + 8 * block, 8)
                ref[rows(place + first), :] = state_ref[strided(first * 8 + row), :]
        return 0

    lax.fori_loop(0, 4 * cases, one, 0)
    for copy in copies:
        copy.wait()
    coefficients(depth, cases, place_ref, *held, *outs)


def columns_kernel(depth, cases, middle_ref, outer_ref, cols_ref):
    planes = 4 * cases * depth
    columns = edge_columns()
    mine = lanes_of((depth, 128)) // 4 == (depth - 1) - rows_of((depth, 128))
    for row in range(8):
        ref, place = row_place((middle_ref, outer_ref), row, planes)
        edges = exact_dot(ref[rows(place, planes), :], columns)
        for pair in range(4 * cases):
            kept = jnp.where(mine, edges[pair * depth : (pair + 1) * depth], 0.0)
            cols_ref[pl.ds(pair * 8 + row, 1), :] = jnp.sum(kept, axis=0, keepdims=True)


def inner_kernel(depth, cases, middle_ref, outer_ref, source_ref, coef_ref, *rest):
    out_ref, *more_refs, deriv_ref = rest
    planes = 4 * cases * depth
    lane, layer = lanes_of((8, 128)), rows_of((8, 128))
    gap = rows_of((128, 256)) - lanes_of((128, 256)) % 128
    second = jnp.where(jnp.abs(gap) == 1, 16.0, jnp.where(jnp.abs(gap) == 2, -1.0, 0.0))
    first = jnp.where(gap == 1, 8.0, jnp.where(gap == -1, -8.0, jnp.where(gap == 2, -1.0, jnp.where(gap == -2, 1.0, 0.0))))
    weights = jnp.where(lanes_of((128, 256)) < 128, second, first).astype(jnp.bfloat16)
    for row in range(8):
        ref, place = row_place((middle_ref, outer_ref), row, planes)
        value = ref[rows(place, planes), :]
        deriv_ref[rows(row * planes, planes), :] = exact_dot(value, weights)

    def one(index, _):
        case, block = index // (depth // 8), index % (depth // 8)
        k = layer + 8 * block
        height = (k.astype(jnp.float32) + 0.5) / depth
        offsets = [pl.multiple_of((c * cases + case) * depth + 8 * block, 8) for c in range(4)]
        places = [row_place((middle_ref, outer_ref), row, planes) for row in range(8)]
        tiles = [[ref[rows(place + offsets[c]), :] for ref, place in places] for c in range(4)]

        for row in range(8):

            def coef(i):
                return coef_ref[pl.ds((case * N_COEF + i) * 8 + row, 1), :]

            along = []
            for c in range(4):
                near = [tiles[c][row + by] if 0 <= row + by < 8 else None for by in (-2, -1, 1, 2)]
                along.append(near)

            def first_x(c):
                m2, m1, p1, p2 = along[c]
                ones = 8.0 * (p1 - m1) if m1 is not None and p1 is not None else 8.0 * p1 if m1 is None else -8.0 * m1
                if m2 is not None and p2 is not None:
                    return ones - (p2 - m2)
                return ones - p2 if m2 is None else ones + m2

            def second_x(c):
                m2, m1, p1, p2 = along[c]
                ones = 16.0 * (p1 + m1) if m1 is not None and p1 is not None else 16.0 * (p1 if m1 is None else m1)
                if m2 is not None and p2 is not None:
                    return ones - (p2 + m2)
                return ones - (p2 if m2 is None else m2)

            carry = coef(CARRY) * height
            sound = coef(SOUND_STEP)
            step = coef(STEP)
            slopes = [first_x(c) for c in range(4)]
            for c in range(4):
                here = row * planes + offsets[c]
                ref, place = places[row]
                behind = jnp.where(k > 0, ref[rows(place + offsets[c] - 1), :], 0.0)
                beyond = jnp.where(k < depth - 1, ref[rows(place + offsets[c] + 1), :], 0.0)
                source = source_ref[strided(offsets[c] * 8 + row), :]
                w = WEIGHT[c]
                value = coef(CENTER + w) * tiles[c][row] + coef(SPREAD + w) * (second_x(c) + deriv_ref[rows(here), 0:128])
                value += coef(ACROSS + w) * (behind + beyond) + step * source + carry * slopes[c]
                if c == 0:
                    other = row * planes + offsets[2]
                    value += sound * (slopes[1] + deriv_ref[rows(other), 128:256])
                elif c == 1:
                    value += sound * slopes[0]
                elif c == 2:
                    other = row * planes + offsets[0]
                    value += sound * deriv_ref[rows(other), 128:256]
                else:
                    value += coef(HEAT) * tiles[1][row]
                out_ref[rows(here), :] = value
        return 0

    lax.fori_loop(0, cases * (depth // 8), one, 0)

    if more_refs:
        (total_ref,) = more_refs
        for case in range(cases):
            for row in range(8):
                total = jnp.zeros((8, 128), jnp.float32)
                for block in range(depth // 8):
                    total += source_ref[strided((case * depth + 8 * block) * 8 + row), :]
                total_ref[pl.ds(case * 8 + row, 1), :] = jnp.sum(total, axis=0, keepdims=True)


def columns_beyond(cases, side_ref, mask_ref, packed_ref, corr_ref):
    slot = lanes_of((8, 128)) % 4
    for case in range(cases):
        coefs = [packed_ref[rows((case * N_PACKED + i) * 8), :] for i in range(N_PACKED)]
        second, first = [], []
        for c in range(4):
            side = side_ref[rows((c * cases + case) * 8), :] * mask_ref[...]
            p1 = jnp.where(slot == 1, pltpu.roll(side, 127, 1), 0.0)
            p2 = jnp.where(slot < 2, pltpu.roll(side, 126, 1), 0.0)
            m1 = jnp.where(slot == 2, pltpu.roll(side, 1, 1), 0.0)
            m2 = jnp.where(slot >= 2, pltpu.roll(side, 2, 1), 0.0)
            second.append(16.0 * (p1 + m1) - (p2 + m2))
            first.append(8.0 * (p1 - m1) - (p2 - m2))
        for c in range(4):
            value = coefs[WEIGHT[c]] * second[c]
            if c == 0:
                value += coefs[3] * first[2]
            elif c == 2:
                value += coefs[3] * first[0]
            corr_ref[rows((c * cases + case) * 8), :] = value


def depth_sum(tiles):
    total = tiles[0]
    for tile in tiles[1:]:
        total = total + tile
    return jnp.sum(total, axis=0, keepdims=True)


def next_moments(depth, tiles_of, layer):
    density = tiles_of(0)
    heights = [(layer + (8 * block + 0.5)).astype(jnp.float32) / depth for block in range(depth // 8)]
    return (
        depth_sum(density),
        depth_sum([tile * height for tile, height in zip(density, heights, strict=True)]),
        depth_sum(tiles_of(1)),
        depth_sum(tiles_of(2)),
        density[0][0:1] + density[-1][7:8],
    )


def wall_sums(depth, tiles_of, layer):
    momentum, before = tiles_of(1), tiles_of(1, -1)
    changes = [momentum[0] - jnp.where(layer > 0, before[0], 0.0)]
    changes += [here - there for here, there in zip(momentum[1:], before[1:], strict=True)]
    squares = [change * change for change in changes] + [jnp.where(layer == 7, momentum[-1] * momentum[-1], 0.0)]
    return depth_sum(tiles_of(0)), depth_sum(squares)


def line_sums(depth, cases, planes, sums, ref, which, out_ref, layer):
    for case in range(cases):
        for i, row in enumerate(which):

            def tiles_of(c, by=0):
                start = PAD + i * planes + (c * cases + case) * depth
                return [ref[rows(start + by + 8 * block), :] for block in range(depth // 8)]

            lines = sums(depth, tiles_of, layer)
            for n, line in enumerate(lines):
                out_ref[pl.ds((case * len(lines) + n) * 8 + row, 1), :] = line


def joined_sums(middle_ref, outer_ref, index, layer):
    return jnp.where((layer >= 2) & (layer < 6), middle_ref[rows(index * 8), :], outer_ref[rows(index * 8), :])


def sides_kernel(depth, cases, sums, inner_ref, side_ref, mask_ref, packed_ref, middle_ref, loose_ref, sums_ref, corr_ref):
    planes = 4 * cases * depth
    lane, layer = lanes_of((8, 128)), rows_of((8, 128))
    edge = (lane < 2) | (lane >= 126)
    columns_beyond(cases, side_ref, mask_ref, packed_ref, corr_ref)

    def one(case, _):
        for row in range(8):
            for c in range(4):
                line = jnp.broadcast_to(corr_ref[pl.ds((c * cases + case) * 8 + row, 1), :], (8, 128))
                for block in range(depth // 8):
                    offset = pl.multiple_of((c * cases + case) * depth + 8 * block, 8)
                    moved = pltpu.roll(line, 2 + 32 * block, 1, stride=4, stride_axis=0)
                    value = inner_ref[rows(row * planes + offset), :] + jnp.where(edge, moved, 0.0)
                    ref, place = row_place((middle_ref, loose_ref), row, planes)
                    ref[rows(place + offset), :] = value
        return 0

    lax.fori_loop(0, cases, one, 0, unroll=True)
    line_sums(depth, cases, planes, sums, middle_ref, MIDDLE, sums_ref, layer)


def outer_rows(depth, cases, planes, parts, loose_ref, post, coef_ref, store):
    layer = rows_of((8, 128))

    def one(case, _):
        for block in range(depth // 8):
            height = ((layer + 8 * block).astype(jnp.float32) + 0.5) / depth
            offsets = [pl.multiple_of((c * cases + case) * depth + 8 * block, 8) for c in range(4)]
            near = {c: [post.get(rows(i * planes + offsets[c])) for i in range(2)] for c in parts}
            whole = {c: {} for c in parts}
            for i, row in enumerate(OUTER):

                def coef(n):
                    return coef_ref[pl.ds((case * N_COEF + n) * 8 + row, 1), :]

                second, first = {}, {}
                for c, ((m2, p1), (m1, p2)) in near.items():
                    if row == 0:
                        second[c], first[c] = 16.0 * m1 - m2, m2 - 8.0 * m1
                    elif row == 1:
                        second[c], first[c] = -m1, m1
                    elif row == 6:
                        second[c], first[c] = -p1, -p1
                    else:
                        second[c], first[c] = 16.0 * p1 - p2, 8.0 * p1 - p2
                for c in parts:
                    value = loose_ref[rows(PAD + i * planes + offsets[c]), :]
                    value += coef(SPREAD + WEIGHT[c]) * second[c] + coef(CARRY) * height * first[c]
                    if c < 2:
                        value += coef(SOUND_STEP) * first[1 - c]
                    whole[c][row] = value
            for c in parts:
                store(c, case, block, offsets[c], whole[c])
        return 0

    lax.fori_loop(0, cases, one, 0, unroll=True)


def joined_kernel(
    depth,
    cases,
    place_ref,
    loose_ref,
    middle_sums_ref,
    source_total_ref,
    second_in_ref,
    first_in_ref,
    coef_ref,
    outer_ref,
    second_ref,
    first_ref,
    moment_ref,
    outer_sums_ref,
):
    planes = 4 * cases * depth
    lane, layer = lanes_of((8, 128)), rows_of((8, 128))
    post, arrived = Post(place_ref, first_ref, second_ref), Post(place_ref, first_in_ref, second_in_ref)

    def store(c, case, block, offset, tiles):
        for i, row in enumerate(OUTER):
            outer_ref[rows(PAD + i * planes + offset), :] = tiles[row]
        post.put_tiles(planes, offset, tiles)

    outer_rows(depth, cases, planes, range(4), loose_ref, arrived, coef_ref, store)

    line_sums(depth, cases, planes, next_moments, outer_ref, OUTER, outer_sums_ref, layer)
    for case in range(cases):

        def coef(i):
            return coef_ref[rows((case * N_COEF + i) * 8), :]

        moments = [joined_sums(middle_sums_ref, outer_sums_ref, case * 5 + i, layer) for i in range(5)]
        total, lifted, along, across, walls = moments
        for i in range(3):
            moment_ref[rows((case * 3 + i) * 8), :] = moments[i]

        def x_parts(plane):
            m1, m2 = jnp.where(layer >= 1, pltpu.roll(plane, 1, 0), 0.0), jnp.where(layer >= 2, pltpu.roll(plane, 2, 0), 0.0)
            p1, p2 = jnp.where(layer < 7, pltpu.roll(plane, 7, 0), 0.0), jnp.where(layer < 6, pltpu.roll(plane, 6, 0), 0.0)
            return 16.0 * (p1 + m1) - (p2 + m2), 8.0 * (p1 - m1) - (p2 - m2)

        def y_parts(plane):
            m1, m2 = jnp.where(lane >= 1, pltpu.roll(plane, 1, 1), 0.0), jnp.where(lane >= 2, pltpu.roll(plane, 2, 1), 0.0)
            p1, p2 = jnp.where(lane < 127, pltpu.roll(plane, 127, 1), 0.0), jnp.where(lane < 126, pltpu.roll(plane, 126, 1), 0.0)
            return 16.0 * (p1 + m1) - (p2 + m2), 8.0 * (p1 - m1) - (p2 - m2)

        value = coef(CENTER) * total + coef(SPREAD) * (x_parts(total)[0] + y_parts(total)[0])
        value += coef(ACROSS) * (2.0 * total - walls) + coef(CARRY) * x_parts(lifted)[1]
        value += coef(SOUND_STEP) * (x_parts(along)[1] + y_parts(across)[1]) + coef(STEP) * source_total_ref[rows(case * 8), :]
        sent = (value, coef(SPREAD), coef(CARRY), coef(SOUND_STEP), coef(FLUX))
        for i, plane in enumerate(sent):
            post.put(pl.ds(2 * planes + (case * 5 + i) * 2, 2), plane[6:8], plane[0:2])


def edge_sums(tile):
    for by in (4, 8, 16, 32, 64):
        tile = tile + pltpu.roll(tile, by, 1)
    return pltpu.roll(tile, 2, 1)


def final_kernel(
    depth,
    cases,
    place_ref,
    loose_ref,
    middle_sums_ref,
    corr_ref,
    second_in_ref,
    first_in_ref,
    coef_ref,
    moment_ref,
    outer_ref,
    grad_ref,
    line_ref,
    outer_sums_ref,
):
    planes = 4 * cases * depth
    lane, layer = lanes_of((8, 128)), rows_of((8, 128))
    arrived = Post(place_ref, first_in_ref, second_in_ref)

    def store(c, case, block, offset, tiles):
        for i, row in enumerate(OUTER):
            outer_ref[rows(PAD + i * planes + offset), :] = tiles[row]

    outer_rows(depth, cases, planes, range(2), loose_ref, arrived, coef_ref, store)
    line_sums(depth, cases, planes, wall_sums, outer_ref, OUTER, outer_sums_ref, layer)

    zero = jnp.zeros((8, 128), jnp.float32)
    grad, missing = zero, zero
    for case in range(cases):

        def coef(i):
            return coef_ref[rows((case * N_COEF + i) * 8), :]

        pairs = [arrived.get(pl.ds(2 * planes + (case * 5 + i) * 2, 2)) for i in range(5)]
        below, above = [pair[0] for pair in pairs], [pair[1] for pair in pairs]
        total, lifted, along = (moment_ref[rows((case * 3 + i) * 8), :] for i in range(3))

        def beyond(plane):
            first, second, last, before = plane[0:1], plane[1:2], plane[7:8], plane[6:7]
            down = (jnp.concatenate([-first, 16.0 * first - second], 0), jnp.concatenate([-first, 8.0 * first - second], 0))
            up = (jnp.concatenate([16.0 * last - before, -last], 0), jnp.concatenate([before - 8.0 * last, last], 0))
            return down, up

        down, up = zip(beyond(total), beyond(lifted), beyond(along), strict=True)
        mean_below = below[0] + below[1] * down[0][0] + below[2] * down[1][1] + below[3] * down[2][1]
        mean_above = above[0] + above[1] * up[0][0] + above[2] * up[1][1] + above[3] * up[2][1]
        mean, bend = (joined_sums(middle_sums_ref, outer_sums_ref, case * 2 + i, layer) for i in range(2))
        halo = jnp.concatenate([mean_above, zero[0:4], mean_below], axis=0)
        m1 = pltpu.roll(jnp.where(layer == 7, halo, mean), 1, 0)
        m2 = pltpu.roll(jnp.where(layer >= 6, halo, mean), 2, 0)
        p1 = pltpu.roll(jnp.where(layer == 0, halo, mean), 7, 0)
        p2 = pltpu.roll(jnp.where(layer < 2, halo, mean), 6, 0)
        grad += coef(FLUX) * (8.0 * (p1 - m1) - (p2 - m2)) + coef(BEND) * bend
        change = edge_sums(corr_ref[rows(case * 8), :])
        down_rows = jnp.concatenate([change[6:7] - 8.0 * change[7:8], change[7:8]], axis=0)
        up_rows = jnp.concatenate([-change[0:1], 8.0 * change[0:1] - change[1:2]], axis=0)
        missing += jnp.concatenate([above[4] * down_rows, zero[0:4], below[4] * up_rows], axis=0)
    corner = ((lane < 2) | (lane >= 126)) & ((layer < 2) | (layer >= 6))
    grad_ref[...] = grad
    inside = jnp.where(corner, 0.0, grad)
    rest = jnp.sum(inside * inside, axis=0, keepdims=True)
    corners = pltpu.roll(jnp.where(corner, grad, 0.0), 2, 1, stride=4, stride_axis=0)
    shares = pltpu.roll(jnp.where(corner, missing, 0.0), 34, 1, stride=4, stride_axis=0)
    line = jnp.sum(corners + shares, axis=0, keepdims=True)
    line = jnp.where(lanes_of((1, 128)) < 64, line, rest + pltpu.roll(rest, 64, 1))
    line_ref[...] = jnp.broadcast_to(line[None], line_ref.shape)


def scaled(cells, devices, trans, place_ref, grad_ref, sums_ref, lines_ref):
    pad = -(-trans // 8) * 8
    lane, row = lanes_of((8, 128)), rows_of((8, 128))
    zero = jnp.zeros((pad, 128), jnp.float32)
    lines_ref[rows(0, pad), :] = zero
    lines_ref[rows(pad + devices, pad), :] = zero
    lines_ref[rows(pad, devices), :] = sums_ref[...]
    total, own = jnp.zeros((8, 128), jnp.float32), jnp.zeros((8, 128), jnp.float32)
    device = place_ref[rows(DEVICE * 8), :]
    for block in range(devices // 8):
        here = lines_ref[rows(pad + 8 * block), :]
        below, above = lines_ref[rows(pad - trans + 8 * block), :], lines_ref[rows(pad + trans + 8 * block), :]
        share = pltpu.roll(jnp.where(lane < 48, below, above), 96, 1)
        own += jnp.where(row + 8 * block == device, share, 0.0)
        corner = here + share
        total += jnp.where(lane < 32, corner * corner, jnp.where(lane >= 64, here, 0.0))
    total = jnp.sum(jnp.sum(total, axis=0, keepdims=True), axis=1, keepdims=True)
    own = jnp.broadcast_to(jnp.sum(own, axis=0, keepdims=True), (8, 128))
    grad = grad_ref[...]
    edge = (lane < 2) | (lane >= 126)
    for i in (0, 1, 6, 7):
        grad += jnp.where((row == i) & edge, pltpu.roll(own, (126 - 4 * i) % 128, 1), 0.0)
    return grad / jnp.sqrt(total / cells + 1e-06)


def rest_kernel(
    depth,
    cases,
    cells,
    devices,
    trans,
    place_ref,
    loose_ref,
    middle_ref,
    early_ref,
    second_in_ref,
    first_in_ref,
    coef_ref,
    grad_ref,
    sums_ref,
    out_ref,
    wall_out_ref,
    state_ref,
    wall_ref,
    lines_ref,
    sems,
):
    planes = 4 * cases * depth
    part = planes * 2

    def copy(first, count, sem):
        here = rows(first * part, count * part)
        return pltpu.make_async_copy(state_ref.at[here, :], out_ref.at[here, :], sems.at[sem])

    copies = [copy(2, 2, 0), copy(0, 1, 1), copy(1, 1, 2), pltpu.make_async_copy(wall_ref, wall_out_ref, sems.at[3])]

    def place_tiles(c, refs):
        def one(case, _):
            for block in range(depth // 8):
                offset = pl.multiple_of((c * cases + case) * depth + 8 * block, 8)
                for row in range(8):
                    if refs[row] is not None:
                        ref, place = row_place(refs[row], row, planes)
                        state_ref[strided(offset * 8 + row), :] = ref[rows(place + offset), :]
            return 0

        lax.fori_loop(0, cases, one, 0)

    both = (middle_ref, early_ref)
    for c in range(2, 4):
        place_tiles(c, [both if row in MIDDLE else None for row in range(8)])

    def store(c, case, block, offset, tiles):
        for row, tile in tiles.items():
            state_ref[strided(offset * 8 + row), :] = tile

    arrived = Post(place_ref, first_in_ref, second_in_ref)
    outer_rows(depth, cases, planes, (2, 3), loose_ref, arrived, coef_ref, store)
    copies[0].start()
    for c in range(2):
        place_tiles(c, [both] * 8)
        copies[1 + c].start()
    wall_ref[...] = scaled(cells, devices, trans, place_ref, grad_ref, sums_ref, lines_ref)
    copies[3].start()
    for each in copies:
        each.wait()


def f32(*shape):
    return jax.ShapeDtypeStruct(shape, jnp.float32)


def over_tiles(numbers):
    which = rows_of((8 * len(numbers), 128)) // 8
    held = jnp.full(which.shape, numbers[0], jnp.int32)
    for i, number in enumerate(numbers[1:], 1):
        held = jnp.where(which == i, number, held)
    return held


def in_hbm(array):
    return pltpu.with_memory_space_constraint(array, pltpu.HBM)


def call(kernel, *args, outs, scratch=(), hbm=(), out=VM):
    specs = [VM] * len(args)
    for i in hbm:
        specs[i] = HB
    return pl.pallas_call(
        kernel,
        out_shape=outs,
        in_specs=specs,
        out_specs=tuple([out] * len(outs)),
        scratch_shapes=[pltpu.VMEM(shape, jnp.float32) if isinstance(shape, tuple) else shape for shape in scratch],
        compiler_params=PARAMS,
    )(*args)


def neighbours(axis):
    size = lax.axis_size(axis)
    up = [(i, i + 1) for i in range(size - 1)]
    return up, [(j, i) for i, j in up]


def exchange_rows(first, second):
    size = lax.axis_size("roll")
    inner = [(i, i ^ 1) for i in range(size) if i ^ 1 < size]
    outer = [pair for i in range(1, size - 1, 2) for pair in ((i, i + 1), (i + 1, i))]
    second = lax.ppermute(second, "roll", outer)
    return lax.ppermute(first, "roll", inner), second


def exchange_columns(cols):
    ahead, back = neighbours("trans")
    if lax.axis_size("trans") == 2:
        return lax.ppermute(cols, "trans", ahead + back)
    left, right = lax.ppermute(cols, "trans", ahead), lax.ppermute(cols, "trans", back)
    return jnp.where(lanes_of(cols.shape) % 4 < 2, left, right)


def on_device(adjoint, source, pressure, film, cavity, temp_index):
    components, cases, depth, width_x, width_y = adjoint.shape
    planes = components * cases * depth
    assert (components, width_x, width_y, 4 * depth) == (4, 8, 128, 128)
    state = adjoint.reshape(planes * 8, 128)
    forcing = source.reshape(planes * 8, 128)
    roll, trans, trans_size = lax.axis_index("roll"), lax.axis_index("trans"), lax.axis_size("trans")
    place = over_tiles([trans, trans_size, roll % 2, roll * trans_size + trans])
    devices = lax.axis_size("roll") * trans_size
    inner, part = f32(planes * 8, 128), f32(planes * 4 + 2 * PAD, 128)
    message, tailed, cols_shape = f32(planes * 2, 128), f32(planes * 2 + TAIL, 128), f32(components * cases * 8, 128)
    state, first, second = call(
        functools.partial(send_kernel, depth, cases),
        place,
        in_hbm(state),
        outs=(inner, message, message),
        scratch=[pltpu.SemaphoreType.DMA((PIECES,))],
        hbm=(1,),
    )
    primal = (temp_index.reshape(1, cases), pressure.reshape(cases * 8, 128), film, cavity.reshape(cases * 8, 128))
    (cols,) = call(functools.partial(pack_kernel, depth, cases), state, outs=(cols_shape,))
    middle, outer, coef, packed, mask = call(
        functools.partial(tile_kernel, depth, cases),
        state,
        place,
        *map(in_hbm, primal),
        outs=(part, part, f32(cases * N_COEF * 8, 128), f32(cases * N_PACKED * 8, 128), f32(8, 128)),
        scratch=[pltpu.VMEM(array.shape, array.dtype) for array in primal] + [pltpu.SemaphoreType.DMA((4,))],
        hbm=range(2, 6),
    )
    for index in range(SECTIONS):
        more = index < SECTIONS - 1
        first, second = exchange_rows(first, second)
        side = exchange_columns(cols)
        whole, *total = call(
            functools.partial(inner_kernel, depth, cases),
            middle,
            outer,
            forcing,
            coef,
            outs=(inner, f32(cases * 8, 128)) if more else (inner,),
            scratch=[(planes * 8, 256)],
        )
        middle, loose, sums, *corr = call(
            functools.partial(sides_kernel, depth, cases, next_moments if more else wall_sums),
            whole,
            side,
            mask,
            packed,
            outs=(part, part, f32(cases * (5 if more else 2) * 8, 128)) + (() if more else (cols_shape,)),
            scratch=[cols_shape.shape] if more else [],
        )
        if more:
            outer, second, first, moments = call(
                functools.partial(joined_kernel, depth, cases),
                place,
                loose,
                sums,
                *total,
                second,
                first,
                coef,
                outs=(part, tailed, tailed, f32(cases * 3 * 8, 128)),
                scratch=[(cases * 5 * 8, 128)],
            )
            (cols,) = call(functools.partial(columns_kernel, depth, cases), middle, outer, outs=(cols_shape,))
        else:
            early, grad, sums = call(
                functools.partial(final_kernel, depth, cases),
                place,
                loose,
                sums,
                *corr,
                second,
                first,
                coef,
                moments,
                outs=(part, f32(8, 128), pltpu.VMEM((devices, 1, 128), jnp.float32)),
                scratch=[(cases * 2 * 8, 128)],
            )
    sums = lax.all_to_all(sums, ("roll", "trans"), 0, 0, tiled=True).reshape(devices, 128)
    pad = -(-trans_size // 8) * 8
    state, wall_step = call(
        functools.partial(rest_kernel, depth, cases, devices * width_x * width_y, devices, trans_size),
        place,
        loose,
        middle,
        early,
        second,
        first,
        coef,
        grad,
        sums,
        outs=(pltpu.HBM(inner.shape, jnp.float32), pltpu.HBM((8, 128), jnp.float32)),
        scratch=[inner.shape, (8, 128), (devices + 2 * pad, 128), pltpu.SemaphoreType.DMA((4,))],
        out=HB,
    )
    return (state.reshape(adjoint.shape), wall_step)


def solution(mesh):
    placed = (
        P(None, None, None, "roll", "trans"),
        P(None, None, None, "roll", "trans"),
        P(None, "roll", "trans"),
        P("roll", "trans"),
        P(None, "roll", "trans"),
        P(),
    )
    return jax.shard_map(
        on_device,
        mesh=mesh,
        in_specs=placed,
        out_specs=(P(None, None, None, "roll", "trans"), P("roll", "trans")),
        check_vma=False,
    )
```
